32 devices in a mesh: sx: 8 (over y, x, core), sy: 4 (over z).
Axes of the slice: x: 2, y: 2, z: 4, core: 2. Of those that a mesh axis runs over, the one named last changes fastest.
Arguments:
- force: float32 [3, 64, 32, 256], P(None, 'sx', 'sy'), may hold values from -7.2 to 7.2
- load_mask: int32 [64, 32, 256], P('sx', 'sy'), may hold values 0 or 1
- support_mask: int32 [64, 32, 256], P('sx', 'sy'), may hold values 0 or 1
- start_field: float32 [3, 64, 32, 256], P(None, 'sx', 'sy'), may hold values from -7.2 to 7.2
- density: float32 [32, 16, 128], P('sx', 'sy'), may hold values from 0.1 to 1
- passive_mask: int32 [32, 16, 128], P('sx', 'sy'), may hold values 0 or 1
Outputs:
- displacement: float32 [3, 64, 32, 256], P(None, 'sx', 'sy')
- filtered: float32 [32, 16, 128], P('sx', 'sy')
- compliance: float32 [], replicated
The draws below stay inside these ranges and needn't reach their ends.
All inputs are finite; a program needn't handle non-finite values. No bound on the sum of `load_mask` or of `support_mask` or of `passive_mask` on one device may be relied on, other than what follows from the above.
Results may differ from the reference program's by a relative error of at most 0.0003.
Values sent between devices are 32-bit elements; how exact they have to be, the bound alone decides.
No kernel may reach another device: no remote copies, remote signals or barrier semaphores. Data moves between devices by JAX's collectives and lax.ppermute only.
A program may use at most 128 MiB of HBM per device.

```python
import math
import jax
import jax.numpy as jnp
import numpy as np
from jax import lax

EX = 4
EZ = 128
SWEEPS = 4
NEX = 32
NEY = 16
NX2 = 64
NY2 = 32
NZ2 = 256
N_SX = 8


def rising_field(key, top):
    along = jnp.arange(NX2, dtype=jnp.float32) / jnp.float32(max(NX2 - 1, 1))
    scale = 0.3 * jnp.float32(top) ** along
    values = jnp.clip(jax.random.normal(key, (3, NX2, NY2, NZ2), jnp.float32), -4.0, 4.0)
    return values * scale[None, :, None, None]


def draw_force(key, part):
    key = jax.random.fold_in(key, 11)
    return rising_field(key, 6.0)


def draw_start_field(key, part):
    key = jax.random.fold_in(key, 23)
    return rising_field(key, 6.0)


def draw_density(key, part):
    key = jax.random.fold_in(key, 37)
    along = jnp.arange(NEX, dtype=jnp.float32) / jnp.float32(max(NEX - 1, 1))
    lowest = (0.1 + 0.8 * along)[:, None, None]
    unit = jax.random.uniform(key, (NEX, NEY, EZ), jnp.float32)
    return jnp.exp(jnp.log(lowest) * (1.0 - unit))


def place_ends(values, stream_key, least, high):
    place = [jax.random.randint(jax.random.fold_in(stream_key, axis), (), 0, length) for axis, length in enumerate(values.shape)]
    longest = values.shape.index(max(values.shape))
    beside = place[:longest] + [(place[longest] + 1) % values.shape[longest]] + place[longest + 1:]
    return values.at[tuple(place)].set(least).at[tuple(beside)].set(high)


def setup_inputs(seed: int = 0) -> dict:
    arg_keys = jax.random.split(jax.random.key(seed), 7)
    return {
        "force": draw_force(jax.random.fold_in(arg_keys[6], 71), 0),
        "load_mask": place_ends((jax.random.randint(arg_keys[1], (NX2, NY2, NZ2), 0, 4) < 1).astype(jnp.int32), jax.random.fold_in(arg_keys[1], 1), 0, 1),
        "support_mask": place_ends((jax.random.randint(arg_keys[2], (NX2, NY2, NZ2), 0, 16) < 1).astype(jnp.int32), jax.random.fold_in(arg_keys[2], 1), 0, 1),
        "start_field": draw_start_field(jax.random.fold_in(arg_keys[6], 71), 0),
        "density": draw_density(jax.random.fold_in(arg_keys[6], 71), 0),
        "passive_mask": place_ends((jax.random.randint(arg_keys[5], (NEX, NEY, EZ), 0, 8) < 1).astype(jnp.int32), jax.random.fold_in(arg_keys[5], 1), 0, 1),
    }


EMIN = 0.001
RADIUS = 1.5

def element_matrix():
    poisson = 0.3
    lame_first = poisson / ((1.0 + poisson) * (1.0 - 2.0 * poisson))
    shear = 1.0 / (2.0 * (1.0 + poisson))
    elastic = np.zeros((6, 6))
    elastic[:3, :3] = lame_first
    for entry in range(3):
        elastic[entry, entry] += 2.0 * shear
        elastic[entry + 3, entry + 3] = shear
    points = [-math.sqrt(0.6), 0.0, math.sqrt(0.6)]
    weights = [5.0 / 9.0, 8.0 / 9.0, 5.0 / 9.0]

    def values(point):
        return np.array([point * (point - 1.0) / 2.0, 1.0 - point * point, point * (point + 1.0) / 2.0])

    def slopes(point):
        return np.array([point - 0.5, -2.0 * point, point + 0.5])
    stiff = np.zeros((81, 81))
    for first in range(3):
        for second in range(3):
            for third in range(3):
                val_x, val_y, val_z = (values(points[first]), values(points[second]), values(points[third]))
                der_x, der_y, der_z = (slopes(points[first]), slopes(points[second]), slopes(points[third]))
                strain = np.zeros((6, 81))
                for node_a in range(3):
                    for node_b in range(3):
                        for node_c in range(3):
                            node = node_a * 9 + node_b * 3 + node_c
                            grad_x = 2.0 * der_x[node_a] * val_y[node_b] * val_z[node_c]
                            grad_y = 2.0 * val_x[node_a] * der_y[node_b] * val_z[node_c]
                            grad_z = 2.0 * val_x[node_a] * val_y[node_b] * der_z[node_c]
                            strain[0, node] = grad_x
                            strain[1, 27 + node] = grad_y
                            strain[2, 54 + node] = grad_z
                            strain[3, node] = grad_y
                            strain[3, 27 + node] = grad_x
                            strain[4, 27 + node] = grad_z
                            strain[4, 54 + node] = grad_y
                            strain[5, node] = grad_z
                            strain[5, 54 + node] = grad_x
                factor = weights[first] * weights[second] * weights[third] * 0.125
                stiff = stiff + factor * strain.T @ elastic @ strain
    return jnp.asarray(stiff.astype(np.float32))

def filter_weights():
    table = []
    for first in range(3):
        for second in range(3):
            for third in range(3):
                distance = math.sqrt((first - 1) ** 2 + (second - 1) ** 2 + (third - 1) ** 2)
                table.append(max(0.0, RADIUS - distance))
    return table

def element_vectors(nodes, count_x, count_y, count_z):
    pieces = []
    for comp in range(3):
        for node_a in range(3):
            for node_b in range(3):
                for node_c in range(3):
                    pieces.append(nodes[comp, node_a:node_a + 2 * count_x:2, node_b:node_b + 2 * count_y:2, node_c:node_c + 2 * count_z:2])
    return jnp.stack(pieces)

def element_scatter(products, count_x, count_y, count_z):
    result = jnp.zeros((3, 2 * count_x + 1, 2 * count_y + 1, 2 * count_z + 1), jnp.float32)
    index = 0
    for comp in range(3):
        for node_a in range(3):
            for node_b in range(3):
                for node_c in range(3):
                    result = result.at[comp, node_a:node_a + 2 * count_x:2, node_b:node_b + 2 * count_y:2, node_c:node_c + 2 * count_z:2].add(products[index])
                    index += 1
    return result

def multiply(stiff, vectors):
    return jnp.einsum('ij,jxyz->ixyz', stiff, vectors, precision=lax.Precision.HIGHEST)

def reference(force, load_mask, support_mask, start_field, density, passive_mask):
    stiff = element_matrix()
    rho = jnp.where(passive_mask == 1, jnp.float32(1.0), density)
    young = EMIN + (1.0 - EMIN) * rho ** 3
    free = (1 - support_mask).astype(jnp.float32)[None]
    load = free * load_mask.astype(jnp.float32)[None] * force
    slabs = jnp.arange(N_SX, dtype=jnp.int32)
    stiff_diag = jnp.diagonal(stiff)

    def combine(parts):
        main = parts[:, :, :2 * EX]
        tops = parts[:, :, 2 * EX]
        main = main.at[1:, :, 0].add(tops[:-1])
        whole = jnp.moveaxis(main, 0, 1).reshape(3, NX2, NY2 + 1, NZ2 + 1)
        return whole[:, :, :NY2, :NZ2]

    def slab_young(index):
        return lax.dynamic_slice_in_dim(young, index * EX, EX, 0)

    def stiff_apply(field):
        padded = jnp.pad(field, ((0, 0), (0, 1), (0, 1), (0, 1)))

        def one_slab(index):
            nodes = lax.dynamic_slice_in_dim(padded, index * 2 * EX, 2 * EX + 1, 1)
            vectors = element_vectors(nodes, EX, NEY, EZ)
            products = multiply(stiff, vectors) * slab_young(index)[None]
            return element_scatter(products, EX, NEY, EZ)
        return combine(lax.map(one_slab, slabs))

    def diag_slab(index):
        products = stiff_diag[:, None, None, None] * slab_young(index)[None]
        return element_scatter(products, EX, NEY, EZ)
    diagonal = free * combine(lax.map(diag_slab, slabs)) + (1.0 - free)

    def operator(field):
        return free * stiff_apply(free * field) + (1.0 - free) * field
    displacement = free * start_field
    residual = load - operator(displacement)
    for sweep in range(SWEEPS):
        step = residual / diagonal
        image = operator(step)
        omega = jnp.sum(residual * image) / jnp.sum(image * image)
        displacement = displacement + omega * step
        residual = residual - omega * image
    padded = jnp.pad(displacement, ((0, 0), (0, 1), (0, 1), (0, 1)))

    def energy_slab(index):
        nodes = lax.dynamic_slice_in_dim(padded, index * 2 * EX, 2 * EX + 1, 1)
        vectors = element_vectors(nodes, EX, NEY, EZ)
        return lax.optimization_barrier(jnp.sum(vectors * multiply(stiff, vectors), axis=0))
    energy = lax.map(energy_slab, slabs).reshape(NEX, NEY, EZ)
    compliance = jnp.sum(young * energy)
    sens = jnp.where(passive_mask == 1, jnp.float32(0.0), -3.0 * (1.0 - EMIN) * rho ** 2 * energy)
    rim = jnp.pad(sens, 1)
    covered = jnp.pad(jnp.ones_like(sens), 1)
    table = filter_weights()
    upper = jnp.zeros_like(sens)
    lower = jnp.zeros_like(sens)
    index = 0
    for first in range(3):
        for second in range(3):
            for third in range(3):
                if table[index] > 0.0:
                    upper = upper + table[index] * rim[first:first + NEX, second:second + NEY, third:third + EZ]
                    lower = lower + table[index] * covered[first:first + NEX, second:second + NEY, third:third + EZ]
                index += 1
    return (displacement, upper / lower, compliance)
```

```python
import functools
import math

import jax
import jax.numpy as jnp
import numpy as np
from jax import lax
from jax.experimental import pallas as pl
from jax.experimental.pallas import tpu as pltpu
from jax.sharding import PartitionSpec as P

SWEEPS = 4
EMIN = 0.001
RADIUS = 1.5

OWN = 8
ELEMS = OWN // 2
HALO_U = 5
HALO_F = 3
HALO_Z = 7
PARTS = [
    (0, None),
    (1, None),
    (None, 0),
    (None, 1),
    (0, 0),
    (0, 1),
    (1, 0),
    (1, 1),
]
UP_X, UP_Y, LOW_X, HIGH_X, LOW_Y, HIGH_Y = range(6)
F32 = jnp.float32
BF16 = jnp.bfloat16


def element_matrix():
    poisson = 0.3
    lame_first = poisson / ((1.0 + poisson) * (1.0 - 2.0 * poisson))
    shear = 1.0 / (2.0 * (1.0 + poisson))
    elastic = np.zeros((6, 6))
    elastic[:3, :3] = lame_first
    for entry in range(3):
        elastic[entry, entry] += 2.0 * shear
        elastic[entry + 3, entry + 3] = shear
    points = [-math.sqrt(0.6), 0.0, math.sqrt(0.6)]
    weights = [5.0 / 9.0, 8.0 / 9.0, 5.0 / 9.0]

    def values(point):
        return np.array(
            [point * (point - 1.0) / 2.0, 1.0 - point * point, point * (point + 1.0) / 2.0]
        )

    def slopes(point):
        return np.array([point - 0.5, -2.0 * point, point + 0.5])

    stiff = np.zeros((81, 81))
    for first in range(3):
        for second in range(3):
            for third in range(3):
                val_x, val_y, val_z = (
                    values(points[first]),
                    values(points[second]),
                    values(points[third]),
                )
                der_x, der_y, der_z = (
                    slopes(points[first]),
                    slopes(points[second]),
                    slopes(points[third]),
                )
                strain = np.zeros((6, 81))
                for node_a in range(3):
                    for node_b in range(3):
                        for node_c in range(3):
                            node = node_a * 9 + node_b * 3 + node_c
                            grad_x = 2.0 * der_x[node_a] * val_y[node_b] * val_z[node_c]
                            grad_y = 2.0 * val_x[node_a] * der_y[node_b] * val_z[node_c]
                            grad_z = 2.0 * val_x[node_a] * val_y[node_b] * der_z[node_c]
                            strain[0, node] = grad_x
                            strain[1, 27 + node] = grad_y
                            strain[2, 54 + node] = grad_z
                            strain[3, node] = grad_y
                            strain[3, 27 + node] = grad_x
                            strain[4, 27 + node] = grad_z
                            strain[4, 54 + node] = grad_y
                            strain[5, node] = grad_z
                            strain[5, 54 + node] = grad_x
                factor = weights[first] * weights[second] * weights[third] * 0.125
                stiff = stiff + factor * strain.T @ elastic @ strain
    return stiff.astype(np.float32)


def operator_matrix(stiff):
    hi = stiff.astype(BF16).astype(np.float32)
    parts = (hi, stiff - hi)
    out = np.zeros((2, 120, 256), np.float32)

    def out_row(comp, a, b, c):
        if c < 2:
            return (a * 3 + b) * 8 + c * 3 + comp
        return 72 + (a * 2 + b // 2) * 8 + (b % 2) * 3 + comp

    def in_row(comp, a, b, c, low):
        if c < 2:
            return (a * 3 + b) * 16 + low * 8 + c * 3 + comp
        return 144 + (a * 2 + b // 2) * 16 + (b % 2) * 8 + low * 3 + comp

    index = [(p, a, b, c) for p in range(3) for a in range(3) for b in range(3) for c in range(3)]
    for i, first in enumerate(index):
        for j, second in enumerate(index):
            row = out_row(*first)
            out[0, row, in_row(*second, 0)] = parts[0][i, j]
            out[0, row, in_row(*second, 1)] = parts[0][i, j]
            out[1, row, in_row(*second, 0)] = parts[1][i, j]
    return out.reshape(240, 256).astype(BF16)


def diagonal_columns(stiff):
    out = np.zeros((4, 8, 128), np.float32)
    for pa in range(2):
        for pb in range(2):
            for c in range(2):
                for comp in range(3):
                    dof = comp * 27 + pa * 9 + pb * 3 + c
                    out[pa * 2 + pb, c * 3 + comp] = stiff[dof, dof]
    return out


def iota(shape, dim):
    return lax.broadcasted_iota(jnp.int32, shape, dim)


def parity_matrix(transposed):
    node = iota((256, 256), 1 if transposed else 0)
    place = iota((256, 256), 0 if transposed else 1)
    return (node == 2 * (place % 128) + place // 128).astype(F32).astype(BF16)


def exact_product(rows, matrix):
    first = rows.astype(BF16)
    left = rows - first.astype(F32)
    second = left.astype(BF16)
    third = (left - second.astype(F32)).astype(BF16)
    stacked = jnp.concatenate([first, second, third], axis=0)
    out = jnp.dot(stacked, matrix, preferred_element_type=F32)
    count = rows.shape[0]
    return out[:count] + out[count : 2 * count] + out[2 * count :]


def span(k, up, width):
    if k is None:
        return 0, OWN
    upward = up if k == 0 else 1 - up
    return upward * (OWN - width), width


def landing(k, up, width):
    if k is None:
        return width, OWN
    upward = up if k == 0 else 1 - up
    return upward * (OWN + width), width


def rows8(start):
    return pl.multiple_of(start * 8, 8) if not isinstance(start, int) else start * 8


def part_shape(part, width):
    return [OWN if k is None else width for k in part]


def take(ref, part, flags, width):
    sx, nx = span(part[0], flags[UP_X], width)
    sy, ny = span(part[1], flags[UP_Y], width)
    return ref[pl.ds(sx, nx), pl.ds(rows8(sy), ny * 8), :].reshape(nx * ny * 8, 128)


def place(ref, value, part, flags, width):
    dx, nx = landing(part[0], flags[UP_X], width)
    dy, ny = landing(part[1], flags[UP_Y], width)
    valid = present(part[0], flags, 0) * present(part[1], flags, 1)
    value = value * valid.astype(F32) if not isinstance(valid, int) else value
    ref[pl.ds(dx, nx), pl.ds(rows8(dy), ny * 8), :] = value.reshape(nx, ny * 8, 128)


def present(k, flags, dim):
    if k is None:
        return 1
    up, low, high = flags[(UP_X, UP_Y)[dim]], flags[(LOW_X, LOW_Y)[dim]], flags[(HIGH_X, HIGH_Y)[dim]]
    upward = up if k == 0 else 1 - up
    return upward * high + (1 - upward) * low


def young_place(e):
    return (e if e <= 2 else 7 if e == 3 else e + 4) + HALO_F


def split_store(z, x, s_ref, t_ref):
    count = z.shape[0]
    hi = z.astype(BF16).astype(F32)
    lo = z - hi
    s_ref[x, : count * 16, :] = jnp.concatenate([hi, lo], axis=1).astype(BF16).reshape(count * 16, 128)
    row = iota(z.shape, 1)
    nxt = next_even(jnp.where(row < 3, hi, pltpu.roll(lo, 3, 1)))
    if count % 2:
        nxt = jnp.concatenate([nxt, nxt[count - 1 :]], axis=0)
        count += 1
    t_ref[x, : count * 8, :] = nxt.reshape(count // 2, 16, 128).astype(BF16).reshape(count * 8, 128)


def next_even(z):
    count = z.shape[0]
    moved = pltpu.roll(z.reshape(count * 8, 128), 127, 1)
    return jnp.where(iota(moved.shape, 1) < 127, moved, 0.0).reshape(count, 8, 128)


def element_operand(s_ref, t_ref, x, y, pair):
    pieces = [s_ref[x + a, pl.ds(y * 16, 48), :] for a in range(3)]
    pieces += [t_ref[x + a, pl.ds(pair * 16, 32), :] for a in range(3)]
    pieces.append(jnp.zeros((16, 128), BF16))
    return jnp.concatenate(pieces, axis=0)


def products(matrix_ref, s_ref, t_ref, x, j):
    operand = jnp.concatenate(
        [element_operand(s_ref, t_ref, x, 2 * e, e) for e in (j, j + 1)], axis=1
    )
    out = jnp.dot(matrix_ref[...], operand, preferred_element_type=F32)
    out = out[:120] + out[120:]
    return out[:, :128], out[:, 128:]


def apply(matrix_ref, s_ref, t_ref, young_ref, w_ref, o_ref, count_x, pairs_y, young_at):
    w_ref[: 2 * count_x + 1] = jnp.zeros((2 * count_x + 1,) + w_ref.shape[1:], F32)
    o_ref[: 2 * count_x + 1] = jnp.zeros((2 * count_x + 1,) + o_ref.shape[1:], F32)

    def row(i, carry):
        for j in range(0, 2 * pairs_y, 2):
            both = products(matrix_ref, s_ref, t_ref, 2 * i, j)
            for e in range(2):
                k = j + e
                out = both[e] * young_ref[i + young_at, k + young_at : k + young_at + 1, :]
                for a in range(3):
                    w_ref[2 * i + a, 16 * k : 16 * k + 24, :] += out[24 * a : 24 * a + 24]
                    o_ref[2 * i + a, 8 * k : 8 * k + 16, :] += out[72 + 16 * a : 88 + 16 * a]
        return carry

    lax.fori_loop(0, count_x, row, 0)


def collect(w_ref, o_ref, x, low, count):
    half = (count + 1) // 2
    moved = pltpu.roll(o_ref[x, 4 * low : 4 * low + 8 * half, :], 1, 1)
    moved = jnp.where(iota(moved.shape, 1) > 0, moved, 0.0).reshape(half, 8, 128)
    row = iota(moved.shape, 1)
    even = jnp.where(row < 3, moved, 0.0)
    odd = jnp.where(row < 3, pltpu.roll(moved, 5, 1), 0.0)
    both = jnp.stack([even, odd], axis=1).reshape(2 * half, 8, 128)[:count]
    return w_ref[x, 8 * low : 8 * (low + count), :].reshape(count, 8, 128) + both


def load_columns(ref, x, low, count):
    return ref[x, 8 * low : 8 * (low + count), :].reshape(count, 8, 128)


def store_columns(ref, x, value):
    ref[x, : 8 * value.shape[0], :] = value.reshape(8 * value.shape[0], 128)


def prepare_kernel(flags, force, load_mask, support, start, density, passive, u_ref, f_ref, *sends):
    matrix = parity_matrix(False)
    rho = jnp.where(passive[...] == 1, 1.0, density[...])
    young = EMIN + (1.0 - EMIN) * rho * rho * rho
    factor = jnp.where(passive[...] == 1, 0.0, -3.0 * (1.0 - EMIN) * rho * rho)
    for x in range(OWN):
        free = (1 - support[x]).astype(F32)
        loaded = free * load_mask[x].astype(F32)
        rows = [free * start[c, x] for c in range(3)] + [loaded * force[c, x] for c in range(3)] + [free]
        split = exact_product(jnp.concatenate(rows, axis=0), matrix)
        for index in range(7):
            ref, row = ((u_ref, index), (f_ref, index - 3), (u_ref, 6))[index // 3]
            step = 1 if index == 6 else 3
            for parity in range(2):
                ref[x, pl.ds(row + parity * step, 8, stride=8), :] = split[
                    8 * index : 8 * index + 8, 128 * parity : 128 * parity + 128
                ]
        element = {0: 0, 1: 1, 2: 2, 5: 1, 6: 2, 7: 3}.get(x)
        for row, values in ((6, young), (7, factor)):
            if element is None:
                column = jnp.zeros((8, 128), F32)
            else:
                column = jnp.concatenate(
                    [values[element, :3], jnp.zeros((2, 128), F32), values[element, 1:]], axis=0
                )
            f_ref[x, pl.ds(row, 8, stride=8), :] = column
    for part, send in zip(PARTS, sends):
        first = take(u_ref, part, flags, HALO_U)
        send[: first.shape[0], :] = first
        send[first.shape[0] :, :] = take(f_ref, part, flags, HALO_F)


def first_kernel(flags, matrix, diag, u_own, f_own, *rest):
    received, rest = rest[:8], rest[8:]
    (z0_ref, u_ref, dinv, young, factor, w0_ref, w1_ref, z1_ref), rest = rest[:8], rest[8:]
    sends, (u_reg, f_reg, s_ref, t_ref, w_ref, o_ref) = rest[:8], rest[8:]
    u_reg[HALO_U : HALO_U + OWN, 8 * HALO_U : 8 * (HALO_U + OWN), :] = u_own[...]
    f_reg[HALO_F : HALO_F + OWN, 8 * HALO_F : 8 * (HALO_F + OWN), :] = f_own[...]
    for part, value in zip(PARTS, received):
        nx, ny = part_shape(part, HALO_U)
        place(u_reg, value[: nx * ny * 8, :], part, flags, HALO_U)
        place(f_reg, value[nx * ny * 8 :, :], part, flags, HALO_F)
    zero = jnp.zeros((1, 128), F32)
    for e in range(-3, 7):
        rows = [f_reg[young_place(e), 8 * young_place(f) + 6 : 8 * young_place(f) + 7, :] for f in range(-3, 7)]
        young[e + 3] = jnp.concatenate(rows + [zero] * 6, axis=0)
    for e in range(-1, 5):
        rows = [f_reg[young_place(e), 8 * young_place(f) + 7 : 8 * young_place(f) + 8, :] for f in range(-1, 5)]
        factor[e + 1] = jnp.concatenate(rows + [zero] * 2, axis=0)

    def inverse(x, pa, near):
        free = load_columns(u_reg, x + 1, 1, 17)
        below = jnp.concatenate([jnp.zeros((1, 128), F32), near[:15]], axis=0)
        sums = (near + below, near)
        cols = []
        for y in range(17):
            pb, f = y % 2, y // 2 + 1
            total = jnp.broadcast_to(sums[pb][f : f + 1], (8, 128))
            before = jnp.where(iota((8, 128), 1) > 0, pltpu.roll(total, 1, 1), 0.0)
            row = iota((8, 128), 0)
            held = jnp.where(row < 3, total + before, total) * diag[pa * 2 + pb]
            even = jnp.broadcast_to(free[y, 6:7], (8, 128))
            odd = jnp.broadcast_to(free[y, 7:8], (8, 128))
            open_ = jnp.where(row < 3, even, jnp.where(row < 6, odd, 0.0))
            cols.append(open_ / (open_ * held + (1.0 - open_)))
        dinv[x] = jnp.concatenate(cols, axis=0)

    def pair(e, carry):
        inverse(2 * e, 0, young[e] + young[e + 1])

        @pl.when(e < 8)
        def _():
            inverse(2 * e + 1, 1, young[e + 1])

        return carry

    lax.fori_loop(0, 9, pair, 0)

    def operand(x, carry):
        split_store(load_columns(u_reg, x + 1, 1, 17), x, s_ref, t_ref)
        return carry

    lax.fori_loop(0, 17, operand, 0)
    apply(matrix, s_ref, t_ref, young, w_ref, o_ref, 8, 4, 1)

    def residual(x, carry):
        image = collect(w_ref, o_ref, x + 2, 2, 13)
        inv = load_columns(dinv, x + 2, 2, 13)
        res = load_columns(f_reg, x + 1, 1, 13) - image
        z0 = inv * res
        store_columns(z0_ref, x, z0)
        store_columns(u_ref, x, load_columns(u_reg, x + 3, 3, 13))

        @pl.when(jnp.logical_and(x >= 2, x < 10))
        def _():
            store_columns(w0_ref, x - 2, jnp.where(inv > 0.0, res, 0.0)[2:10])

        return carry

    lax.fori_loop(0, 13, residual, 0)

    def operand_0(x, carry):
        split_store(load_columns(z0_ref, x, 0, 13), x, s_ref, t_ref)
        return carry

    lax.fori_loop(0, 13, operand_0, 0)
    apply(matrix, s_ref, t_ref, young, w_ref, o_ref, 5, 3, 2)

    def image_1(x, carry):
        image = collect(w_ref, o_ref, x + 2, 2, 8)
        inv = load_columns(dinv, x + 4, 4, 8)
        store_columns(w1_ref, x, jnp.where(inv > 0.0, image, 0.0))
        store_columns(z1_ref, x, inv * image)
        return carry

    lax.fori_loop(0, OWN, image_1, 0)
    for part, send in zip(PARTS, sends):
        send[...] = take(z1_ref, part, flags, HALO_Z)


def second_kernel(flags, matrix, z1_own, dinv, young, w0_ref, w1_ref, z0_ref, u_ref, f_own, *rest):
    received, rest = rest[:8], rest[8:]
    (z1_ref, z2_ref, z3_ref, sums_ref), rest = rest[:4], rest[4:]
    z_reg, z2_reg, s_ref, t_ref, w_ref, o_ref, w2_ref, w3_ref, w4_ref, table = rest
    z_reg[HALO_Z : HALO_Z + OWN, 8 * HALO_Z : 8 * (HALO_Z + OWN), :] = z1_own[...]
    for part, value in zip(PARTS, received):
        place(z_reg, value[...], part, flags, HALO_Z)

    def operand_1(x, carry):
        split_store(load_columns(z_reg, x + 1, 1, 21), x, s_ref, t_ref)
        return carry

    lax.fori_loop(0, 21, operand_1, 0)

    def keep(x, carry):
        store_columns(z1_ref, x, load_columns(z_reg, x + 5, 5, 13))
        return carry

    lax.fori_loop(0, 13, keep, 0)
    apply(matrix, s_ref, t_ref, young, w_ref, o_ref, 10, 5, 0)

    def image_2(x, carry):
        image = collect(w_ref, o_ref, x + 2, 2, 17)
        inv = load_columns(dinv, x, 0, 17)
        z2 = inv * image
        split_store(z2, x, s_ref, t_ref)

        @pl.when(jnp.logical_and(x >= 2, x < 15))
        def _():
            store_columns(z2_ref, x - 2, z2[2:15])

        @pl.when(jnp.logical_and(x >= 4, x < 12))
        def _():
            store_columns(w2_ref, x - 4, jnp.where(inv > 0.0, image, 0.0)[4:12])

        return carry

    lax.fori_loop(0, 17, image_2, 0)
    apply(matrix, s_ref, t_ref, young, w_ref, o_ref, 8, 4, 1)

    def image_3(x, carry):
        image = collect(w_ref, o_ref, x + 2, 2, 13)
        inv = load_columns(dinv, x + 2, 2, 13)
        z3 = inv * image
        split_store(z3, x, s_ref, t_ref)
        store_columns(z3_ref, x, z3)

        @pl.when(jnp.logical_and(x >= 2, x < 10))
        def _():
            store_columns(w3_ref, x - 2, jnp.where(inv > 0.0, image, 0.0)[2:10])

        return carry

    lax.fori_loop(0, 13, image_3, 0)
    apply(matrix, s_ref, t_ref, young, w_ref, o_ref, 5, 3, 2)
    table[...] = jnp.zeros(table.shape, F32)

    def dots(x, carry):
        inv = load_columns(dinv, x + 4, 4, 8)
        w4 = jnp.where(inv > 0.0, collect(w_ref, o_ref, x + 2, 2, 8), 0.0)
        w = [load_columns(ref, x, 0, 8) for ref in (w0_ref, w1_ref, w2_ref, w3_ref)] + [w4]
        z = [inv * value for value in w[:4]]
        load = jnp.where(inv > 0.0, load_columns(f_own, x, 0, 8), 0.0)
        u = load_columns(u_ref, x + 2, 2, 8)
        for index, (first, second) in enumerate(dot_list()):
            first = u if first is None else (w if first[0] == "w" else z)[first[1]]
            second = load if second is None else w[second[1]]
            table[index : index + 1, :] += jnp.sum(
                jnp.sum(first * second, axis=0), axis=0, keepdims=True
            )
        return carry

    lax.fori_loop(0, OWN, dots, 0)
    totals = jnp.sum(table[...], axis=1, keepdims=True)
    shape = table.shape
    line = jnp.sum(
        jnp.where(iota(shape, 0) == iota(shape, 1), jnp.broadcast_to(totals, shape), 0.0),
        axis=0,
        keepdims=True,
    )
    sums_ref[...] = jnp.broadcast_to(line, sums_ref.shape)


def dot_list():
    out = [(("w", i), ("w", j)) for i in range(5) for j in range(i, 5)]
    out += [(None, None)] + [(("z", i), None) for i in range(4)]
    out += [(None, ("w", j)) for j in range(5)]
    out += [(("z", i), ("w", j)) for i in range(4) for j in range(5)]
    return out


def step_sizes(total):
    place_of = {pair: index for index, pair in enumerate(dot_list())}

    def gram(i, j):
        return total(place_of[("w", min(i, j)), ("w", max(i, j))])

    one = jnp.ones((1, 128), F32)
    poly = [one]
    coef = [jnp.zeros((1, 128), F32)] * SWEEPS
    for sweep in range(SWEEPS):
        top = sum(poly[i] * poly[j] * gram(i, j + 1) for i in range(sweep + 1) for j in range(sweep + 1))
        bottom = sum(
            poly[i] * poly[j] * gram(i + 1, j + 1) for i in range(sweep + 1) for j in range(sweep + 1)
        )
        omega = top / bottom
        for i in range(sweep + 1):
            coef[i] = coef[i] + omega * poly[i]
        poly = [
            (poly[i] if i <= sweep else 0.0) - (omega * poly[i - 1] if i else 0.0)
            for i in range(sweep + 2)
        ]
    work = total(place_of[None, None])
    for i in range(SWEEPS):
        work = work + coef[i] * total(place_of[("z", i), None])
    for j in range(SWEEPS + 1):
        part = total(place_of[None, ("w", j)])
        for i in range(SWEEPS):
            part = part + coef[i] * total(place_of[("z", i), ("w", j)])
        work = work - poly[j] * part
    return coef, work


def last_kernel(flags, matrix, sums, u_ref, z0_ref, z1_ref, z2_ref, z3_ref, factor, *rest):
    (out_u, out_f, out_c), (own, s_ref, t_ref, uf_ref, tf_ref, sens_ref) = rest[:3], rest[3:]
    line = jnp.sum(sums[...], axis=0, keepdims=True)
    shape = (48, 128)
    spread = jnp.where(iota(shape, 0) == iota(shape, 1), jnp.broadcast_to(line, shape), 0.0)
    spread = jnp.broadcast_to(jnp.sum(spread, axis=1, keepdims=True), shape)
    coef, work = step_sizes(lambda index: spread[index : index + 1])
    out_c[...] = work

    def combine(x, carry):
        value = load_columns(u_ref, x, 0, 13)
        for index, ref in enumerate((z0_ref, z1_ref, z2_ref, z3_ref)):
            value = value + coef[index] * load_columns(ref, x, 0, 13)
        store_columns(uf_ref, x, value)
        split_store(value, x, s_ref, t_ref)
        row = iota((7, 8, 128), 1)
        even = jnp.concatenate([value[y : y + 1] for y in range(0, 13, 2)], axis=0)
        odd = jnp.concatenate([value[min(y, 12) : min(y, 12) + 1] for y in range(1, 14, 2)], axis=0)
        nxt = next_even(jnp.where(row < 3, even, pltpu.roll(odd, 3, 1)))
        store_columns(tf_ref, x, nxt)

        @pl.when(jnp.logical_and(x >= 2, x < 10))
        def _():
            store_columns(own, x - 2, value[2:10])

        return carry

    lax.fori_loop(0, 13, combine, 0)

    def energies(i, carry):
        for j in range(0, 6, 2):
            both = products(matrix, s_ref, t_ref, 2 * i, j)
            for e in range(2):
                k = j + e
                acc = jnp.zeros((8, 128), F32)
                for a in range(3):
                    left = uf_ref[2 * i + a, 16 * k : 16 * k + 24, :] * both[e][24 * a : 24 * a + 24]
                    right = tf_ref[2 * i + a, 8 * k : 8 * k + 16, :] * both[e][72 + 16 * a : 88 + 16 * a]
                    acc = acc + left[:8] + left[8:16] + left[16:] + right[:8] + right[8:]
                sens_ref[i, k : k + 1, :] = jnp.sum(acc, axis=0, keepdims=True)
        sens_ref[i, 6:8, :] = jnp.zeros((2, 128), F32)
        return carry

    lax.fori_loop(0, 6, energies, 0)
    edge = RADIUS - 1.0
    corner = RADIUS - math.sqrt(2.0)
    row = iota((8, 128), 0)
    lane = iota((8, 128), 1)
    sens = [sens_ref[x] * factor[x] for x in range(6)]
    low, high = flags[LOW_Y].astype(F32), flags[HIGH_Y].astype(F32)
    inside = jnp.where(row == 0, low, jnp.where(row < 5, 1.0, jnp.where(row == 5, high, 0.0)))
    inside_x = [flags[LOW_X].astype(F32)] + [1.0] * 4 + [flags[HIGH_X].astype(F32)]
    covered = [inside * value for value in inside_x]

    def along_y(v):
        return pltpu.roll(v, 1, 0) + pltpu.roll(v, 7, 0)

    def along_z(v):
        return jnp.where(lane > 0, pltpu.roll(v, 1, 1), 0.0) + jnp.where(lane < 127, pltpu.roll(v, 127, 1), 0.0)

    def gathered(layers, x):
        here, sides = layers[x], layers[x - 1] + layers[x + 1]
        ys = along_y(here)
        return (
            RADIUS * here
            + edge * (ys + along_z(here) + sides)
            + corner * (along_z(ys) + along_y(sides) + along_z(sides))
        )

    for x in range(ELEMS):
        out_f[x] = (gathered(sens, x + 1) / gathered(covered, x + 1))[1:5]
    merge = parity_matrix(True)
    for x in range(OWN):
        rows = [
            jnp.concatenate(
                [own[x, pl.ds(comp + 3 * parity, 8, stride=8), :] for parity in range(2)], axis=1
            )
            for comp in range(3)
        ]
        joined = exact_product(jnp.concatenate(rows, axis=0), merge)
        for comp in range(3):
            out_u[comp, x] = joined[8 * comp : 8 * comp + 8]


def partners(part, count_x, count_y):
    def other(i, k, count):
        if k is None:
            return i
        if k == 0:
            return i ^ 1
        return ((i + 1) ^ 1) - 1 if 0 < i < count - 1 else None

    out = []
    for x in range(count_x):
        for y in range(count_y):
            px, py = other(x, part[0], count_x), other(y, part[1], count_y)
            if px is None and py is None:
                px, py = count_x - 1 - x, y
            elif px is None:
                px, py = x, (y ^ 1 if part[1] is None else py)
            elif py is None:
                px, py = (x ^ 1 if part[0] is None else px), y
            out.append((x * count_y + y, px * count_y + py))
    return out


def shapes(*items):
    return [jax.ShapeDtypeStruct(item, F32) for item in items]


def call(kernel, out_shape, scratch, operands):
    spec = pl.BlockSpec(memory_space=pltpu.VMEM)
    return pl.pallas_call(
        kernel,
        out_shape=out_shape,
        in_specs=[pl.BlockSpec(memory_space=pltpu.SMEM)] + [spec] * (len(operands) - 1),
        out_specs=[spec] * len(out_shape),
        scratch_shapes=scratch,
        compiler_params=pltpu.CompilerParams(vmem_limit_bytes=48 * 1024 * 1024),
    )(*operands)


def body(force, load_mask, support_mask, start_field, density, passive_mask):
    count_x, count_y = lax.axis_size("sx"), lax.axis_size("sy")
    devices = count_x * count_y
    index_x, index_y = lax.axis_index("sx"), lax.axis_index("sy")
    flags = jnp.stack(
        [
            1 - index_x % 2,
            1 - index_y % 2,
            jnp.minimum(index_x, 1),
            jnp.minimum(count_x - 1 - index_x, 1),
            jnp.minimum(index_y, 1),
            jnp.minimum(count_y - 1 - index_y, 1),
        ]
    ).astype(jnp.int32)
    stiff = element_matrix()
    matrix = jnp.asarray(operator_matrix(stiff))
    diag = jnp.asarray(diagonal_columns(stiff))

    def swap(values):
        return [
            lax.ppermute(value, ("sx", "sy"), partners(part, count_x, count_y))
            for part, value in zip(PARTS, values)
        ]

    def sizes(width):
        return [math.prod(part_shape(part, width)) * 8 for part in PARTS]

    own = (OWN, OWN * 8, 128)
    middle = (13, 13 * 8, 128)
    first = call(
        prepare_kernel,
        shapes(own, own, *((a + b, 128) for a, b in zip(sizes(HALO_U), sizes(HALO_F)))),
        [],
        [flags, force, load_mask, support_mask, start_field, density, passive_mask],
    )
    u_own, f_own = first[:2]
    second = call(
        first_kernel,
        shapes(
            middle,
            middle,
            (17, 17 * 8, 128),
            (10, 16, 128),
            (6, 8, 128),
            own,
            own,
            own,
            *((a, 128) for a in sizes(HALO_Z)),
        ),
        [
            pltpu.VMEM((18, 18 * 8, 128), F32),
            pltpu.VMEM((14, 14 * 8, 128), F32),
            pltpu.VMEM((17, 17 * 16, 128), BF16),
            pltpu.VMEM((17, 9 * 16, 128), BF16),
            pltpu.VMEM((17, 17 * 8, 128), F32),
            pltpu.VMEM((17, 9 * 8, 128), F32),
        ],
        [flags, matrix, diag, u_own, f_own, *swap(first[2:])],
    )
    z0, u0, dinv, young, factor, w0, w1, z1 = second[:8]
    z1, z2, z3, sums = call(
        second_kernel,
        shapes(middle, middle, middle, (devices, 128)),
        [
            pltpu.VMEM((22, 22 * 8, 128), F32),
            pltpu.VMEM((8, 128), F32),
            pltpu.VMEM((21, 21 * 16, 128), BF16),
            pltpu.VMEM((21, 11 * 16, 128), BF16),
            pltpu.VMEM((21, 21 * 8, 128), F32),
            pltpu.VMEM((21, 11 * 8, 128), F32),
            pltpu.VMEM(own, F32),
            pltpu.VMEM(own, F32),
            pltpu.VMEM(own, F32),
            pltpu.VMEM((48, 128), F32),
        ],
        [flags, matrix, z1, dinv, young, w0, w1, z0, u0, f_own, *swap(second[8:])],
    )
    sums = lax.all_to_all(sums, ("sx", "sy"), 0, 0, tiled=True)
    displacement, filtered, compliance = call(
        last_kernel,
        shapes(start_field.shape, density.shape, (1, 128)),
        [
            pltpu.VMEM(own, F32),
            pltpu.VMEM((13, 13 * 16, 128), BF16),
            pltpu.VMEM((13, 7 * 16, 128), BF16),
            pltpu.VMEM(middle, F32),
            pltpu.VMEM((13, 7 * 8, 128), F32),
            pltpu.VMEM((6, 8, 128), F32),
        ],
        [flags, matrix, sums, u0, z0, z1, z2, z3, factor],
    )
    return displacement, filtered, compliance[0, 0]


def solution(mesh):
    in_specs = (
        P(None, "sx", "sy", None),
        P("sx", "sy", None),
        P("sx", "sy", None),
        P(None, "sx", "sy", None),
        P("sx", "sy", None),
        P("sx", "sy", None),
    )
    out_specs = (P(None, "sx", "sy", None), P("sx", "sy", None), P())
    return jax.shard_map(body, mesh=mesh, in_specs=in_specs, out_specs=out_specs, check_vma=False)
```

```python
import functools
import math

import jax
import jax.numpy as jnp
import numpy as np
from jax import lax
from jax.experimental import pallas as pl
from jax.experimental.pallas import tpu as pltpu
from jax.sharding import PartitionSpec as P

SWEEPS = 4
EMIN = 0.001
RADIUS = 1.5

OWN = 8
ELEMS = OWN // 2
HALO_U = 5
HALO_F = 3
HALO_Z = 7
PARTS = [
    (None, 0),
    (None, 1),
    (1, 0),
    (1, 1),
    (1, None),
    (0, None),
]
MATE = (0, None)
UP_X, UP_Y, LOW_X, HIGH_X, LOW_Y, HIGH_Y = range(6)
SHIFTS = (0.59, 0.73, 0.645, 0.69)
F32 = jnp.float32
BF16 = jnp.bfloat16


def element_matrix():
    poisson = 0.3
    lame_first = poisson / ((1.0 + poisson) * (1.0 - 2.0 * poisson))
    shear = 1.0 / (2.0 * (1.0 + poisson))
    elastic = np.zeros((6, 6))
    elastic[:3, :3] = lame_first
    for entry in range(3):
        elastic[entry, entry] += 2.0 * shear
        elastic[entry + 3, entry + 3] = shear
    points = [-math.sqrt(0.6), 0.0, math.sqrt(0.6)]
    weights = [5.0 / 9.0, 8.0 / 9.0, 5.0 / 9.0]

    def values(point):
        return np.array(
            [point * (point - 1.0) / 2.0, 1.0 - point * point, point * (point + 1.0) / 2.0]
        )

    def slopes(point):
        return np.array([point - 0.5, -2.0 * point, point + 0.5])

    stiff = np.zeros((81, 81))
    for first in range(3):
        for second in range(3):
            for third in range(3):
                val_x, val_y, val_z = (
                    values(points[first]),
                    values(points[second]),
                    values(points[third]),
                )
                der_x, der_y, der_z = (
                    slopes(points[first]),
                    slopes(points[second]),
                    slopes(points[third]),
                )
                strain = np.zeros((6, 81))
                for node_a in range(3):
                    for node_b in range(3):
                        for node_c in range(3):
                            node = node_a * 9 + node_b * 3 + node_c
                            grad_x = 2.0 * der_x[node_a] * val_y[node_b] * val_z[node_c]
                            grad_y = 2.0 * val_x[node_a] * der_y[node_b] * val_z[node_c]
                            grad_z = 2.0 * val_x[node_a] * val_y[node_b] * der_z[node_c]
                            strain[0, node] = grad_x
                            strain[1, 27 + node] = grad_y
                            strain[2, 54 + node] = grad_z
                            strain[3, node] = grad_y
                            strain[3, 27 + node] = grad_x
                            strain[4, 27 + node] = grad_z
                            strain[4, 54 + node] = grad_y
                            strain[5, node] = grad_z
                            strain[5, 54 + node] = grad_x
                factor = weights[first] * weights[second] * weights[third] * 0.125
                stiff = stiff + factor * strain.T @ elastic @ strain
    return stiff.astype(np.float32)


def operator_matrix(stiff):
    hi = stiff.astype(BF16).astype(np.float32)
    lo = stiff - hi
    out = np.zeros((240, 256), np.float32)

    def out_row(comp, a, b, c):
        if c < 2:
            return 80 * a + b * 8 + c * 3 + comp
        return 80 * a + 24 + (b // 2) * 8 + (b % 2) * 3 + comp

    def in_row(comp, a, b, c, low):
        if c < 2:
            return (a * 3 + b) * 16 + low * 8 + c * 3 + comp
        return 144 + (a * 2 + b // 2) * 16 + (b % 2) * 8 + low * 3 + comp

    index = [(p, a, b, c) for p in range(3) for a in range(3) for b in range(3) for c in range(3)]
    for i, first in enumerate(index):
        for j, second in enumerate(index):
            row = out_row(*first)
            out[row, in_row(*second, 0)] = hi[i, j]
            out[row, in_row(*second, 1)] = hi[i, j]
            out[row + 40, in_row(*second, 0)] = lo[i, j]
    return out.astype(BF16)


def diagonal_columns(stiff):
    out = np.zeros((4, 8, 128), np.float32)
    for pa in range(2):
        for pb in range(2):
            for c in range(2):
                for comp in range(3):
                    dof = comp * 27 + pa * 9 + pb * 3 + c
                    out[pa * 2 + pb, c * 3 + comp] = 1.0 / stiff[dof, dof]
    return out


def iota(shape, dim):
    return lax.broadcasted_iota(jnp.int32, shape, dim)


def parity_matrix(transposed):
    node = iota((256, 256), 1 if transposed else 0)
    place = iota((256, 256), 0 if transposed else 1)
    return (node == 2 * (place % 128) + place // 128).astype(F32).astype(BF16)


def exact_product(rows, matrix):
    first = rows.astype(BF16)
    left = rows - first.astype(F32)
    second = left.astype(BF16)
    third = (left - second.astype(F32)).astype(BF16)
    stacked = jnp.concatenate([first, second, third], axis=0)
    out = jnp.dot(stacked, matrix, preferred_element_type=F32)
    count = rows.shape[0]
    return out[:count] + out[count : 2 * count] + out[2 * count :]


def span(k, up, width):
    if k is None:
        return 0, OWN
    upward = up if k == 0 else 1 - up
    return upward * (OWN - width), width


def landing(k, up, width, margin):
    if k is None:
        return margin, OWN
    upward = up if k == 0 else 1 - up
    return upward * (OWN + margin) + (1 - upward) * (margin - width), width


def rows8(start):
    return pl.multiple_of(start * 8, 8) if not isinstance(start, int) else start * 8


def part_shape(part, width):
    return [OWN if k is None else width for k in part]


def take(ref, part, flags, width):
    sx, nx = span(part[0], flags[UP_X], width)
    sy, ny = span(part[1], flags[UP_Y], width)
    return ref[pl.ds(sx, nx), pl.ds(rows8(sy), ny * 8), :].reshape(nx * ny * 8, 128)


def place(ref, value, part, flags, width, passed=False):
    dx, nx = landing(part[0], flags[UP_X], OWN if passed else width, OWN)
    dy, ny = landing(part[1], flags[UP_Y], width, width)
    valid = present(part[0], flags, 0) * present(part[1], flags, 1)
    value = value * valid.astype(F32)
    ref[pl.ds(dx, nx), pl.ds(rows8(dy), ny * 8), :] = value.reshape(nx, ny * 8, 128)


def position():
    index = [lax.axis_index(axis) for axis in ("sx", "sy")]
    last = [lax.axis_size(axis) - 1 for axis in ("sx", "sy")]
    out = [1 - lax.rem(i, 2) for i in index]
    for i, end in zip(index, last):
        out += [jnp.minimum(i, 1), jnp.minimum(end - i, 1)]
    return out


def dense(cols):
    count = cols.shape[0] // 4
    c = cols.reshape(count, 4, 8, 128)
    row = iota((count, 8, 128), 1)
    tiles = [
        jnp.where(row < 6, c[:, 0], pltpu.roll(c[:, 1], 6, 1)),
        jnp.where(row < 4, pltpu.roll(c[:, 1], 6, 1), pltpu.roll(c[:, 2], 4, 1)),
        jnp.where(row < 2, pltpu.roll(c[:, 2], 4, 1), pltpu.roll(c[:, 3], 2, 1)),
    ]
    return jnp.stack(tiles, axis=1).reshape(count * 24, 128)


def sparse(rows):
    count = rows.shape[0] // 24
    t = rows.reshape(count, 3, 8, 128)
    row = iota((count, 8, 128), 1)
    cols = [
        t[:, 0],
        jnp.where(row < 2, pltpu.roll(t[:, 0], 2, 1), pltpu.roll(t[:, 1], 2, 1)),
        jnp.where(row < 4, pltpu.roll(t[:, 1], 4, 1), pltpu.roll(t[:, 2], 4, 1)),
        pltpu.roll(t[:, 2], 6, 1),
    ]
    return jnp.stack(cols, axis=1).reshape(count * 4, 8, 128)


def column_count(part, width):
    return math.prod(part_shape(part, width))


def present(k, flags, dim):
    if k is None:
        return 1
    up, low, high = flags[(UP_X, UP_Y)[dim]], flags[(LOW_X, LOW_Y)[dim]], flags[(HIGH_X, HIGH_Y)[dim]]
    upward = up if k == 0 else 1 - up
    return upward * high + (1 - upward) * low


def young_place(e):
    return e if e <= 2 else 7 if e == 3 else e + 4


def moduli_row(f_reg, e, f, row):
    start = 8 * (young_place(f) + HALO_F) + row
    return f_reg[young_place(e) + OWN, start : start + 1, :]


def split_store(z, x, s_ref, t_ref):
    count = z.shape[0]
    far = z * 65537.0
    hi = far - (far - z)
    lo = z - hi
    s_ref[x, : count * 16, :] = jnp.concatenate([hi, lo], axis=1).astype(BF16).reshape(count * 16, 128)
    row = iota(z.shape, 1)
    nxt = next_even(jnp.where(row < 3, hi, pltpu.roll(lo, 3, 1)))
    if count % 2:
        nxt = jnp.concatenate([nxt, nxt[count - 1 :]], axis=0)
        count += 1
    t_ref[x, : count * 8, :] = nxt.reshape(count // 2, 16, 128).astype(BF16).reshape(count * 8, 128)


def next_even(z):
    count = z.shape[0]
    moved = pltpu.roll(z.reshape(count * 8, 128), 127, 1)
    return jnp.where(iota(moved.shape, 1) < 127, moved, 0.0).reshape(count, 8, 128)


def element_operand(s_ref, t_ref, x, y, pair):
    pieces = [s_ref[x + a, pl.ds(y * 16, 48), :] for a in range(3)]
    pieces += [t_ref[x + a, pl.ds(pair * 16, 32), :] for a in range(3)]
    pieces.append(jnp.zeros((16, 128), BF16))
    return jnp.concatenate(pieces, axis=0)


def products(matrix, s_ref, t_ref, x, j):
    operand = jnp.concatenate(
        [element_operand(s_ref, t_ref, x, 2 * e, e) for e in (j, j + 1)], axis=1
    )
    out = jnp.dot(matrix, operand, preferred_element_type=F32)
    layers = [out[r : r + 40] + out[r + 40 : r + 80] for r in range(0, matrix.shape[0], 80)]
    return [[layer[:, :128] for layer in layers], [layer[:, 128:] for layer in layers]]


def apply(matrix_ref, s_ref, t_ref, young_ref, w_ref, o_ref, count_x, pairs_y, young_at, last=(0,)):
    for i in range(count_x):
        layers = (2,) if i == 0 else last if i == count_x - 1 else (0, 1, 2)
        matrix = matrix_ref[80 * layers[0] : 80 * (layers[-1] + 1), :]
        tails = [None] * 3
        for j in range(0, 2 * pairs_y, 2):
            both = products(matrix, s_ref, t_ref, 2 * i, j)
            for e in range(2):
                k = j + e
                scale = young_ref[i + young_at, k + young_at : k + young_at + 1, :]
                for a, out in zip(layers, both[e]):
                    out = out * scale
                    x = 2 * i + a
                    nodes, over = out[:16], out[24:32]
                    if tails[a] is not None:
                        nodes = jnp.concatenate([nodes[:8] + tails[a][0], nodes[8:]], axis=0)
                        over = over + tails[a][1]
                    if a == 0:
                        nodes = nodes + w_ref[x, 16 * k : 16 * k + 16, :]
                        over = over + o_ref[x, 8 * k : 8 * k + 8, :]
                    w_ref[x, 16 * k : 16 * k + 16, :] = nodes
                    o_ref[x, 8 * k : 8 * k + 8, :] = over
                    tails[a] = (out[16:24], out[32:40])
        k = 2 * pairs_y
        for a in layers:
            x = 2 * i + a
            nodes, over = tails[a]
            if a == 0:
                nodes = nodes + w_ref[x, 16 * k : 16 * k + 8, :]
                over = over + o_ref[x, 8 * k : 8 * k + 8, :]
            w_ref[x, 16 * k : 16 * k + 8, :] = nodes
            o_ref[x, 8 * k : 8 * k + 8, :] = over


def collect(w_ref, o_ref, x, low, count):
    half = (count + 1) // 2
    moved = pltpu.roll(o_ref[x, 4 * low : 4 * low + 8 * half, :], 1, 1)
    moved = jnp.where(iota(moved.shape, 1) > 0, moved, 0.0).reshape(half, 8, 128)
    row = iota(moved.shape, 1)
    even = jnp.where(row < 3, moved, 0.0)
    odd = jnp.where(row < 3, pltpu.roll(moved, 5, 1), 0.0)
    both = jnp.stack([even, odd], axis=1).reshape(2 * half, 8, 128)[:count]
    return w_ref[x, 8 * low : 8 * (low + count), :].reshape(count, 8, 128) + both


def load_columns(ref, x, low, count):
    return ref[x, 8 * low : 8 * (low + count), :].reshape(count, 8, 128)


def store_columns(ref, x, value):
    ref[x, : 8 * value.shape[0], :] = value.reshape(8 * value.shape[0], 128)


def prepare_kernel(fields, moduli, u_ref, f_ref, matrix_ref, diag_ref, *sends):
    flags = position()
    matrix = parity_matrix(False)
    matrix_ref[...] = fields[448:688, :].astype(BF16)
    for index in range(4):
        diag_ref[index] = fields[688 + 8 * index : 696 + 8 * index, :128]
    young, factor = moduli[0], moduli[1]
    for x in range(OWN):
        rows = [fields[64 * c + 8 * x : 64 * c + 8 * x + 8, :] for c in range(7)]
        split = exact_product(jnp.concatenate(rows, axis=0), matrix)
        for index in range(7):
            ref, row = ((u_ref, index), (f_ref, index - 3), (u_ref, 6))[index // 3]
            step = 1 if index == 6 else 3
            for parity in range(2):
                ref[x, pl.ds(row + parity * step, 8, stride=8), :] = split[
                    8 * index : 8 * index + 8, 128 * parity : 128 * parity + 128
                ]
        element = {0: 0, 1: 1, 2: 2, 5: 1, 6: 2, 7: 3}.get(x)
        for row, values in ((6, young), (7, factor)):
            if element is None:
                column = jnp.zeros((8, 128), F32)
            else:
                column = jnp.concatenate(
                    [values[element, :3], jnp.zeros((2, 128), F32), values[element, 1:]], axis=0
                )
            f_ref[x, pl.ds(row, 8, stride=8), :] = column
    for part, send in zip(PARTS, sends):
        first = take(u_ref, part, flags, HALO_U)
        send[: first.shape[0], :] = first
        send[first.shape[0] :, :] = take(f_ref, part, flags, HALO_F)


def first_kernel(matrix, diag, u_own, f_own, *rest):
    flags = position()
    received, rest = rest[:8], rest[8:]
    (z0_ref, u_ref, dinv, young, factor, w0_ref, w1_ref, z1_ref), rest = rest[:8], rest[8:]
    sends, (u_reg, f_reg, s_ref, t_ref, w_ref, o_ref) = rest[:6], rest[6:]
    u_reg[OWN : 2 * OWN, 8 * HALO_U : 8 * (HALO_U + OWN), :] = u_own[...]
    f_reg[OWN : 2 * OWN, 8 * HALO_F : 8 * (HALO_F + OWN), :] = f_own[...]
    for index, value in enumerate(received):
        passed = index >= 6
        part = (0, index - 6) if passed else PARTS[index]
        end = column_count(PARTS[index - 6] if passed else part, HALO_U) * 8
        place(u_reg, value[:end, :], part, flags, HALO_U, passed)
        place(f_reg, value[end:, :], part, flags, HALO_F, passed)
    zero = jnp.zeros((1, 128), F32)
    for e in range(-3, 7):
        rows = [moduli_row(f_reg, e, f, 6) for f in range(-3, 7)]
        young[e + 3] = jnp.concatenate(rows + [zero] * 6, axis=0)
    for e in range(-1, 5):
        rows = [moduli_row(f_reg, e, f, 7) for f in range(-1, 5)]
        factor[e + 1] = jnp.concatenate(rows + [zero] * 2, axis=0)

    def inverse(x):
        e = x // 2
        near = young[e] + young[e + 1] if x % 2 == 0 else young[e + 1]
        both = near + pltpu.roll(near, 1, 0)
        lines = {}
        for pb, total in ((0, both), (1, near)):
            before = jnp.where(iota(total.shape, 1) > 0, pltpu.roll(total, 1, 1), 0.0)
            for pc, value in ((0, total + before), (1, total)):
                lines[pb, pc] = jnp.where(value > 0.0, 1.0 / value, 0.0)
        row = iota((8, 128), 0)
        cols = []
        for y in range(17):
            pb, f = y % 2, y // 2 + 1
            even, odd = [
                lines[pb, pc][f : f + 1] * u_reg[x + 4, 8 * (y + 1) + 6 + pc : 8 * (y + 1) + 7 + pc, :]
                for pc in range(2)
            ]
            line = jnp.where(row < 3, jnp.broadcast_to(even, (8, 128)), jnp.broadcast_to(odd, (8, 128)))
            cols.append(line * diag[(x % 2) * 2 + pb])
        dinv[x] = jnp.concatenate(cols, axis=0)

    for x in range(17):
        inverse(x)

    def operand(x):
        split_store(load_columns(u_reg, x + 4, 1, 17), x, s_ref, t_ref)

    for x in range(17):
        operand(x)
    apply(matrix, s_ref, t_ref, young, w_ref, o_ref, 8, 4, 1)

    def residual(x):
        image = collect(w_ref, o_ref, x + 2, 2, 13)
        inv = load_columns(dinv, x + 2, 2, 13)
        res = load_columns(f_reg, x + 6, 1, 13) - image
        z0 = inv * res
        store_columns(z0_ref, x, z0)
        store_columns(u_ref, x, load_columns(u_reg, x + 6, 3, 13))

        if 2 <= x < 10:
            store_columns(w0_ref, x - 2, jnp.where(inv > 0.0, res, 0.0)[2:10])

    for x in range(13):
        residual(x)

    def operand_0(x):
        split_store(load_columns(z0_ref, x, 0, 13), x, s_ref, t_ref)

    for x in range(13):
        operand_0(x)
    apply(matrix, s_ref, t_ref, young, w_ref, o_ref, 5, 3, 2, last=(0, 1))

    def image_1(x):
        image = collect(w_ref, o_ref, x + 2, 2, 8)
        inv = load_columns(dinv, x + 4, 4, 8)
        image = SHIFTS[0] * jnp.where(inv > 0.0, image, 0.0)
        store_columns(w1_ref, x, load_columns(w0_ref, x, 0, 8) - image)
        store_columns(z1_ref, x, load_columns(z0_ref, x + 2, 2, 8) - inv * image)

    for x in range(OWN):
        image_1(x)
    for part, send in zip(PARTS, sends):
        cols = take(z1_ref, part, flags, HALO_Z)
        extra = send.shape[0] * 8 // 6 - cols.shape[0]
        if extra:
            cols = jnp.concatenate([cols, jnp.zeros((extra, 128), F32)], axis=0)
        send[...] = dense(cols.reshape(-1, 8, 128))


def second_kernel(matrix, z1_own, dinv, young, w0_ref, w1_ref, z0_ref, u_ref, f_own, *rest):
    received, rest = rest[:8], rest[8:]
    (z1_ref, z2_ref, z3_ref, sums_ref), rest = rest[:4], rest[4:]
    z_reg, s_ref, t_ref, w_ref, o_ref, w2_ref, w3_ref = rest
    flags = position()
    z_reg[OWN : 2 * OWN, 8 * HALO_Z : 8 * (HALO_Z + OWN), :] = z1_own[...]
    for index, value in enumerate(received):
        passed = index >= 6
        part = (0, index - 6) if passed else PARTS[index]
        count = column_count(PARTS[index - 6] if passed else part, HALO_Z)
        place(z_reg, sparse(value[...])[:count], part, flags, HALO_Z, passed)

    def operand_1(x):
        split_store(load_columns(z_reg, x + 2, 1, 21), x, s_ref, t_ref)

    for x in range(21):
        operand_1(x)

    def keep(x):
        store_columns(z1_ref, x, load_columns(z_reg, x + 6, 5, 13))

    for x in range(13):
        keep(x)
    apply(matrix, s_ref, t_ref, young, w_ref, o_ref, 10, 5, 0)

    def image_2(x):
        image = collect(w_ref, o_ref, x + 2, 2, 17)
        inv = load_columns(dinv, x, 0, 17)
        image = SHIFTS[1] * jnp.where(inv > 0.0, image, 0.0)
        z2 = load_columns(z_reg, x + 4, 3, 17) - inv * image
        split_store(z2, x, s_ref, t_ref)

        if 2 <= x < 15:
            store_columns(z2_ref, x - 2, z2[2:15])

        if 4 <= x < 12:
            store_columns(w2_ref, x - 4, load_columns(w1_ref, x - 4, 0, 8) - image[4:12])

    for x in range(17):
        image_2(x)
    apply(matrix, s_ref, t_ref, young, w_ref, o_ref, 8, 4, 1)

    def image_3(x):
        image = collect(w_ref, o_ref, x + 2, 2, 13)
        inv = load_columns(dinv, x + 2, 2, 13)
        image = SHIFTS[2] * jnp.where(inv > 0.0, image, 0.0)
        z3 = load_columns(z2_ref, x, 0, 13) - inv * image
        split_store(z3, x, s_ref, t_ref)
        store_columns(z3_ref, x, z3)

        if 2 <= x < 10:
            store_columns(w3_ref, x - 2, load_columns(w2_ref, x - 2, 0, 8) - image[2:10])

    for x in range(13):
        image_3(x)
    apply(matrix, s_ref, t_ref, young, w_ref, o_ref, 5, 3, 2, last=(0, 1))
    sums = [jnp.zeros((8, 128), F32) for _ in dot_list()]

    def dots(x):
        inv = load_columns(dinv, x + 4, 4, 8)
        w = [load_columns(ref, x, 0, 8) for ref in (w0_ref, w1_ref, w2_ref, w3_ref)]
        w.append(w[3] - SHIFTS[3] * jnp.where(inv > 0.0, collect(w_ref, o_ref, x + 2, 2, 8), 0.0))
        z = [inv * value for value in w[:4]]
        load = jnp.where(inv > 0.0, load_columns(f_own, x, 0, 8), 0.0)
        u = load_columns(u_ref, x + 2, 2, 8)
        for index, (first, second) in enumerate(dot_list()):
            first = u if first is None else (w if first[0] == "w" else z)[first[1]]
            second = load if second is None else w[second[1]]
            sums[index] += jnp.sum(first * second, axis=0)

    for x in range(OWN):
        dots(x)
    shape = (48, 128)
    lines = [jnp.sum(value, axis=0, keepdims=True) for value in sums]
    lines = jnp.concatenate(lines + [jnp.zeros((shape[0] - len(lines), 128), F32)], axis=0)
    totals = jnp.sum(lines, axis=1, keepdims=True)
    line = jnp.sum(
        jnp.where(iota(shape, 0) == iota(shape, 1), jnp.broadcast_to(totals, shape), 0.0),
        axis=0,
        keepdims=True,
    )
    sums_ref[...] = jnp.broadcast_to(line, sums_ref.shape)


def dot_list():
    out = [(("w", i), ("w", j)) for i in range(5) for j in range(i, 5)]
    out += [(None, None)] + [(("z", i), None) for i in range(4)]
    out += [(None, ("w", j)) for j in range(5)]
    out += [(("z", i), ("w", j)) for i in range(4) for j in range(i, 5)]
    return out


def step_sizes(total):
    place_of = {pair: index for index, pair in enumerate(dot_list())}

    def gram(i, j):
        return total(place_of[("w", min(i, j)), ("w", max(i, j))])

    poly = [jnp.ones((1, 128), F32)]
    coef = [jnp.zeros((1, 128), F32)] * SWEEPS
    for sweep in range(SWEEPS):
        scaled = [poly[i] / SHIFTS[i] for i in range(sweep + 1)]
        image = [scaled[0]] + [scaled[i] - scaled[i - 1] for i in range(1, sweep + 1)] + [-scaled[sweep]]
        times = [sum(gram(i, j) * image[j] for j in range(sweep + 2)) for i in range(sweep + 2)]
        top = sum(poly[i] * times[i] for i in range(sweep + 1))
        bottom = sum(image[i] * times[i] for i in range(sweep + 2))
        omega = top / bottom
        for i in range(sweep + 1):
            coef[i] = coef[i] + omega * poly[i]
        poly = [
            (poly[i] if i <= sweep else 0.0) - omega * image[i] for i in range(sweep + 2)
        ]
    work = total(place_of[None, None])
    for i in range(SWEEPS):
        work = work + coef[i] * total(place_of[("z", i), None])
    for j in range(SWEEPS + 1):
        part = total(place_of[None, ("w", j)])
        for i in range(SWEEPS):
            part = part + coef[i] * total(place_of[("z", min(i, j)), ("w", max(i, j))])
        work = work - poly[j] * part
    return coef, work


def last_kernel(matrix, sums, u_ref, z0_ref, z1_ref, z2_ref, z3_ref, factor, *rest):
    (out_u, out_f, out_c), (own, s_ref, t_ref, uf_ref, tf_ref, sens_ref) = rest[:3], rest[3:]
    flags = position()
    line = jnp.sum(sums[...], axis=0, keepdims=True)
    shape = (48, 128)
    spread = jnp.where(iota(shape, 0) == iota(shape, 1), jnp.broadcast_to(line, shape), 0.0)
    spread = jnp.broadcast_to(jnp.sum(spread, axis=1, keepdims=True), shape)
    coef, work = step_sizes(lambda index: spread[index : index + 1])
    out_c[...] = work

    def combine(x):
        value = load_columns(u_ref, x, 0, 13)
        for index, ref in enumerate((z0_ref, z1_ref, z2_ref, z3_ref)):
            value = value + coef[index] * load_columns(ref, x, 0, 13)
        store_columns(uf_ref, x, value)
        split_store(value, x, s_ref, t_ref)
        row = iota((7, 8, 128), 1)
        even = jnp.concatenate([value[y : y + 1] for y in range(0, 13, 2)], axis=0)
        odd = jnp.concatenate([value[min(y, 12) : min(y, 12) + 1] for y in range(1, 14, 2)], axis=0)
        nxt = next_even(jnp.where(row < 3, even, pltpu.roll(odd, 3, 1)))
        store_columns(tf_ref, x, nxt)

        if 2 <= x < 10:
            store_columns(own, x - 2, value[2:10])

    for x in range(13):
        combine(x)

    for i in range(6):
        for j in range(0, 6, 2):
            both = products(matrix[...], s_ref, t_ref, 2 * i, j)
            for e in range(2):
                k = j + e
                acc = jnp.zeros((8, 128), F32)
                for a in range(3):
                    left = uf_ref[2 * i + a, 16 * k : 16 * k + 24, :] * both[e][a][:24]
                    right = tf_ref[2 * i + a, 8 * k : 8 * k + 16, :] * both[e][a][24:]
                    acc = acc + left[:8] + left[8:16] + left[16:] + right[:8] + right[8:]
                sens_ref[i, k : k + 1, :] = jnp.sum(acc, axis=0, keepdims=True)
        sens_ref[i, 6:8, :] = jnp.zeros((2, 128), F32)
    edge = RADIUS - 1.0
    corner = RADIUS - math.sqrt(2.0)
    row = iota((8, 128), 0)
    lane = iota((8, 128), 1)
    sens = [sens_ref[x] * factor[x] for x in range(6)]
    low, high = flags[LOW_Y].astype(F32), flags[HIGH_Y].astype(F32)
    inside = jnp.where(row == 0, low, jnp.where(row < 5, 1.0, jnp.where(row == 5, high, 0.0)))
    inside_x = [flags[LOW_X].astype(F32)] + [1.0] * 4 + [flags[HIGH_X].astype(F32)]
    covered = [inside * value for value in inside_x]

    def along_y(v):
        return pltpu.roll(v, 1, 0) + pltpu.roll(v, 7, 0)

    def along_z(v):
        return jnp.where(lane > 0, pltpu.roll(v, 1, 1), 0.0) + jnp.where(lane < 127, pltpu.roll(v, 127, 1), 0.0)

    def gathered(layers, x):
        here, sides = layers[x], layers[x - 1] + layers[x + 1]
        ys = along_y(here)
        return (
            RADIUS * here
            + edge * (ys + along_z(here) + sides)
            + corner * (along_z(ys) + along_y(sides) + along_z(sides))
        )

    for x in range(ELEMS):
        out_f[x] = (gathered(sens, x + 1) / gathered(covered, x + 1))[1:5]
    merge = parity_matrix(True)
    for x in range(OWN):
        rows = [
            jnp.concatenate(
                [own[x, pl.ds(comp + 3 * parity, 8, stride=8), :] for parity in range(2)], axis=1
            )
            for comp in range(3)
        ]
        joined = exact_product(jnp.concatenate(rows, axis=0), merge)
        for comp in range(3):
            out_u[comp, x] = joined[8 * comp : 8 * comp + 8]


def partners(part, count_x, count_y):
    def other(i, k, count):
        if k is None:
            return i
        if k == 0:
            return i ^ 1
        return ((i + 1) ^ 1) - 1 if 0 < i < count - 1 else None

    out = []
    for x in range(count_x):
        for y in range(count_y):
            px, py = other(x, part[0], count_x), other(y, part[1], count_y)
            if px is None and py is None:
                px, py = count_x - 1 - x, y
            elif px is None:
                px, py = x, (y ^ 1 if part[1] is None else py)
            elif py is None:
                px, py = (x ^ 1 if part[0] is None else px), y
            out.append((x * count_y + y, px * count_y + py))
    return out


def shapes(*items):
    return [jax.ShapeDtypeStruct(item, F32) for item in items]


def call(kernel, out_shape, scratch, operands):
    spec = pl.BlockSpec(memory_space=pltpu.VMEM)
    return pl.pallas_call(
        kernel,
        out_shape=out_shape,
        in_specs=[spec] * len(operands),
        out_specs=[spec] * len(out_shape),
        scratch_shapes=scratch,
        compiler_params=pltpu.CompilerParams(vmem_limit_bytes=24 * 1024 * 1024),
    )(*operands)


def body(force, load_mask, support_mask, start_field, density, passive_mask):
    count_x, count_y = lax.axis_size("sx"), lax.axis_size("sy")
    devices = count_x * count_y
    stiff = element_matrix()
    constants = np.zeros((272, 256), np.float32)
    constants[:240] = operator_matrix(stiff).astype(np.float32)
    constants[240:, :128] = diagonal_columns(stiff).reshape(32, 128)
    free = (1 - support_mask).astype(F32)[None]
    load = free * load_mask.astype(F32)[None] * force
    fields = jnp.concatenate(
        [value.reshape(-1, 256) for value in (free * start_field, load, free)] + [jnp.asarray(constants)]
    )
    rho = jnp.where(passive_mask == 1, F32(1.0), density)
    young = EMIN + (1.0 - EMIN) * rho**3
    moduli = jnp.stack([young, jnp.where(passive_mask == 1, F32(0.0), -3.0 * (1.0 - EMIN) * rho**2)])

    def send(value, part):
        return lax.ppermute(value, ("sx", "sy"), partners(part, count_x, count_y))

    def swap(values):
        received = [send(value, part) for part, value in zip(PARTS, values)]
        return received + [send(value, MATE) for value in received[:2]]

    def sizes(width):
        return [column_count(part, width) for part in PARTS]

    own = (OWN, OWN * 8, 128)
    middle = (13, 13 * 8, 128)
    first = call(
        prepare_kernel,
        [
            *shapes(own, own),
            jax.ShapeDtypeStruct((240, 256), BF16),
            *shapes((4, 8, 128)),
            *shapes(*((8 * (a + b), 128) for a, b in zip(sizes(HALO_U), sizes(HALO_F)))),
        ],
        [],
        [fields, moduli],
    )
    u_own, f_own, matrix, diag = first[:4]
    second = call(
        first_kernel,
        shapes(
            middle,
            middle,
            (17, 17 * 8, 128),
            (10, 16, 128),
            (6, 8, 128),
            own,
            own,
            own,
            *(((a + 3) // 4 * 24, 128) for a in sizes(HALO_Z)),
        ),
        [
            pltpu.VMEM((24, 18 * 8, 128), F32),
            pltpu.VMEM((24, 14 * 8, 128), F32),
            pltpu.VMEM((17, 17 * 16, 128), BF16),
            pltpu.VMEM((17, 9 * 16, 128), BF16),
            pltpu.VMEM((17, 17 * 8, 128), F32),
            pltpu.VMEM((17, 9 * 8, 128), F32),
        ],
        [matrix, diag, u_own, f_own, *swap(first[4:])],
    )
    z0, u0, dinv, young, factor, w0, w1, z1 = second[:8]
    z1, z2, z3, sums = call(
        second_kernel,
        shapes(middle, middle, middle, (devices, 128)),
        [
            pltpu.VMEM((24, 22 * 8, 128), F32),
            pltpu.VMEM((21, 21 * 16, 128), BF16),
            pltpu.VMEM((21, 11 * 16, 128), BF16),
            pltpu.VMEM((21, 21 * 8, 128), F32),
            pltpu.VMEM((21, 11 * 8, 128), F32),
            pltpu.VMEM(own, F32),
            pltpu.VMEM(own, F32),
        ],
        [matrix, z1, dinv, young, w0, w1, z0, u0, f_own, *swap(second[8:])],
    )
    sums = lax.all_to_all(sums, ("sx", "sy"), 0, 0, tiled=True)
    displacement, filtered, compliance = call(
        last_kernel,
        shapes(start_field.shape, density.shape, (1, 128)),
        [
            pltpu.VMEM(own, F32),
            pltpu.VMEM((13, 13 * 16, 128), BF16),
            pltpu.VMEM((13, 7 * 16, 128), BF16),
            pltpu.VMEM(middle, F32),
            pltpu.VMEM((13, 7 * 8, 128), F32),
            pltpu.VMEM((6, 8, 128), F32),
        ],
        [matrix, sums, u0, z0, z1, z2, z3, factor],
    )
    return displacement, filtered, compliance[0, 0]


def solution(mesh):
    in_specs = (
        P(None, "sx", "sy", None),
        P("sx", "sy", None),
        P("sx", "sy", None),
        P(None, "sx", "sy", None),
        P("sx", "sy", None),
        P("sx", "sy", None),
    )
    out_specs = (P(None, "sx", "sy", None), P("sx", "sy", None), P())
    return jax.shard_map(body, mesh=mesh, in_specs=in_specs, out_specs=out_specs, check_vma=False)
```

```python
import functools
import math

import jax
import jax.numpy as jnp
import numpy as np
from jax import lax
from jax.experimental import pallas as pl
from jax.experimental.pallas import tpu as pltpu
from jax.sharding import PartitionSpec as P

SWEEPS = 4
EMIN = 0.001
RADIUS = 1.5

OWN = 8
ELEMS = OWN // 2
HALO_U = 5
HALO_F = 3
HALO_Z = 7
PARTS = [
    (None, 0),
    (None, 1),
    (1, 0),
    (1, 1),
    (1, None),
    (0, None),
]
MATE = (0, None)
UP_X, UP_Y, LOW_X, HIGH_X, LOW_Y, HIGH_Y = range(6)
SHIFTS = (0.59, 0.73, 0.645, 0.69)
F32 = jnp.float32
BF16 = jnp.bfloat16


def element_matrix():
    poisson = 0.3
    lame_first = poisson / ((1.0 + poisson) * (1.0 - 2.0 * poisson))
    shear = 1.0 / (2.0 * (1.0 + poisson))
    elastic = np.zeros((6, 6))
    elastic[:3, :3] = lame_first
    for entry in range(3):
        elastic[entry, entry] += 2.0 * shear
        elastic[entry + 3, entry + 3] = shear
    points = [-math.sqrt(0.6), 0.0, math.sqrt(0.6)]
    weights = [5.0 / 9.0, 8.0 / 9.0, 5.0 / 9.0]

    def values(point):
        return np.array(
            [point * (point - 1.0) / 2.0, 1.0 - point * point, point * (point + 1.0) / 2.0]
        )

    def slopes(point):
        return np.array([point - 0.5, -2.0 * point, point + 0.5])

    stiff = np.zeros((81, 81))
    for first in range(3):
        for second in range(3):
            for third in range(3):
                val_x, val_y, val_z = (
                    values(points[first]),
                    values(points[second]),
                    values(points[third]),
                )
                der_x, der_y, der_z = (
                    slopes(points[first]),
                    slopes(points[second]),
                    slopes(points[third]),
                )
                strain = np.zeros((6, 81))
                for node_a in range(3):
                    for node_b in range(3):
                        for node_c in range(3):
                            node = node_a * 9 + node_b * 3 + node_c
                            grad_x = 2.0 * der_x[node_a] * val_y[node_b] * val_z[node_c]
                            grad_y = 2.0 * val_x[node_a] * der_y[node_b] * val_z[node_c]
                            grad_z = 2.0 * val_x[node_a] * val_y[node_b] * der_z[node_c]
                            strain[0, node] = grad_x
                            strain[1, 27 + node] = grad_y
                            strain[2, 54 + node] = grad_z
                            strain[3, node] = grad_y
                            strain[3, 27 + node] = grad_x
                            strain[4, 27 + node] = grad_z
                            strain[4, 54 + node] = grad_y
                            strain[5, node] = grad_z
                            strain[5, 54 + node] = grad_x
                factor = weights[first] * weights[second] * weights[third] * 0.125
                stiff = stiff + factor * strain.T @ elastic @ strain
    return stiff.astype(np.float32)


def operator_matrix(stiff):
    hi = stiff.astype(BF16).astype(np.float32)
    lo = stiff - hi
    out = np.zeros((240, 256), np.float32)

    def out_row(comp, a, b, c):
        if c < 2:
            return 80 * a + b * 8 + c * 3 + comp
        return 80 * a + 24 + (b // 2) * 8 + (b % 2) * 3 + comp

    def in_row(comp, a, b, c, low):
        if c < 2:
            return (a * 3 + b) * 16 + low * 8 + c * 3 + comp
        return 144 + (a * 2 + b // 2) * 16 + (b % 2) * 8 + low * 3 + comp

    index = [(p, a, b, c) for p in range(3) for a in range(3) for b in range(3) for c in range(3)]
    for i, first in enumerate(index):
        for j, second in enumerate(index):
            row = out_row(*first)
            out[row, in_row(*second, 0)] = hi[i, j]
            out[row, in_row(*second, 1)] = hi[i, j]
            out[row + 40, in_row(*second, 0)] = lo[i, j]
    return out.astype(BF16)


def diagonal_columns(stiff):
    out = np.zeros((4, 8, 128), np.float32)
    for pa in range(2):
        for pb in range(2):
            for c in range(2):
                for comp in range(3):
                    dof = comp * 27 + pa * 9 + pb * 3 + c
                    out[pa * 2 + pb, c * 3 + comp] = 1.0 / stiff[dof, dof]
    return out


def iota(shape, dim):
    return lax.broadcasted_iota(jnp.int32, shape, dim)


def parity_matrix(transposed):
    node = iota((256, 256), 1 if transposed else 0)
    place = iota((256, 256), 0 if transposed else 1)
    return (node == 2 * (place % 128) + place // 128).astype(F32).astype(BF16)


def exact_product(rows, matrix):
    first = rows.astype(BF16)
    left = rows - first.astype(F32)
    second = left.astype(BF16)
    third = (left - second.astype(F32)).astype(BF16)
    stacked = jnp.concatenate([first, second, third], axis=0)
    out = jnp.dot(stacked, matrix, preferred_element_type=F32)
    count = rows.shape[0]
    return out[:count] + out[count : 2 * count] + out[2 * count :]


def span(k, up, width):
    if k is None:
        return 0, OWN
    upward = up if k == 0 else 1 - up
    return upward * (OWN - width), width


def landing(k, up, width, margin):
    if k is None:
        return margin, OWN
    upward = up if k == 0 else 1 - up
    return upward * (OWN + margin) + (1 - upward) * (margin - width), width


def rows8(start):
    return pl.multiple_of(start * 8, 8) if not isinstance(start, int) else start * 8


def part_shape(part, width):
    return [OWN if k is None else width for k in part]


def take(ref, part, flags, width):
    sx, nx = span(part[0], flags[UP_X], width)
    sy, ny = span(part[1], flags[UP_Y], width)
    return ref[pl.ds(sx, nx), pl.ds(rows8(sy), ny * 8), :].reshape(nx * ny * 8, 128)


def place(ref, value, part, flags, width, passed=False):
    dx, nx = landing(part[0], flags[UP_X], OWN if passed else width, OWN)
    dy, ny = landing(part[1], flags[UP_Y], width, width)
    valid = present(part[0], flags, 0) * present(part[1], flags, 1)
    value = value * valid.astype(F32)
    ref[pl.ds(dx, nx), pl.ds(rows8(dy), ny * 8), :] = value.reshape(nx, ny * 8, 128)


def position():
    index = [lax.axis_index(axis) for axis in ("sx", "sy")]
    last = [lax.axis_size(axis) - 1 for axis in ("sx", "sy")]
    out = [1 - lax.rem(i, 2) for i in index]
    for i, end in zip(index, last):
        out += [jnp.minimum(i, 1), jnp.minimum(end - i, 1)]
    return out


def dense(cols):
    count = cols.shape[0] // 4
    c = cols.reshape(count, 4, 8, 128)
    row = iota((count, 8, 128), 1)
    tiles = [
        jnp.where(row < 6, c[:, 0], pltpu.roll(c[:, 1], 6, 1)),
        jnp.where(row < 4, pltpu.roll(c[:, 1], 6, 1), pltpu.roll(c[:, 2], 4, 1)),
        jnp.where(row < 2, pltpu.roll(c[:, 2], 4, 1), pltpu.roll(c[:, 3], 2, 1)),
    ]
    return jnp.stack(tiles, axis=1).reshape(count * 24, 128)


def sparse(rows):
    count = rows.shape[0] // 24
    t = rows.reshape(count, 3, 8, 128)
    row = iota((count, 8, 128), 1)
    cols = [
        t[:, 0],
        jnp.where(row < 2, pltpu.roll(t[:, 0], 2, 1), pltpu.roll(t[:, 1], 2, 1)),
        jnp.where(row < 4, pltpu.roll(t[:, 1], 4, 1), pltpu.roll(t[:, 2], 4, 1)),
        pltpu.roll(t[:, 2], 6, 1),
    ]
    return jnp.stack(cols, axis=1).reshape(count * 4, 8, 128)


def column_count(part, width):
    return math.prod(part_shape(part, width))


def present(k, flags, dim):
    if k is None:
        return 1
    up, low, high = flags[(UP_X, UP_Y)[dim]], flags[(LOW_X, LOW_Y)[dim]], flags[(HIGH_X, HIGH_Y)[dim]]
    upward = up if k == 0 else 1 - up
    return upward * high + (1 - upward) * low


def young_place(e):
    return e if e <= 2 else 7 if e == 3 else e + 4


def moduli_row(f_reg, e, f, row):
    start = 8 * (young_place(f) + HALO_F) + row
    return f_reg[young_place(e) + OWN, start : start + 1, :]


def split_store(z, x, s_ref, t_ref):
    count = z.shape[0]
    far = z * 65537.0
    hi = far - (far - z)
    lo = z - hi
    s_ref[x, : count * 16, :] = jnp.concatenate([hi, lo], axis=1).astype(BF16).reshape(count * 16, 128)
    row = iota(z.shape, 1)
    nxt = next_even(jnp.where(row < 3, hi, pltpu.roll(lo, 3, 1)))
    if count % 2:
        nxt = jnp.concatenate([nxt, nxt[count - 1 :]], axis=0)
        count += 1
    t_ref[x, : count * 8, :] = nxt.reshape(count // 2, 16, 128).astype(BF16).reshape(count * 8, 128)


def next_even(z):
    count = z.shape[0]
    moved = pltpu.roll(z.reshape(count * 8, 128), 127, 1)
    return jnp.where(iota(moved.shape, 1) < 127, moved, 0.0).reshape(count, 8, 128)


def element_operand(s_ref, t_ref, x, y, pair):
    pieces = [s_ref[x + a, pl.ds(y * 16, 48), :] for a in range(3)]
    pieces += [t_ref[x + a, pl.ds(pair * 16, 32), :] for a in range(3)]
    pieces.append(jnp.zeros((16, 128), BF16))
    return jnp.concatenate(pieces, axis=0)


def products(matrix, s_ref, t_ref, x, j):
    operand = jnp.concatenate(
        [element_operand(s_ref, t_ref, x, 2 * e, e) for e in (j, j + 1)], axis=1
    )
    out = jnp.dot(matrix, operand, preferred_element_type=F32)
    layers = [out[r : r + 40] + out[r + 40 : r + 80] for r in range(0, matrix.shape[0], 80)]
    return [[layer[:, :128] for layer in layers], [layer[:, 128:] for layer in layers]]


def apply(matrix_ref, s_ref, t_ref, young_ref, w_ref, o_ref, count_x, pairs_y, young_at, last=(0,)):
    for i in range(count_x):
        layers = (2,) if i == 0 else last if i == count_x - 1 else (0, 1, 2)
        matrix = matrix_ref[80 * layers[0] : 80 * (layers[-1] + 1), :]
        tails = [None] * 3
        for j in range(0, 2 * pairs_y, 2):
            both = products(matrix, s_ref, t_ref, 2 * i, j)
            for e in range(2):
                k = j + e
                scale = young_ref[i + young_at, k + young_at : k + young_at + 1, :]
                for a, out in zip(layers, both[e]):
                    out = out * scale
                    x = 2 * i + a
                    nodes, over = out[:16], out[24:32]
                    if tails[a] is not None:
                        nodes = jnp.concatenate([nodes[:8] + tails[a][0], nodes[8:]], axis=0)
                        over = over + tails[a][1]
                    if a == 0:
                        nodes = nodes + w_ref[x, 16 * k : 16 * k + 16, :]
                        over = over + o_ref[x, 8 * k : 8 * k + 8, :]
                    w_ref[x, 16 * k : 16 * k + 16, :] = nodes
                    o_ref[x, 8 * k : 8 * k + 8, :] = over
                    tails[a] = (out[16:24], out[32:40])
        k = 2 * pairs_y
        for a in layers:
            x = 2 * i + a
            nodes, over = tails[a]
            if a == 0:
                nodes = nodes + w_ref[x, 16 * k : 16 * k + 8, :]
                over = over + o_ref[x, 8 * k : 8 * k + 8, :]
            w_ref[x, 16 * k : 16 * k + 8, :] = nodes
            o_ref[x, 8 * k : 8 * k + 8, :] = over


def collect(w_ref, o_ref, x, low, count):
    half = (count + 1) // 2
    moved = pltpu.roll(o_ref[x, 4 * low : 4 * low + 8 * half, :], 1, 1)
    moved = jnp.where(iota(moved.shape, 1) > 0, moved, 0.0).reshape(half, 8, 128)
    row = iota(moved.shape, 1)
    even = jnp.where(row < 3, moved, 0.0)
    odd = jnp.where(row < 3, pltpu.roll(moved, 5, 1), 0.0)
    both = jnp.stack([even, odd], axis=1).reshape(2 * half, 8, 128)[:count]
    return w_ref[x, 8 * low : 8 * (low + count), :].reshape(count, 8, 128) + both


def load_columns(ref, x, low, count):
    return ref[x, 8 * low : 8 * (low + count), :].reshape(count, 8, 128)


def store_columns(ref, x, value):
    ref[x, : 8 * value.shape[0], :] = value.reshape(8 * value.shape[0], 128)


def prepare_kernel(fields, design, u_ref, f_ref, *sends):
    flags = position()
    matrix = parity_matrix(False)
    solid = design[1] == 1.0
    rho = jnp.where(solid, 1.0, design[0])
    young = EMIN + (1.0 - EMIN) * (rho * rho * rho)
    factor = jnp.where(solid, 0.0, -3.0 * (1.0 - EMIN) * (rho * rho))
    for x in range(OWN):
        free = 1.0 - fields[7, x]
        loaded = free * fields[6, x]
        rows = [free * fields[c, x] for c in range(3)] + [loaded * fields[c, x] for c in range(3, 6)] + [free]
        split = exact_product(jnp.concatenate(rows, axis=0), matrix)
        for index in range(7):
            ref, row = ((u_ref, index), (f_ref, index - 3), (u_ref, 6))[index // 3]
            step = 1 if index == 6 else 3
            for parity in range(2):
                ref[x, pl.ds(row + parity * step, 8, stride=8), :] = split[
                    8 * index : 8 * index + 8, 128 * parity : 128 * parity + 128
                ]
        element = {0: 0, 1: 1, 2: 2, 5: 1, 6: 2, 7: 3}.get(x)
        for row, values in ((6, young), (7, factor)):
            if element is None:
                column = jnp.zeros((8, 128), F32)
            else:
                column = jnp.concatenate(
                    [values[element, :3], jnp.zeros((2, 128), F32), values[element, 1:]], axis=0
                )
            f_ref[x, pl.ds(row, 8, stride=8), :] = column
    for part, send in zip(PARTS, sends):
        first = take(u_ref, part, flags, HALO_U)
        send[: first.shape[0], :] = first
        send[first.shape[0] :, :] = take(f_ref, part, flags, HALO_F)


def first_kernel(matrix, diag, u_own, f_own, *rest):
    flags = position()
    received, rest = rest[:8], rest[8:]
    (z0_ref, u_ref, dinv, young, factor, w0_ref, w1_ref, z1_ref), rest = rest[:8], rest[8:]
    sends, (u_reg, f_reg, s_ref, t_ref, w_ref, o_ref) = rest[:6], rest[6:]
    u_reg[OWN : 2 * OWN, 8 * HALO_U : 8 * (HALO_U + OWN), :] = u_own[...]
    f_reg[OWN : 2 * OWN, 8 * HALO_F : 8 * (HALO_F + OWN), :] = f_own[...]
    for index, value in enumerate(received):
        passed = index >= 6
        part = (0, index - 6) if passed else PARTS[index]
        end = column_count(PARTS[index - 6] if passed else part, HALO_U) * 8
        place(u_reg, value[:end, :], part, flags, HALO_U, passed)
        place(f_reg, value[end:, :], part, flags, HALO_F, passed)
    zero = jnp.zeros((1, 128), F32)
    for e in range(-3, 7):
        rows = [moduli_row(f_reg, e, f, 6) for f in range(-3, 7)]
        young[e + 3] = jnp.concatenate(rows + [zero] * 6, axis=0)
    for e in range(-1, 5):
        rows = [moduli_row(f_reg, e, f, 7) for f in range(-1, 5)]
        factor[e + 1] = jnp.concatenate(rows + [zero] * 2, axis=0)

    def inverse(x):
        e = x // 2
        near = young[e] + young[e + 1] if x % 2 == 0 else young[e + 1]
        both = near + pltpu.roll(near, 1, 0)
        lines = {}
        for pb, total in ((0, both), (1, near)):
            before = jnp.where(iota(total.shape, 1) > 0, pltpu.roll(total, 1, 1), 0.0)
            for pc, value in ((0, total + before), (1, total)):
                lines[pb, pc] = jnp.where(value > 0.0, 1.0 / value, 0.0)
        row = iota((8, 128), 0)
        cols = []
        for y in range(17):
            pb, f = y % 2, y // 2 + 1
            even, odd = [
                lines[pb, pc][f : f + 1] * u_reg[x + 4, 8 * (y + 1) + 6 + pc : 8 * (y + 1) + 7 + pc, :]
                for pc in range(2)
            ]
            line = jnp.where(row < 3, jnp.broadcast_to(even, (8, 128)), jnp.broadcast_to(odd, (8, 128)))
            cols.append(line * diag[(x % 2) * 2 + pb])
        dinv[x] = jnp.concatenate(cols, axis=0)

    for x in range(17):
        inverse(x)

    def operand(x):
        split_store(load_columns(u_reg, x + 4, 1, 17), x, s_ref, t_ref)

    for x in range(17):
        operand(x)
    apply(matrix, s_ref, t_ref, young, w_ref, o_ref, 8, 4, 1)

    def residual(x):
        image = collect(w_ref, o_ref, x + 2, 2, 13)
        inv = load_columns(dinv, x + 2, 2, 13)
        res = load_columns(f_reg, x + 6, 1, 13) - image
        z0 = inv * res
        store_columns(z0_ref, x, z0)
        store_columns(u_ref, x, load_columns(u_reg, x + 6, 3, 13))

        if 2 <= x < 10:
            store_columns(w0_ref, x - 2, jnp.where(inv > 0.0, res, 0.0)[2:10])

    for x in range(13):
        residual(x)

    def operand_0(x):
        split_store(load_columns(z0_ref, x, 0, 13), x, s_ref, t_ref)

    for x in range(13):
        operand_0(x)
    apply(matrix, s_ref, t_ref, young, w_ref, o_ref, 5, 3, 2, last=(0, 1))

    def image_1(x):
        image = collect(w_ref, o_ref, x + 2, 2, 8)
        inv = load_columns(dinv, x + 4, 4, 8)
        image = SHIFTS[0] * jnp.where(inv > 0.0, image, 0.0)
        store_columns(w1_ref, x, load_columns(w0_ref, x, 0, 8) - image)
        store_columns(z1_ref, x, load_columns(z0_ref, x + 2, 2, 8) - inv * image)

    for x in range(OWN):
        image_1(x)
    for part, send in zip(PARTS, sends):
        cols = take(z1_ref, part, flags, HALO_Z)
        extra = send.shape[0] * 8 // 6 - cols.shape[0]
        if extra:
            cols = jnp.concatenate([cols, jnp.zeros((extra, 128), F32)], axis=0)
        send[...] = dense(cols.reshape(-1, 8, 128))


def second_kernel(matrix, z1_own, dinv, young, w0_ref, w1_ref, z0_ref, u_ref, f_own, *rest):
    received, rest = rest[:8], rest[8:]
    (z1_ref, z2_ref, z3_ref, sums_ref), rest = rest[:4], rest[4:]
    z_reg, s_ref, t_ref, w_ref, o_ref, w2_ref, w3_ref = rest
    flags = position()
    z_reg[OWN : 2 * OWN, 8 * HALO_Z : 8 * (HALO_Z + OWN), :] = z1_own[...]
    for index, value in enumerate(received):
        passed = index >= 6
        part = (0, index - 6) if passed else PARTS[index]
        count = column_count(PARTS[index - 6] if passed else part, HALO_Z)
        place(z_reg, sparse(value[...])[:count], part, flags, HALO_Z, passed)

    def operand_1(x):
        split_store(load_columns(z_reg, x + 2, 1, 21), x, s_ref, t_ref)

    for x in range(21):
        operand_1(x)

    def keep(x):
        store_columns(z1_ref, x, load_columns(z_reg, x + 6, 5, 13))

    for x in range(13):
        keep(x)
    apply(matrix, s_ref, t_ref, young, w_ref, o_ref, 10, 5, 0)

    def image_2(x):
        image = collect(w_ref, o_ref, x + 2, 2, 17)
        inv = load_columns(dinv, x, 0, 17)
        image = SHIFTS[1] * jnp.where(inv > 0.0, image, 0.0)
        z2 = load_columns(z_reg, x + 4, 3, 17) - inv * image
        split_store(z2, x, s_ref, t_ref)

        if 2 <= x < 15:
            store_columns(z2_ref, x - 2, z2[2:15])

        if 4 <= x < 12:
            store_columns(w2_ref, x - 4, load_columns(w1_ref, x - 4, 0, 8) - image[4:12])

    for x in range(17):
        image_2(x)
    apply(matrix, s_ref, t_ref, young, w_ref, o_ref, 8, 4, 1)

    def image_3(x):
        image = collect(w_ref, o_ref, x + 2, 2, 13)
        inv = load_columns(dinv, x + 2, 2, 13)
        image = SHIFTS[2] * jnp.where(inv > 0.0, image, 0.0)
        z3 = load_columns(z2_ref, x, 0, 13) - inv * image
        split_store(z3, x, s_ref, t_ref)
        store_columns(z3_ref, x, z3)

        if 2 <= x < 10:
            store_columns(w3_ref, x - 2, load_columns(w2_ref, x - 2, 0, 8) - image[2:10])

    for x in range(13):
        image_3(x)
    apply(matrix, s_ref, t_ref, young, w_ref, o_ref, 5, 3, 2, last=(0, 1))
    sums = [jnp.zeros((8, 128), F32) for _ in dot_list()]

    def dots(x):
        inv = load_columns(dinv, x + 4, 4, 8)
        w = [load_columns(ref, x, 0, 8) for ref in (w0_ref, w1_ref, w2_ref, w3_ref)]
        w.append(w[3] - SHIFTS[3] * jnp.where(inv > 0.0, collect(w_ref, o_ref, x + 2, 2, 8), 0.0))
        z = [inv * value for value in w[:4]]
        load = jnp.where(inv > 0.0, load_columns(f_own, x, 0, 8), 0.0)
        u = load_columns(u_ref, x + 2, 2, 8)
        for index, (first, second) in enumerate(dot_list()):
            first = u if first is None else (w if first[0] == "w" else z)[first[1]]
            second = load if second is None else w[second[1]]
            sums[index] += jnp.sum(first * second, axis=0)

    for x in range(OWN):
        dots(x)
    shape = (48, 128)
    lines = [jnp.sum(value, axis=0, keepdims=True) for value in sums]
    lines = jnp.concatenate(lines + [jnp.zeros((shape[0] - len(lines), 128), F32)], axis=0)
    totals = jnp.sum(lines, axis=1, keepdims=True)
    line = jnp.sum(
        jnp.where(iota(shape, 0) == iota(shape, 1), jnp.broadcast_to(totals, shape), 0.0),
        axis=0,
        keepdims=True,
    )
    sums_ref[...] = jnp.broadcast_to(line, sums_ref.shape)


def dot_list():
    out = [(("w", i), ("w", j)) for i in range(5) for j in range(i, 5)]
    out += [(None, None)] + [(("z", i), None) for i in range(4)]
    out += [(None, ("w", j)) for j in range(5)]
    out += [(("z", i), ("w", j)) for i in range(4) for j in range(i, 5)]
    return out


def step_sizes(total):
    place_of = {pair: index for index, pair in enumerate(dot_list())}

    def gram(i, j):
        return total(place_of[("w", min(i, j)), ("w", max(i, j))])

    poly = [jnp.ones((1, 128), F32)]
    coef = [jnp.zeros((1, 128), F32)] * SWEEPS
    for sweep in range(SWEEPS):
        scaled = [poly[i] / SHIFTS[i] for i in range(sweep + 1)]
        image = [scaled[0]] + [scaled[i] - scaled[i - 1] for i in range(1, sweep + 1)] + [-scaled[sweep]]
        times = [sum(gram(i, j) * image[j] for j in range(sweep + 2)) for i in range(sweep + 2)]
        top = sum(poly[i] * times[i] for i in range(sweep + 1))
        bottom = sum(image[i] * times[i] for i in range(sweep + 2))
        omega = top / bottom
        for i in range(sweep + 1):
            coef[i] = coef[i] + omega * poly[i]
        poly = [
            (poly[i] if i <= sweep else 0.0) - omega * image[i] for i in range(sweep + 2)
        ]
    work = total(place_of[None, None])
    for i in range(SWEEPS):
        work = work + coef[i] * total(place_of[("z", i), None])
    for j in range(SWEEPS + 1):
        part = total(place_of[None, ("w", j)])
        for i in range(SWEEPS):
            part = part + coef[i] * total(place_of[("z", min(i, j)), ("w", max(i, j))])
        work = work - poly[j] * part
    return coef, work


def last_kernel(matrix, sums, u_ref, z0_ref, z1_ref, z2_ref, z3_ref, factor, *rest):
    (out_u, out_f, out_c), (own, s_ref, t_ref, uf_ref, tf_ref, sens_ref) = rest[:3], rest[3:]
    flags = position()
    line = jnp.sum(sums[...], axis=0, keepdims=True)
    shape = (48, 128)
    spread = jnp.where(iota(shape, 0) == iota(shape, 1), jnp.broadcast_to(line, shape), 0.0)
    spread = jnp.broadcast_to(jnp.sum(spread, axis=1, keepdims=True), shape)
    coef, work = step_sizes(lambda index: spread[index : index + 1])
    out_c[...] = work

    def combine(x):
        value = load_columns(u_ref, x, 0, 13)
        for index, ref in enumerate((z0_ref, z1_ref, z2_ref, z3_ref)):
            value = value + coef[index] * load_columns(ref, x, 0, 13)
        store_columns(uf_ref, x, value)
        split_store(value, x, s_ref, t_ref)
        row = iota((7, 8, 128), 1)
        even = jnp.concatenate([value[y : y + 1] for y in range(0, 13, 2)], axis=0)
        odd = jnp.concatenate([value[min(y, 12) : min(y, 12) + 1] for y in range(1, 14, 2)], axis=0)
        nxt = next_even(jnp.where(row < 3, even, pltpu.roll(odd, 3, 1)))
        store_columns(tf_ref, x, nxt)

        if 2 <= x < 10:
            store_columns(own, x - 2, value[2:10])

    for x in range(13):
        combine(x)

    for i in range(6):
        for j in range(0, 6, 2):
            both = products(matrix[...], s_ref, t_ref, 2 * i, j)
            for e in range(2):
                k = j + e
                acc = jnp.zeros((8, 128), F32)
                for a in range(3):
                    left = uf_ref[2 * i + a, 16 * k : 16 * k + 24, :] * both[e][a][:24]
                    right = tf_ref[2 * i + a, 8 * k : 8 * k + 16, :] * both[e][a][24:]
                    acc = acc + left[:8] + left[8:16] + left[16:] + right[:8] + right[8:]
                sens_ref[i, k : k + 1, :] = jnp.sum(acc, axis=0, keepdims=True)
        sens_ref[i, 6:8, :] = jnp.zeros((2, 128), F32)
    edge = RADIUS - 1.0
    corner = RADIUS - math.sqrt(2.0)
    row = iota((8, 128), 0)
    lane = iota((8, 128), 1)
    sens = [sens_ref[x] * factor[x] for x in range(6)]
    low, high = flags[LOW_Y].astype(F32), flags[HIGH_Y].astype(F32)
    inside = jnp.where(row == 0, low, jnp.where(row < 5, 1.0, jnp.where(row == 5, high, 0.0)))
    inside_x = [flags[LOW_X].astype(F32)] + [1.0] * 4 + [flags[HIGH_X].astype(F32)]
    covered = [inside * value for value in inside_x]

    def along_y(v):
        return pltpu.roll(v, 1, 0) + pltpu.roll(v, 7, 0)

    def along_z(v):
        return jnp.where(lane > 0, pltpu.roll(v, 1, 1), 0.0) + jnp.where(lane < 127, pltpu.roll(v, 127, 1), 0.0)

    def gathered(layers, x):
        here, sides = layers[x], layers[x - 1] + layers[x + 1]
        ys = along_y(here)
        return (
            RADIUS * here
            + edge * (ys + along_z(here) + sides)
            + corner * (along_z(ys) + along_y(sides) + along_z(sides))
        )

    for x in range(ELEMS):
        out_f[x] = (gathered(sens, x + 1) / gathered(covered, x + 1))[1:5]
    merge = parity_matrix(True)
    for x in range(OWN):
        rows = [
            jnp.concatenate(
                [own[x, pl.ds(comp + 3 * parity, 8, stride=8), :] for parity in range(2)], axis=1
            )
            for comp in range(3)
        ]
        joined = exact_product(jnp.concatenate(rows, axis=0), merge)
        for comp in range(3):
            out_u[comp, x] = joined[8 * comp : 8 * comp + 8]


def partners(part, count_x, count_y):
    def other(i, k, count):
        if k is None:
            return i
        if k == 0:
            return i ^ 1
        return ((i + 1) ^ 1) - 1 if 0 < i < count - 1 else None

    out = []
    for x in range(count_x):
        for y in range(count_y):
            px, py = other(x, part[0], count_x), other(y, part[1], count_y)
            if px is None and py is None:
                px, py = count_x - 1 - x, y
            elif px is None:
                px, py = x, (y ^ 1 if part[1] is None else py)
            elif py is None:
                px, py = (x ^ 1 if part[0] is None else px), y
            out.append((x * count_y + y, px * count_y + py))
    return out


def shapes(*items):
    return [jax.ShapeDtypeStruct(item, F32) for item in items]


def call(kernel, out_shape, scratch, operands):
    spec = pl.BlockSpec(memory_space=pltpu.VMEM)
    return pl.pallas_call(
        kernel,
        out_shape=out_shape,
        in_specs=[spec] * len(operands),
        out_specs=[spec] * len(out_shape),
        scratch_shapes=scratch,
        compiler_params=pltpu.CompilerParams(vmem_limit_bytes=24 * 1024 * 1024),
    )(*operands)


def body(force, load_mask, support_mask, start_field, density, passive_mask):
    count_x, count_y = lax.axis_size("sx"), lax.axis_size("sy")
    devices = count_x * count_y
    stiff = element_matrix()
    matrix = jnp.asarray(operator_matrix(stiff))
    diag = jnp.asarray(diagonal_columns(stiff))
    zero = F32(0.0)
    none = (0, 0, 0)
    fields = (
        lax.pad(start_field, zero, ((0, 5, 0), none, none, none))
        + lax.pad(force, zero, ((3, 2, 0), none, none, none))
        + (
            lax.pad(load_mask[None], 0, ((6, 1, 0), none, none, none))
            + lax.pad(support_mask[None], 0, ((7, 0, 0), none, none, none))
        ).astype(F32)
    )
    design = lax.pad(density[None], zero, ((0, 1, 0), none, none, none)) + lax.pad(
        passive_mask[None], 0, ((1, 0, 0), none, none, none)
    ).astype(F32)

    def send(value, part):
        return lax.ppermute(value, ("sx", "sy"), partners(part, count_x, count_y))

    def swap(values):
        first, second, *corners, x_side = [send(value, part) for part, value in zip(PARTS[:5], values)]
        x_side, mate = lax.optimization_barrier((x_side, values[5]))
        *corners, second = lax.optimization_barrier((*corners, second))
        passed = [send(value, MATE) for value in (mate, first, second)]
        return [first, second, *corners, x_side, *passed]

    def sizes(width):
        return [column_count(part, width) for part in PARTS]

    own = (OWN, OWN * 8, 128)
    middle = (13, 13 * 8, 128)
    first = call(
        prepare_kernel,
        [
            *shapes(own, own),
            *shapes(*((8 * (a + b), 128) for a, b in zip(sizes(HALO_U), sizes(HALO_F)))),
        ],
        [],
        [fields, design],
    )
    u_own, f_own = first[:2]
    second = call(
        first_kernel,
        shapes(
            middle,
            middle,
            (17, 17 * 8, 128),
            (10, 16, 128),
            (6, 8, 128),
            own,
            own,
            own,
            *(((a + 3) // 4 * 24, 128) for a in sizes(HALO_Z)),
        ),
        [
            pltpu.VMEM((24, 18 * 8, 128), F32),
            pltpu.VMEM((24, 14 * 8, 128), F32),
            pltpu.VMEM((17, 17 * 16, 128), BF16),
            pltpu.VMEM((17, 9 * 16, 128), BF16),
            pltpu.VMEM((17, 17 * 8, 128), F32),
            pltpu.VMEM((17, 9 * 8, 128), F32),
        ],
        [matrix, diag, u_own, f_own, *swap(first[2:])],
    )
    z0, u0, dinv, young, factor, w0, w1, z1 = second[:8]
    z1, z2, z3, sums = call(
        second_kernel,
        shapes(middle, middle, middle, (devices, 128)),
        [
            pltpu.VMEM((24, 22 * 8, 128), F32),
            pltpu.VMEM((21, 21 * 16, 128), BF16),
            pltpu.VMEM((21, 11 * 16, 128), BF16),
            pltpu.VMEM((21, 21 * 8, 128), F32),
            pltpu.VMEM((21, 11 * 8, 128), F32),
            pltpu.VMEM(own, F32),
            pltpu.VMEM(own, F32),
        ],
        [matrix, z1, dinv, young, w0, w1, z0, u0, f_own, *swap(second[8:])],
    )
    sums = lax.all_to_all(sums, ("sx", "sy"), 0, 0, tiled=True)
    displacement, filtered, compliance = call(
        last_kernel,
        shapes(start_field.shape, density.shape, (1, 128)),
        [
            pltpu.VMEM(own, F32),
            pltpu.VMEM((13, 13 * 16, 128), BF16),
            pltpu.VMEM((13, 7 * 16, 128), BF16),
            pltpu.VMEM(middle, F32),
            pltpu.VMEM((13, 7 * 8, 128), F32),
            pltpu.VMEM((6, 8, 128), F32),
        ],
        [matrix, sums, u0, z0, z1, z2, z3, factor],
    )
    return displacement, filtered, compliance[0, 0]


def solution(mesh):
    in_specs = (
        P(None, "sx", "sy", None),
        P("sx", "sy", None),
        P("sx", "sy", None),
        P(None, "sx", "sy", None),
        P("sx", "sy", None),
        P("sx", "sy", None),
    )
    out_specs = (P(None, "sx", "sy", None), P("sx", "sy", None), P())
    return jax.shard_map(body, mesh=mesh, in_specs=in_specs, out_specs=out_specs, check_vma=False)
```

```python
import functools
import math

import jax
import jax.numpy as jnp
import numpy as np
from jax import lax
from jax.experimental import pallas as pl
from jax.experimental.pallas import tpu as pltpu
from jax.sharding import PartitionSpec as P

SWEEPS = 4
EMIN = 0.001
RADIUS = 1.5

OWN = 8
ELEMS = OWN // 2
HALO_U = 5
HALO_F = 3
HALO_Z = 7
PARTS = [
    (None, 0),
    (None, 1),
    (1, 0),
    (1, 1),
    (1, None),
    (0, None),
]
MATE = (0, None)
UP_X, UP_Y, LOW_X, HIGH_X, LOW_Y, HIGH_Y = range(6)
SHIFTS = (0.59, 0.73, 0.645, 0.69)
F32 = jnp.float32
BF16 = jnp.bfloat16


def element_matrix():
    poisson = 0.3
    lame_first = poisson / ((1.0 + poisson) * (1.0 - 2.0 * poisson))
    shear = 1.0 / (2.0 * (1.0 + poisson))
    elastic = np.zeros((6, 6))
    elastic[:3, :3] = lame_first
    for entry in range(3):
        elastic[entry, entry] += 2.0 * shear
        elastic[entry + 3, entry + 3] = shear
    points = [-math.sqrt(0.6), 0.0, math.sqrt(0.6)]
    weights = [5.0 / 9.0, 8.0 / 9.0, 5.0 / 9.0]

    def values(point):
        return np.array(
            [point * (point - 1.0) / 2.0, 1.0 - point * point, point * (point + 1.0) / 2.0]
        )

    def slopes(point):
        return np.array([point - 0.5, -2.0 * point, point + 0.5])

    stiff = np.zeros((81, 81))
    for first in range(3):
        for second in range(3):
            for third in range(3):
                val_x, val_y, val_z = (
                    values(points[first]),
                    values(points[second]),
                    values(points[third]),
                )
                der_x, der_y, der_z = (
                    slopes(points[first]),
                    slopes(points[second]),
                    slopes(points[third]),
                )
                strain = np.zeros((6, 81))
                for node_a in range(3):
                    for node_b in range(3):
                        for node_c in range(3):
                            node = node_a * 9 + node_b * 3 + node_c
                            grad_x = 2.0 * der_x[node_a] * val_y[node_b] * val_z[node_c]
                            grad_y = 2.0 * val_x[node_a] * der_y[node_b] * val_z[node_c]
                            grad_z = 2.0 * val_x[node_a] * val_y[node_b] * der_z[node_c]
                            strain[0, node] = grad_x
                            strain[1, 27 + node] = grad_y
                            strain[2, 54 + node] = grad_z
                            strain[3, node] = grad_y
                            strain[3, 27 + node] = grad_x
                            strain[4, 27 + node] = grad_z
                            strain[4, 54 + node] = grad_y
                            strain[5, node] = grad_z
                            strain[5, 54 + node] = grad_x
                factor = weights[first] * weights[second] * weights[third] * 0.125
                stiff = stiff + factor * strain.T @ elastic @ strain
    return stiff.astype(np.float32)


def operator_matrix(stiff):
    hi = stiff.astype(BF16).astype(np.float32)
    lo = stiff - hi
    out = np.zeros((240, 256), np.float32)

    def out_row(comp, a, b, c):
        if c < 2:
            return 80 * a + b * 8 + c * 3 + comp
        return 80 * a + 24 + (b // 2) * 8 + (b % 2) * 4 + comp

    def in_row(comp, a, b, c, low):
        if c < 2:
            return (a * 3 + b) * 16 + low * 8 + c * 3 + comp
        return 144 + (a * 2 + b // 2) * 16 + low * 8 + (b % 2) * 4 + comp

    index = [(p, a, b, c) for p in range(3) for a in range(3) for b in range(3) for c in range(3)]
    for i, first in enumerate(index):
        for j, second in enumerate(index):
            row = out_row(*first)
            out[row, in_row(*second, 0)] = hi[i, j]
            out[row, in_row(*second, 1)] = hi[i, j]
            out[row + 40, in_row(*second, 0)] = lo[i, j]
    return out.astype(BF16)


def diagonal_columns(stiff):
    out = np.zeros((4, 8, 128), np.float32)
    for pa in range(2):
        for pb in range(2):
            for c in range(2):
                for comp in range(3):
                    dof = comp * 27 + pa * 9 + pb * 3 + c
                    out[pa * 2 + pb, c * 3 + comp] = 1.0 / stiff[dof, dof]
    return out


def iota(shape, dim):
    return lax.broadcasted_iota(jnp.int32, shape, dim)


def parity_matrix(transposed):
    node = iota((256, 256), 1 if transposed else 0)
    place = iota((256, 256), 0 if transposed else 1)
    return (node == 2 * (place % 128) + place // 128).astype(F32).astype(BF16)


def exact_product(rows, matrix):
    first = rows.astype(BF16)
    left = rows - first.astype(F32)
    second = left.astype(BF16)
    third = (left - second.astype(F32)).astype(BF16)
    stacked = jnp.concatenate([first, second, third], axis=0)
    out = jnp.dot(stacked, matrix, preferred_element_type=F32)
    count = rows.shape[0]
    return out[:count] + out[count : 2 * count] + out[2 * count :]


def span(k, up, width):
    if k is None:
        return 0, OWN
    upward = up if k == 0 else 1 - up
    return upward * (OWN - width), width


def landing(k, up, width, margin):
    if k is None:
        return margin, OWN
    upward = up if k == 0 else 1 - up
    return upward * (OWN + margin) + (1 - upward) * (margin - width), width


def rows8(start):
    return pl.multiple_of(start * 8, 8) if not isinstance(start, int) else start * 8


def part_shape(part, width):
    return [OWN if k is None else width for k in part]


def take(ref, part, flags, width):
    sx, nx = span(part[0], flags[UP_X], width)
    sy, ny = span(part[1], flags[UP_Y], width)
    return ref[pl.ds(sx, nx), pl.ds(rows8(sy), ny * 8), :].reshape(nx * ny * 8, 128)


def place(ref, value, part, flags, width, passed=False):
    dx, nx = landing(part[0], flags[UP_X], OWN if passed else width, OWN)
    dy, ny = landing(part[1], flags[UP_Y], width, width)
    valid = present(part[0], flags, 0) * present(part[1], flags, 1)
    value = value * valid.astype(F32)
    ref[pl.ds(dx, nx), pl.ds(rows8(dy), ny * 8), :] = value.reshape(nx, ny * 8, 128)


def position():
    index = [lax.axis_index(axis) for axis in ("sx", "sy")]
    last = [lax.axis_size(axis) - 1 for axis in ("sx", "sy")]
    out = [1 - lax.rem(i, 2) for i in index]
    for i, end in zip(index, last):
        out += [jnp.minimum(i, 1), jnp.minimum(end - i, 1)]
    return out


def dense(cols):
    count = cols.shape[0] // 4
    c = cols.reshape(count, 4, 8, 128)
    row = iota((count, 8, 128), 1)
    tiles = [
        jnp.where(row < 6, c[:, 0], pltpu.roll(c[:, 1], 6, 1)),
        jnp.where(row < 4, pltpu.roll(c[:, 1], 6, 1), pltpu.roll(c[:, 2], 4, 1)),
        jnp.where(row < 2, pltpu.roll(c[:, 2], 4, 1), pltpu.roll(c[:, 3], 2, 1)),
    ]
    return jnp.stack(tiles, axis=1).reshape(count * 24, 128)


def sparse(rows):
    count = rows.shape[0] // 24
    t = rows.reshape(count, 3, 8, 128)
    row = iota((count, 8, 128), 1)
    cols = [
        t[:, 0],
        jnp.where(row < 2, pltpu.roll(t[:, 0], 2, 1), pltpu.roll(t[:, 1], 2, 1)),
        jnp.where(row < 4, pltpu.roll(t[:, 1], 4, 1), pltpu.roll(t[:, 2], 4, 1)),
        pltpu.roll(t[:, 2], 6, 1),
    ]
    return jnp.stack(cols, axis=1).reshape(count * 4, 8, 128)


def column_count(part, width):
    return math.prod(part_shape(part, width))


def present(k, flags, dim):
    if k is None:
        return 1
    up, low, high = flags[(UP_X, UP_Y)[dim]], flags[(LOW_X, LOW_Y)[dim]], flags[(HIGH_X, HIGH_Y)[dim]]
    upward = up if k == 0 else 1 - up
    return upward * high + (1 - upward) * low


def young_place(e):
    return e if e <= 2 else 7 if e == 3 else e + 4


def moduli_row(f_reg, e, f, row):
    start = 8 * (young_place(f) + HALO_F) + row
    return f_reg[young_place(e) + OWN, start : start + 1, :]


def parts_of(z):
    far = z * 65537.0
    hi = far - (far - z)
    return jnp.concatenate([hi, z - hi], axis=1).astype(BF16).reshape(z.shape[0] * 16, 128)


def split_store(z, x, s_ref, t_ref):
    count = z.shape[0]
    s_ref[x, : count * 16, :] = parts_of(z)
    if count % 2:
        z = jnp.concatenate([z, z[count - 1 :]], axis=0)
        count += 1
    z = z.reshape(count // 2, 2, 8, 128)
    nxt = jnp.where(iota((count // 2, 8, 128), 1) < 4, z[:, 0], pltpu.roll(z[:, 1], 4, 1))
    nxt = pltpu.roll(nxt.reshape(count * 4, 128), 127, 1)
    nxt = jnp.where(iota(nxt.shape, 1) < 127, nxt, 0.0).reshape(count // 2, 8, 128)
    t_ref[x, : count * 8, :] = parts_of(nxt)
    return nxt


def element_operand(s_ref, t_ref, x, y, pair):
    pieces = [s_ref[x + a, pl.ds(y * 16, 48), :] for a in range(3)]
    pieces += [t_ref[x + a, pl.ds(pair * 16, 32), :] for a in range(3)]
    pieces.append(jnp.zeros((16, 128), BF16))
    return jnp.concatenate(pieces, axis=0)


def products(matrix, s_ref, t_ref, x, j):
    operand = jnp.concatenate(
        [element_operand(s_ref, t_ref, x, 2 * e, e) for e in (j, j + 1)], axis=1
    )
    out = jnp.dot(matrix, operand, preferred_element_type=F32)
    layers = [out[r : r + 40] + out[r + 40 : r + 80] for r in range(0, matrix.shape[0], 80)]
    return [[layer[:, :128] for layer in layers], [layer[:, 128:] for layer in layers]]


def apply(matrix_ref, s_ref, t_ref, young_ref, w_ref, o_ref, count_x, pairs_y, young_at, last=(0,)):
    for i in range(count_x):
        layers = (2,) if i == 0 else last if i == count_x - 1 else (0, 1, 2)
        matrix = matrix_ref[80 * layers[0] : 80 * (layers[-1] + 1), :]
        tails = [None] * 3
        for j in range(0, 2 * pairs_y, 2):
            both = products(matrix, s_ref, t_ref, 2 * i, j)
            for e in range(2):
                k = j + e
                scale = young_ref[i + young_at, k + young_at : k + young_at + 1, :]
                for a, out in zip(layers, both[e]):
                    out = out * scale
                    x = 2 * i + a
                    nodes, over = out[:16], out[24:32]
                    if tails[a] is not None:
                        nodes = jnp.concatenate([nodes[:8] + tails[a][0], nodes[8:]], axis=0)
                        over = over + tails[a][1]
                    if a == 0:
                        nodes = nodes + w_ref[x, 16 * k : 16 * k + 16, :]
                        over = over + o_ref[x, 8 * k : 8 * k + 8, :]
                    w_ref[x, 16 * k : 16 * k + 16, :] = nodes
                    o_ref[x, 8 * k : 8 * k + 8, :] = over
                    tails[a] = (out[16:24], out[32:40])
        k = 2 * pairs_y
        for a in layers:
            x = 2 * i + a
            nodes, over = tails[a]
            if a == 0:
                nodes = nodes + w_ref[x, 16 * k : 16 * k + 8, :]
                over = over + o_ref[x, 8 * k : 8 * k + 8, :]
            w_ref[x, 16 * k : 16 * k + 8, :] = nodes
            o_ref[x, 8 * k : 8 * k + 8, :] = over


def collect(w_ref, o_ref, x, low, count):
    half = (count + 1) // 2
    moved = pltpu.roll(o_ref[x, 4 * low : 4 * low + 8 * half, :], 1, 1)
    moved = jnp.where(iota(moved.shape, 1) > 0, moved, 0.0).reshape(half, 8, 128)
    row = iota(moved.shape, 1)
    even = jnp.where(row < 3, moved, 0.0)
    odd = jnp.where(row < 3, pltpu.roll(moved, 4, 1), 0.0)
    both = jnp.stack([even, odd], axis=1).reshape(2 * half, 8, 128)[:count]
    return w_ref[x, 8 * low : 8 * (low + count), :].reshape(count, 8, 128) + both


def load_columns(ref, x, low, count):
    return ref[x, 8 * low : 8 * (low + count), :].reshape(count, 8, 128)


def store_columns(ref, x, value):
    ref[x, : 8 * value.shape[0], :] = value.reshape(8 * value.shape[0], 128)


def prepare_kernel(fields, u_ref, f_ref, *sends):
    flags = position()
    matrix = parity_matrix(False)
    solid = fields[9, :ELEMS, :ELEMS, :128] == 1.0
    rho = jnp.where(solid, 1.0, fields[8, :ELEMS, :ELEMS, :128])
    young = EMIN + (1.0 - EMIN) * (rho * rho * rho)
    factor = jnp.where(solid, 0.0, -3.0 * (1.0 - EMIN) * (rho * rho))
    for x in range(OWN):
        free = 1.0 - fields[7, x]
        loaded = free * fields[6, x]
        rows = [free * fields[c, x] for c in range(3)] + [loaded * fields[c, x] for c in range(3, 6)] + [free]
        split = exact_product(jnp.concatenate(rows, axis=0), matrix)
        for index in range(7):
            ref, row = ((u_ref, index), (f_ref, index - 3), (u_ref, 6))[index // 3]
            step = 1 if index == 6 else 3
            for parity in range(2):
                ref[x, pl.ds(row + parity * step, 8, stride=8), :] = split[
                    8 * index : 8 * index + 8, 128 * parity : 128 * parity + 128
                ]
        element = {0: 0, 1: 1, 2: 2, 5: 1, 6: 2, 7: 3}.get(x)
        for row, values in ((6, young), (7, factor)):
            if element is None:
                column = jnp.zeros((8, 128), F32)
            else:
                column = jnp.concatenate(
                    [values[element, :3], jnp.zeros((2, 128), F32), values[element, 1:]], axis=0
                )
            f_ref[x, pl.ds(row, 8, stride=8), :] = column
    for part, send in zip(PARTS, sends):
        first = take(u_ref, part, flags, HALO_U)
        send[: first.shape[0], :] = first
        send[first.shape[0] :, :] = take(f_ref, part, flags, HALO_F)


def first_kernel(matrix, diag, u_own, f_own, *rest):
    flags = position()
    received, rest = rest[:8], rest[8:]
    (z0_ref, u_ref, dinv, young, factor, w0_ref, w1_ref, z1_ref), rest = rest[:8], rest[8:]
    sends, (u_reg, f_reg, s_ref, t_ref, w_ref, o_ref) = rest[:6], rest[6:]
    u_reg[OWN : 2 * OWN, 8 * HALO_U : 8 * (HALO_U + OWN), :] = u_own[...]
    f_reg[OWN : 2 * OWN, 8 * HALO_F : 8 * (HALO_F + OWN), :] = f_own[...]
    for index, value in enumerate(received):
        passed = index >= 6
        part = (0, index - 6) if passed else PARTS[index]
        end = column_count(PARTS[index - 6] if passed else part, HALO_U) * 8
        place(u_reg, value[:end, :], part, flags, HALO_U, passed)
        place(f_reg, value[end:, :], part, flags, HALO_F, passed)
    zero = jnp.zeros((1, 128), F32)
    for e in range(-3, 7):
        rows = [moduli_row(f_reg, e, f, 6) for f in range(-3, 7)]
        young[e + 3] = jnp.concatenate(rows + [zero] * 6, axis=0)
    for e in range(-1, 5):
        rows = [moduli_row(f_reg, e, f, 7) for f in range(-1, 5)]
        factor[e + 1] = jnp.concatenate(rows + [zero] * 2, axis=0)

    def inverse(x):
        e = x // 2
        near = young[e] + young[e + 1] if x % 2 == 0 else young[e + 1]
        both = near + pltpu.roll(near, 1, 0)
        lines = {}
        for pb, total in ((0, both), (1, near)):
            before = jnp.where(iota(total.shape, 1) > 0, pltpu.roll(total, 1, 1), 0.0)
            for pc, value in ((0, total + before), (1, total)):
                lines[pb, pc] = jnp.where(value > 0.0, 1.0 / value, 0.0)
        row = iota((8, 128), 0)
        cols = []
        for y in range(17):
            pb, f = y % 2, y // 2 + 1
            even, odd = [
                lines[pb, pc][f : f + 1] * u_reg[x + 4, 8 * (y + 1) + 6 + pc : 8 * (y + 1) + 7 + pc, :]
                for pc in range(2)
            ]
            line = jnp.where(row < 3, jnp.broadcast_to(even, (8, 128)), jnp.broadcast_to(odd, (8, 128)))
            cols.append(line * diag[(x % 2) * 2 + pb])
        dinv[x] = jnp.concatenate(cols, axis=0)

    for x in range(17):
        inverse(x)

    def operand(x):
        split_store(load_columns(u_reg, x + 4, 1, 17), x, s_ref, t_ref)

    for x in range(17):
        operand(x)
    apply(matrix, s_ref, t_ref, young, w_ref, o_ref, 8, 4, 1)

    def residual(x):
        image = collect(w_ref, o_ref, x + 2, 2, 13)
        inv = load_columns(dinv, x + 2, 2, 13)
        res = load_columns(f_reg, x + 6, 1, 13) - image
        z0 = inv * res
        store_columns(z0_ref, x, z0)
        store_columns(u_ref, x, load_columns(u_reg, x + 6, 3, 13))

        if 2 <= x < 10:
            store_columns(w0_ref, x - 2, jnp.where(inv > 0.0, res, 0.0)[2:10])

    for x in range(13):
        residual(x)

    def operand_0(x):
        split_store(load_columns(z0_ref, x, 0, 13), x, s_ref, t_ref)

    for x in range(13):
        operand_0(x)
    apply(matrix, s_ref, t_ref, young, w_ref, o_ref, 5, 3, 2, last=(0, 1))

    def image_1(x):
        image = collect(w_ref, o_ref, x + 2, 2, 8)
        inv = load_columns(dinv, x + 4, 4, 8)
        image = SHIFTS[0] * jnp.where(inv > 0.0, image, 0.0)
        store_columns(w1_ref, x, load_columns(w0_ref, x, 0, 8) - image)
        store_columns(z1_ref, x, load_columns(z0_ref, x + 2, 2, 8) - inv * image)

    for x in range(OWN):
        image_1(x)
    for part, send in zip(PARTS, sends):
        cols = take(z1_ref, part, flags, HALO_Z)
        extra = send.shape[0] * 8 // 6 - cols.shape[0]
        if extra:
            cols = jnp.concatenate([cols, jnp.zeros((extra, 128), F32)], axis=0)
        send[...] = dense(cols.reshape(-1, 8, 128))


def second_kernel(matrix, z1_own, dinv, young, w0_ref, w1_ref, z0_ref, u_ref, f_own, *rest):
    received, rest = rest[:8], rest[8:]
    (z1_ref, z2_ref, z3_ref, sums_ref), rest = rest[:4], rest[4:]
    z_reg, s_ref, t_ref, w_ref, o_ref, w2_ref, w3_ref = rest
    flags = position()
    z_reg[OWN : 2 * OWN, 8 * HALO_Z : 8 * (HALO_Z + OWN), :] = z1_own[...]
    for index, value in enumerate(received):
        passed = index >= 6
        part = (0, index - 6) if passed else PARTS[index]
        count = column_count(PARTS[index - 6] if passed else part, HALO_Z)
        place(z_reg, sparse(value[...])[:count], part, flags, HALO_Z, passed)

    def operand_1(x):
        split_store(load_columns(z_reg, x + 2, 1, 21), x, s_ref, t_ref)

    for x in range(21):
        operand_1(x)

    def keep(x):
        store_columns(z1_ref, x, load_columns(z_reg, x + 6, 5, 13))

    for x in range(13):
        keep(x)
    apply(matrix, s_ref, t_ref, young, w_ref, o_ref, 10, 5, 0)

    def image_2(x):
        image = collect(w_ref, o_ref, x + 2, 2, 17)
        inv = load_columns(dinv, x, 0, 17)
        image = SHIFTS[1] * jnp.where(inv > 0.0, image, 0.0)
        z2 = load_columns(z_reg, x + 4, 3, 17) - inv * image
        split_store(z2, x, s_ref, t_ref)

        if 2 <= x < 15:
            store_columns(z2_ref, x - 2, z2[2:15])

        if 4 <= x < 12:
            store_columns(w2_ref, x - 4, load_columns(w1_ref, x - 4, 0, 8) - image[4:12])

    for x in range(17):
        image_2(x)
    apply(matrix, s_ref, t_ref, young, w_ref, o_ref, 8, 4, 1)

    def image_3(x):
        image = collect(w_ref, o_ref, x + 2, 2, 13)
        inv = load_columns(dinv, x + 2, 2, 13)
        image = SHIFTS[2] * jnp.where(inv > 0.0, image, 0.0)
        z3 = load_columns(z2_ref, x, 0, 13) - inv * image
        split_store(z3, x, s_ref, t_ref)
        store_columns(z3_ref, x, z3)

        if 2 <= x < 10:
            store_columns(w3_ref, x - 2, load_columns(w2_ref, x - 2, 0, 8) - image[2:10])

    for x in range(13):
        image_3(x)
    apply(matrix, s_ref, t_ref, young, w_ref, o_ref, 5, 3, 2, last=(0, 1))
    sums = [jnp.zeros((8, 128), F32) for _ in dot_list()]

    def dots(x):
        inv = load_columns(dinv, x + 4, 4, 8)
        w = [load_columns(ref, x, 0, 8) for ref in (w0_ref, w1_ref, w2_ref, w3_ref)]
        w.append(w[3] - SHIFTS[3] * jnp.where(inv > 0.0, collect(w_ref, o_ref, x + 2, 2, 8), 0.0))
        z = [inv * value for value in w[:4]]
        load = jnp.where(inv > 0.0, load_columns(f_own, x, 0, 8), 0.0)
        u = load_columns(u_ref, x + 2, 2, 8)
        for index, (first, second) in enumerate(dot_list()):
            first = u if first is None else (w if first[0] == "w" else z)[first[1]]
            second = load if second is None else w[second[1]]
            sums[index] += jnp.sum(first * second, axis=0)

    for x in range(OWN):
        dots(x)
    shape = (48, 128)
    lines = [jnp.sum(value, axis=0, keepdims=True) for value in sums]
    lines = jnp.concatenate(lines + [jnp.zeros((shape[0] - len(lines), 128), F32)], axis=0)
    totals = jnp.sum(lines, axis=1, keepdims=True)
    line = jnp.sum(
        jnp.where(iota(shape, 0) == iota(shape, 1), jnp.broadcast_to(totals, shape), 0.0),
        axis=0,
        keepdims=True,
    )
    sums_ref[...] = jnp.broadcast_to(line, sums_ref.shape)


def dot_list():
    out = [(("w", i), ("w", j)) for i in range(5) for j in range(i, 5)]
    out += [(None, None)] + [(("z", i), None) for i in range(4)]
    out += [(None, ("w", j)) for j in range(5)]
    out += [(("z", i), ("w", j)) for i in range(4) for j in range(i, 5)]
    return out


def step_sizes(total):
    place_of = {pair: index for index, pair in enumerate(dot_list())}

    def gram(i, j):
        return total(place_of[("w", min(i, j)), ("w", max(i, j))])

    poly = [jnp.ones((1, 128), F32)]
    coef = [jnp.zeros((1, 128), F32)] * SWEEPS
    for sweep in range(SWEEPS):
        scaled = [poly[i] / SHIFTS[i] for i in range(sweep + 1)]
        image = [scaled[0]] + [scaled[i] - scaled[i - 1] for i in range(1, sweep + 1)] + [-scaled[sweep]]
        times = [sum(gram(i, j) * image[j] for j in range(sweep + 2)) for i in range(sweep + 2)]
        top = sum(poly[i] * times[i] for i in range(sweep + 1))
        bottom = sum(image[i] * times[i] for i in range(sweep + 2))
        omega = top / bottom
        for i in range(sweep + 1):
            coef[i] = coef[i] + omega * poly[i]
        poly = [
            (poly[i] if i <= sweep else 0.0) - omega * image[i] for i in range(sweep + 2)
        ]
    work = total(place_of[None, None])
    for i in range(SWEEPS):
        work = work + coef[i] * total(place_of[("z", i), None])
    for j in range(SWEEPS + 1):
        part = total(place_of[None, ("w", j)])
        for i in range(SWEEPS):
            part = part + coef[i] * total(place_of[("z", min(i, j)), ("w", max(i, j))])
        work = work - poly[j] * part
    return coef, work


def last_kernel(matrix, sums, u_ref, z0_ref, z1_ref, z2_ref, z3_ref, factor, *rest):
    (out_u, out_f, out_c), (own, s_ref, t_ref, uf_ref, tf_ref, sens_ref) = rest[:3], rest[3:]
    flags = position()
    line = jnp.sum(sums[...], axis=0, keepdims=True)
    shape = (48, 128)
    spread = jnp.where(iota(shape, 0) == iota(shape, 1), jnp.broadcast_to(line, shape), 0.0)
    spread = jnp.broadcast_to(jnp.sum(spread, axis=1, keepdims=True), shape)
    coef, work = step_sizes(lambda index: spread[index : index + 1])
    out_c[...] = work

    def combine(x):
        value = load_columns(u_ref, x, 0, 13)
        for index, ref in enumerate((z0_ref, z1_ref, z2_ref, z3_ref)):
            value = value + coef[index] * load_columns(ref, x, 0, 13)
        store_columns(uf_ref, x, value)
        store_columns(tf_ref, x, split_store(value, x, s_ref, t_ref))
        if 2 <= x < 10:
            store_columns(own, x - 2, value[2:10])

    for x in range(13):
        combine(x)

    for i in range(6):
        for j in range(0, 6, 2):
            both = products(matrix[...], s_ref, t_ref, 2 * i, j)
            for e in range(2):
                k = j + e
                acc = jnp.zeros((8, 128), F32)
                for a in range(3):
                    left = uf_ref[2 * i + a, 16 * k : 16 * k + 24, :] * both[e][a][:24]
                    right = tf_ref[2 * i + a, 8 * k : 8 * k + 16, :] * both[e][a][24:]
                    acc = acc + left[:8] + left[8:16] + left[16:] + right[:8] + right[8:]
                sens_ref[i, k : k + 1, :] = jnp.sum(acc, axis=0, keepdims=True)
        sens_ref[i, 6:8, :] = jnp.zeros((2, 128), F32)
    edge = RADIUS - 1.0
    corner = RADIUS - math.sqrt(2.0)
    row = iota((8, 128), 0)
    lane = iota((8, 128), 1)
    sens = [sens_ref[x] * factor[x] for x in range(6)]
    low, high = flags[LOW_Y].astype(F32), flags[HIGH_Y].astype(F32)
    inside = jnp.where(row == 0, low, jnp.where(row < 5, 1.0, jnp.where(row == 5, high, 0.0)))
    inside_x = [flags[LOW_X].astype(F32)] + [1.0] * 4 + [flags[HIGH_X].astype(F32)]
    covered = [inside * value for value in inside_x]

    def along_y(v):
        return pltpu.roll(v, 1, 0) + pltpu.roll(v, 7, 0)

    def along_z(v):
        return jnp.where(lane > 0, pltpu.roll(v, 1, 1), 0.0) + jnp.where(lane < 127, pltpu.roll(v, 127, 1), 0.0)

    def gathered(layers, x):
        here, sides = layers[x], layers[x - 1] + layers[x + 1]
        ys = along_y(here)
        return (
            RADIUS * here
            + edge * (ys + along_z(here) + sides)
            + corner * (along_z(ys) + along_y(sides) + along_z(sides))
        )

    for x in range(ELEMS):
        out_f[x] = (gathered(sens, x + 1) / gathered(covered, x + 1))[1:5]
    merge = parity_matrix(True)
    for x in range(OWN):
        rows = [
            jnp.concatenate(
                [own[x, pl.ds(comp + 3 * parity, 8, stride=8), :] for parity in range(2)], axis=1
            )
            for comp in range(3)
        ]
        joined = exact_product(jnp.concatenate(rows, axis=0), merge)
        for comp in range(3):
            out_u[comp, x] = joined[8 * comp : 8 * comp + 8]


def partners(part, count_x, count_y):
    def other(i, k, count):
        if k is None:
            return i
        if k == 0:
            return i ^ 1
        return ((i + 1) ^ 1) - 1 if 0 < i < count - 1 else None

    out = []
    for x in range(count_x):
        for y in range(count_y):
            px, py = other(x, part[0], count_x), other(y, part[1], count_y)
            if px is None and py is None:
                px, py = count_x - 1 - x, y
            elif px is None:
                px, py = x, (y ^ 1 if part[1] is None else py)
            elif py is None:
                px, py = (x ^ 1 if part[0] is None else px), y
            out.append((x * count_y + y, px * count_y + py))
    return out


def shapes(*items):
    return [jax.ShapeDtypeStruct(item, F32) for item in items]


def call(kernel, out_shape, scratch, operands):
    spec = pl.BlockSpec(memory_space=pltpu.VMEM)
    return pl.pallas_call(
        kernel,
        out_shape=out_shape,
        in_specs=[spec] * len(operands),
        out_specs=[spec] * len(out_shape),
        scratch_shapes=scratch,
        compiler_params=pltpu.CompilerParams(vmem_limit_bytes=24 * 1024 * 1024),
    )(*operands)


def body(force, load_mask, support_mask, start_field, density, passive_mask):
    count_x, count_y = lax.axis_size("sx"), lax.axis_size("sy")
    devices = count_x * count_y
    stiff = element_matrix()
    matrix = jnp.asarray(operator_matrix(stiff))
    diag = jnp.asarray(diagonal_columns(stiff))
    zero = F32(0.0)
    none = (0, 0, 0)
    small = ((0, OWN - ELEMS, 0), (0, OWN - ELEMS, 0), (0, 128, 0))
    fields = (
        lax.pad(start_field, zero, ((0, 7, 0), none, none, none))
        + lax.pad(force, zero, ((3, 4, 0), none, none, none))
        + lax.pad(density[None], zero, ((8, 1, 0), *small))
        + (
            lax.pad(load_mask[None], 0, ((6, 3, 0), none, none, none))
            + lax.pad(support_mask[None], 0, ((7, 2, 0), none, none, none))
            + lax.pad(passive_mask[None], 0, ((9, 0, 0), *small))
        ).astype(F32)
    )

    def send(value, part):
        return lax.ppermute(value, ("sx", "sy"), partners(part, count_x, count_y))

    def swap(values):
        first, second, *corners, x_side = [send(value, part) for part, value in zip(PARTS[:5], values)]
        x_side, mate = lax.optimization_barrier((x_side, values[5]))
        *corners, second = lax.optimization_barrier((*corners, second))
        passed = [send(value, MATE) for value in (mate, first, second)]
        return [first, second, *corners, x_side, *passed]

    def sizes(width):
        return [column_count(part, width) for part in PARTS]

    own = (OWN, OWN * 8, 128)
    middle = (13, 13 * 8, 128)
    first = call(
        prepare_kernel,
        [
            *shapes(own, own),
            *shapes(*((8 * (a + b), 128) for a, b in zip(sizes(HALO_U), sizes(HALO_F)))),
        ],
        [],
        [fields],
    )
    u_own, f_own = first[:2]
    second = call(
        first_kernel,
        shapes(
            middle,
            middle,
            (17, 17 * 8, 128),
            (10, 16, 128),
            (6, 8, 128),
            own,
            own,
            own,
            *(((a + 3) // 4 * 24, 128) for a in sizes(HALO_Z)),
        ),
        [
            pltpu.VMEM((24, 18 * 8, 128), F32),
            pltpu.VMEM((24, 14 * 8, 128), F32),
            pltpu.VMEM((17, 17 * 16, 128), BF16),
            pltpu.VMEM((17, 9 * 16, 128), BF16),
            pltpu.VMEM((17, 17 * 8, 128), F32),
            pltpu.VMEM((17, 9 * 8, 128), F32),
        ],
        [matrix, diag, u_own, f_own, *swap(first[2:])],
    )
    z0, u0, dinv, young, factor, w0, w1, z1 = second[:8]
    z1, z2, z3, sums = call(
        second_kernel,
        shapes(middle, middle, middle, (devices, 128)),
        [
            pltpu.VMEM((24, 22 * 8, 128), F32),
            pltpu.VMEM((21, 21 * 16, 128), BF16),
            pltpu.VMEM((21, 11 * 16, 128), BF16),
            pltpu.VMEM((21, 21 * 8, 128), F32),
            pltpu.VMEM((21, 11 * 8, 128), F32),
            pltpu.VMEM(own, F32),
            pltpu.VMEM(own, F32),
        ],
        [matrix, z1, dinv, young, w0, w1, z0, u0, f_own, *swap(second[8:])],
    )
    sums = lax.all_to_all(sums, ("sx", "sy"), 0, 0, tiled=True)
    displacement, filtered, compliance = call(
        last_kernel,
        shapes(start_field.shape, density.shape, (1, 128)),
        [
            pltpu.VMEM(own, F32),
            pltpu.VMEM((13, 13 * 16, 128), BF16),
            pltpu.VMEM((13, 7 * 16, 128), BF16),
            pltpu.VMEM(middle, F32),
            pltpu.VMEM((13, 7 * 8, 128), F32),
            pltpu.VMEM((6, 8, 128), F32),
        ],
        [matrix, sums, u0, z0, z1, z2, z3, factor],
    )
    return displacement, filtered, compliance[0, 0]


def solution(mesh):
    in_specs = (
        P(None, "sx", "sy", None),
        P("sx", "sy", None),
        P("sx", "sy", None),
        P(None, "sx", "sy", None),
        P("sx", "sy", None),
        P("sx", "sy", None),
    )
    out_specs = (P(None, "sx", "sy", None), P("sx", "sy", None), P())
    return jax.shard_map(body, mesh=mesh, in_specs=in_specs, out_specs=out_specs, check_vma=False)
```

```python
import functools
import math

import jax
import jax.numpy as jnp
import numpy as np
from jax import lax
from jax.experimental import pallas as pl
from jax.experimental.pallas import tpu as pltpu
from jax.sharding import PartitionSpec as P

SWEEPS = 4
EMIN = 0.001
RADIUS = 1.5

OWN = 8
ELEMS = OWN // 2
HALO_U = 5
HALO_F = 3
HALO_Z = 7
PARTS = [
    (None, 0),
    (None, 1),
    (1, 0),
    (1, 1),
    (1, None),
    (0, None),
]
MATE = (0, None)
UP_X, UP_Y, LOW_X, HIGH_X, LOW_Y, HIGH_Y = range(6)
SHIFTS = (0.59, 0.73, 0.645, 0.69)
F32 = jnp.float32
BF16 = jnp.bfloat16


def element_matrix():
    poisson = 0.3
    lame_first = poisson / ((1.0 + poisson) * (1.0 - 2.0 * poisson))
    shear = 1.0 / (2.0 * (1.0 + poisson))
    elastic = np.zeros((6, 6))
    elastic[:3, :3] = lame_first
    for entry in range(3):
        elastic[entry, entry] += 2.0 * shear
        elastic[entry + 3, entry + 3] = shear
    points = [-math.sqrt(0.6), 0.0, math.sqrt(0.6)]
    weights = [5.0 / 9.0, 8.0 / 9.0, 5.0 / 9.0]

    def values(point):
        return np.array(
            [point * (point - 1.0) / 2.0, 1.0 - point * point, point * (point + 1.0) / 2.0]
        )

    def slopes(point):
        return np.array([point - 0.5, -2.0 * point, point + 0.5])

    stiff = np.zeros((81, 81))
    for first in range(3):
        for second in range(3):
            for third in range(3):
                val_x, val_y, val_z = (
                    values(points[first]),
                    values(points[second]),
                    values(points[third]),
                )
                der_x, der_y, der_z = (
                    slopes(points[first]),
                    slopes(points[second]),
                    slopes(points[third]),
                )
                strain = np.zeros((6, 81))
                for node_a in range(3):
                    for node_b in range(3):
                        for node_c in range(3):
                            node = node_a * 9 + node_b * 3 + node_c
                            grad_x = 2.0 * der_x[node_a] * val_y[node_b] * val_z[node_c]
                            grad_y = 2.0 * val_x[node_a] * der_y[node_b] * val_z[node_c]
                            grad_z = 2.0 * val_x[node_a] * val_y[node_b] * der_z[node_c]
                            strain[0, node] = grad_x
                            strain[1, 27 + node] = grad_y
                            strain[2, 54 + node] = grad_z
                            strain[3, node] = grad_y
                            strain[3, 27 + node] = grad_x
                            strain[4, 27 + node] = grad_z
                            strain[4, 54 + node] = grad_y
                            strain[5, node] = grad_z
                            strain[5, 54 + node] = grad_x
                factor = weights[first] * weights[second] * weights[third] * 0.125
                stiff = stiff + factor * strain.T @ elastic @ strain
    return stiff


def balanced_parts(stiff):
    hi = stiff.astype(BF16).astype(np.float64)
    lo = (stiff - hi).astype(BF16).astype(np.float64)
    unit = 2.0 ** (np.floor(np.log2(np.maximum(np.abs(lo), 1e-30))) - 7)
    left = (hi + lo).reshape(81, 3, 27).sum(axis=2)
    moved = np.zeros((81, 81))
    for _ in range(6):
        for i in range(81):
            for j in range(i):
                first, second = left[i, j // 27], left[j, i // 27]
                step = np.clip(np.round(-(first + second) / 2 / unit[i, j]), -1 - moved[i, j], 1 - moved[i, j])
                if step and lo[i, j]:
                    moved[i, j] += step
                    left[i, j // 27] += step * unit[i, j]
                    left[j, i // 27] += step * unit[i, j]
    moved = moved + moved.T
    return hi.astype(np.float32), (lo + moved * unit).astype(np.float32)


def operator_matrix(stiff):
    hi, lo = balanced_parts(stiff)
    out = np.zeros((240, 256), np.float32)

    def out_row(comp, a, b, c):
        if c < 2:
            return 80 * a + b * 8 + c * 3 + comp
        return 80 * a + 24 + (b // 2) * 8 + (b % 2) * 4 + comp

    def in_row(comp, a, b, c, low):
        if c < 2:
            return (a * 3 + b) * 16 + low * 8 + c * 3 + comp
        return 144 + (a * 2 + b // 2) * 16 + low * 8 + (b % 2) * 4 + comp

    index = [(p, a, b, c) for p in range(3) for a in range(3) for b in range(3) for c in range(3)]
    for i, first in enumerate(index):
        for j, second in enumerate(index):
            row = out_row(*first)
            out[row, in_row(*second, 0)] = hi[i, j]
            out[row, in_row(*second, 1)] = hi[i, j]
            out[row + 40, in_row(*second, 0)] = lo[i, j]
            out[row + 40, in_row(*second, 1)] = lo[i, j]
    return out.astype(BF16)


def diagonal_columns(stiff):
    out = np.zeros((4, 8, 128), np.float32)
    for pa in range(2):
        for pb in range(2):
            for c in range(2):
                for comp in range(3):
                    dof = comp * 27 + pa * 9 + pb * 3 + c
                    out[pa * 2 + pb, c * 3 + comp] = 1.0 / stiff[dof, dof]
    return out


def iota(shape, dim):
    return lax.broadcasted_iota(jnp.int32, shape, dim)


def parity_matrix(transposed):
    node = iota((256, 256), 1 if transposed else 0)
    place = iota((256, 256), 0 if transposed else 1)
    return (node == 2 * (place % 128) + place // 128).astype(F32).astype(BF16)


def exact_product(rows, matrix):
    first = rows.astype(BF16)
    left = rows - first.astype(F32)
    second = left.astype(BF16)
    third = (left - second.astype(F32)).astype(BF16)
    stacked = jnp.concatenate([first, second, third], axis=0)
    out = jnp.dot(stacked, matrix, preferred_element_type=F32)
    count = rows.shape[0]
    return out[:count] + out[count : 2 * count] + out[2 * count :]


def span(k, up, width):
    if k is None:
        return 0, OWN
    upward = up if k == 0 else 1 - up
    return upward * (OWN - width), width


def landing(k, up, width, margin):
    if k is None:
        return margin, OWN
    upward = up if k == 0 else 1 - up
    return upward * (OWN + margin) + (1 - upward) * (margin - width), width


def rows8(start):
    return pl.multiple_of(start * 8, 8) if not isinstance(start, int) else start * 8


def part_shape(part, width):
    return [OWN if k is None else width for k in part]


def take(ref, part, flags, width):
    sx, nx = span(part[0], flags[UP_X], width)
    sy, ny = span(part[1], flags[UP_Y], width)
    return ref[pl.ds(sx, nx), pl.ds(rows8(sy), ny * 8), :].reshape(nx * ny * 8, 128)


def place(ref, value, part, flags, width, passed=False):
    dx, nx = landing(part[0], flags[UP_X], OWN if passed else width, OWN)
    dy, ny = landing(part[1], flags[UP_Y], width, width)
    valid = present(part[0], flags, 0) * present(part[1], flags, 1)
    value = value * valid.astype(F32)
    ref[pl.ds(dx, nx), pl.ds(rows8(dy), ny * 8), :] = value.reshape(nx, ny * 8, 128)


def position():
    index = [lax.axis_index(axis) for axis in ("sx", "sy")]
    last = [lax.axis_size(axis) - 1 for axis in ("sx", "sy")]
    out = [1 - lax.rem(i, 2) for i in index]
    for i, end in zip(index, last):
        out += [jnp.minimum(i, 1), jnp.minimum(end - i, 1)]
    return out


def dense(cols):
    count = cols.shape[0] // 4
    c = cols.reshape(count, 4, 8, 128)
    row = iota((count, 8, 128), 1)
    tiles = [
        jnp.where(row < 6, c[:, 0], pltpu.roll(c[:, 1], 6, 1)),
        jnp.where(row < 4, pltpu.roll(c[:, 1], 6, 1), pltpu.roll(c[:, 2], 4, 1)),
        jnp.where(row < 2, pltpu.roll(c[:, 2], 4, 1), pltpu.roll(c[:, 3], 2, 1)),
    ]
    return jnp.stack(tiles, axis=1).reshape(count * 24, 128)


def sparse(rows):
    count = rows.shape[0] // 24
    t = rows.reshape(count, 3, 8, 128)
    row = iota((count, 8, 128), 1)
    cols = [
        t[:, 0],
        jnp.where(row < 2, pltpu.roll(t[:, 0], 2, 1), pltpu.roll(t[:, 1], 2, 1)),
        jnp.where(row < 4, pltpu.roll(t[:, 1], 4, 1), pltpu.roll(t[:, 2], 4, 1)),
        pltpu.roll(t[:, 2], 6, 1),
    ]
    return jnp.stack(cols, axis=1).reshape(count * 4, 8, 128)


def column_count(part, width):
    return math.prod(part_shape(part, width))


def present(k, flags, dim):
    if k is None:
        return 1
    up, low, high = flags[(UP_X, UP_Y)[dim]], flags[(LOW_X, LOW_Y)[dim]], flags[(HIGH_X, HIGH_Y)[dim]]
    upward = up if k == 0 else 1 - up
    return upward * high + (1 - upward) * low


def young_place(e):
    return e if e <= 2 else 7 if e == 3 else e + 4


def moduli_row(f_reg, e, f, row):
    start = 8 * (young_place(f) + HALO_F) + row
    return f_reg[young_place(e) + OWN, start : start + 1, :]


def parts_of(z):
    far = z * 65537.0
    hi = far - (far - z)
    return jnp.concatenate([hi, z - hi], axis=1).astype(BF16).reshape(z.shape[0] * 16, 128)


def split_store(z, x, s_ref, t_ref):
    count = z.shape[0]
    s_ref[x, : count * 16, :] = parts_of(z)
    if count % 2:
        z = jnp.concatenate([z, z[count - 1 :]], axis=0)
        count += 1
    z = z.reshape(count // 2, 2, 8, 128)
    nxt = jnp.where(iota((count // 2, 8, 128), 1) < 4, z[:, 0], pltpu.roll(z[:, 1], 4, 1))
    nxt = pltpu.roll(nxt.reshape(count * 4, 128), 127, 1)
    nxt = jnp.where(iota(nxt.shape, 1) < 127, nxt, 0.0).reshape(count // 2, 8, 128)
    t_ref[x, : count * 8, :] = parts_of(nxt)
    return nxt


def element_operand(s_ref, t_ref, x, y, pair):
    pieces = [s_ref[x + a, pl.ds(y * 16, 48), :] for a in range(3)]
    pieces += [t_ref[x + a, pl.ds(pair * 16, 32), :] for a in range(3)]
    pieces.append(jnp.zeros((16, 128), BF16))
    return jnp.concatenate(pieces, axis=0)


def products(matrix, s_ref, t_ref, x, j):
    operand = jnp.concatenate(
        [element_operand(s_ref, t_ref, x, 2 * e, e) for e in (j, j + 1)], axis=1
    )
    out = jnp.dot(matrix, operand, preferred_element_type=F32)
    layers = [out[r : r + 40] + out[r + 40 : r + 80] for r in range(0, matrix.shape[0], 80)]
    return [[layer[:, :128] for layer in layers], [layer[:, 128:] for layer in layers]]


def apply(matrix_ref, s_ref, t_ref, young_ref, w_ref, o_ref, count_x, pairs_y, young_at, last=(0,)):
    for i in range(count_x):
        layers = (2,) if i == 0 else last if i == count_x - 1 else (0, 1, 2)
        matrix = matrix_ref[80 * layers[0] : 80 * (layers[-1] + 1), :]
        tails = [None] * 3
        for j in range(0, 2 * pairs_y, 2):
            both = products(matrix, s_ref, t_ref, 2 * i, j)
            for e in range(2):
                k = j + e
                scale = young_ref[i + young_at, k + young_at : k + young_at + 1, :]
                for a, out in zip(layers, both[e]):
                    out = out * scale
                    x = 2 * i + a
                    nodes, over = out[:16], out[24:32]
                    if tails[a] is not None:
                        nodes = jnp.concatenate([nodes[:8] + tails[a][0], nodes[8:]], axis=0)
                        over = over + tails[a][1]
                    if a == 0:
                        nodes = nodes + w_ref[x, 16 * k : 16 * k + 16, :]
                        over = over + o_ref[x, 8 * k : 8 * k + 8, :]
                    w_ref[x, 16 * k : 16 * k + 16, :] = nodes
                    o_ref[x, 8 * k : 8 * k + 8, :] = over
                    tails[a] = (out[16:24], out[32:40])
        k = 2 * pairs_y
        for a in layers:
            x = 2 * i + a
            nodes, over = tails[a]
            if a == 0:
                nodes = nodes + w_ref[x, 16 * k : 16 * k + 8, :]
                over = over + o_ref[x, 8 * k : 8 * k + 8, :]
            w_ref[x, 16 * k : 16 * k + 8, :] = nodes
            o_ref[x, 8 * k : 8 * k + 8, :] = over


def collect(w_ref, o_ref, x, low, count):
    half = (count + 1) // 2
    moved = pltpu.roll(o_ref[x, 4 * low : 4 * low + 8 * half, :], 1, 1)
    moved = jnp.where(iota(moved.shape, 1) > 0, moved, 0.0).reshape(half, 8, 128)
    row = iota(moved.shape, 1)
    even = jnp.where(row < 3, moved, 0.0)
    odd = jnp.where(row < 3, pltpu.roll(moved, 4, 1), 0.0)
    both = jnp.stack([even, odd], axis=1).reshape(2 * half, 8, 128)[:count]
    return w_ref[x, 8 * low : 8 * (low + count), :].reshape(count, 8, 128) + both


def load_columns(ref, x, low, count):
    return ref[x, 8 * low : 8 * (low + count), :].reshape(count, 8, 128)


def store_columns(ref, x, value):
    ref[x, : 8 * value.shape[0], :] = value.reshape(8 * value.shape[0], 128)


def prepare_kernel(fields, u_ref, f_ref, *sends):
    flags = position()
    matrix = parity_matrix(False)
    solid = fields[9, :ELEMS, :ELEMS, :128] == 1.0
    rho = jnp.where(solid, 1.0, fields[8, :ELEMS, :ELEMS, :128])
    young = EMIN + (1.0 - EMIN) * (rho * rho * rho)
    factor = jnp.where(solid, 0.0, -3.0 * (1.0 - EMIN) * (rho * rho))
    for x in range(OWN):
        free = 1.0 - fields[7, x]
        loaded = free * fields[6, x]
        rows = [free * fields[c, x] for c in range(3)] + [loaded * fields[c, x] for c in range(3, 6)] + [free]
        split = exact_product(jnp.concatenate(rows, axis=0), matrix)
        for index in range(7):
            ref, row = ((u_ref, index), (f_ref, index - 3), (u_ref, 6))[index // 3]
            step = 1 if index == 6 else 3
            for parity in range(2):
                ref[x, pl.ds(row + parity * step, 8, stride=8), :] = split[
                    8 * index : 8 * index + 8, 128 * parity : 128 * parity + 128
                ]
        element = {0: 0, 1: 1, 2: 2, 5: 1, 6: 2, 7: 3}.get(x)
        for row, values in ((6, young), (7, factor)):
            if element is None:
                column = jnp.zeros((8, 128), F32)
            else:
                column = jnp.concatenate(
                    [values[element, :3], jnp.zeros((2, 128), F32), values[element, 1:]], axis=0
                )
            f_ref[x, pl.ds(row, 8, stride=8), :] = column
    for part, send in zip(PARTS, sends):
        first = take(u_ref, part, flags, HALO_U)
        send[: first.shape[0], :] = first
        send[first.shape[0] :, :] = take(f_ref, part, flags, HALO_F)


def first_kernel(matrix, diag, u_own, f_own, *rest):
    flags = position()
    received, rest = rest[:8], rest[8:]
    (z0_ref, u_ref, dinv, young, factor, v0_ref, g0_ref, z1_ref), rest = rest[:8], rest[8:]
    sends, (u_reg, f_reg, s_ref, t_ref, w_ref, o_ref) = rest[:6], rest[6:]
    u_reg[OWN : 2 * OWN, 8 * HALO_U : 8 * (HALO_U + OWN), :] = u_own[...]
    f_reg[OWN : 2 * OWN, 8 * HALO_F : 8 * (HALO_F + OWN), :] = f_own[...]
    for index, value in enumerate(received):
        passed = index >= 6
        part = (0, index - 6) if passed else PARTS[index]
        end = column_count(PARTS[index - 6] if passed else part, HALO_U) * 8
        place(u_reg, value[:end, :], part, flags, HALO_U, passed)
        place(f_reg, value[end:, :], part, flags, HALO_F, passed)
    zero = jnp.zeros((1, 128), F32)
    for e in range(-3, 7):
        rows = [moduli_row(f_reg, e, f, 6) for f in range(-3, 7)]
        young[e + 3] = jnp.concatenate(rows + [zero] * 6, axis=0)
    for e in range(-1, 5):
        rows = [moduli_row(f_reg, e, f, 7) for f in range(-1, 5)]
        factor[e + 1] = jnp.concatenate(rows + [zero] * 2, axis=0)

    def inverse(x):
        e = x // 2
        near = young[e] + young[e + 1] if x % 2 == 0 else young[e + 1]
        both = near + pltpu.roll(near, 1, 0)
        lines = {}
        for pb, total in ((0, both), (1, near)):
            before = jnp.where(iota(total.shape, 1) > 0, pltpu.roll(total, 1, 1), 0.0)
            for pc, value in ((0, total + before), (1, total)):
                lines[pb, pc] = jnp.where(value > 0.0, 1.0 / value, 0.0)
        row = iota((8, 128), 0)
        cols = []
        for y in range(17):
            pb, f = y % 2, y // 2 + 1
            even, odd = [
                lines[pb, pc][f : f + 1] * u_reg[x + 4, 8 * (y + 1) + 6 + pc : 8 * (y + 1) + 7 + pc, :]
                for pc in range(2)
            ]
            line = jnp.where(row < 3, jnp.broadcast_to(even, (8, 128)), jnp.broadcast_to(odd, (8, 128)))
            cols.append(line * diag[(x % 2) * 2 + pb])
        dinv[x] = jnp.concatenate(cols, axis=0)

    for x in range(17):
        inverse(x)

    def operand(x):
        split_store(load_columns(u_reg, x + 4, 1, 17), x, s_ref, t_ref)

    for x in range(17):
        operand(x)
    apply(matrix, s_ref, t_ref, young, w_ref, o_ref, 8, 4, 1)

    def residual(x):
        image = collect(w_ref, o_ref, x + 2, 2, 13)
        inv = load_columns(dinv, x + 2, 2, 13)
        res = load_columns(f_reg, x + 6, 1, 13) - image
        z0 = inv * res
        store_columns(z0_ref, x, z0)
        store_columns(u_ref, x, load_columns(u_reg, x + 6, 3, 13))

        if 2 <= x < 10:
            store_columns(v0_ref, x - 2, jnp.where(inv > 0.0, res, 0.0)[2:10])

    for x in range(13):
        residual(x)

    def operand_0(x):
        split_store(load_columns(z0_ref, x, 0, 13), x, s_ref, t_ref)

    for x in range(13):
        operand_0(x)
    apply(matrix, s_ref, t_ref, young, w_ref, o_ref, 5, 3, 2, last=(0, 1))

    def image_1(x):
        image = collect(w_ref, o_ref, x + 2, 2, 8)
        inv = load_columns(dinv, x + 4, 4, 8)
        image = SHIFTS[0] * jnp.where(inv > 0.0, image, 0.0)
        store_columns(g0_ref, x, image)
        store_columns(z1_ref, x, load_columns(z0_ref, x + 2, 2, 8) - inv * image)

    for x in range(OWN):
        image_1(x)
    for part, send in zip(PARTS, sends):
        cols = take(z1_ref, part, flags, HALO_Z)
        extra = send.shape[0] * 8 // 6 - cols.shape[0]
        if extra:
            cols = jnp.concatenate([cols, jnp.zeros((extra, 128), F32)], axis=0)
        send[...] = dense(cols.reshape(-1, 8, 128))


def second_kernel(matrix, z1_own, dinv, young, v0_ref, g0_ref, z0_ref, u_ref, f_own, *rest):
    received, rest = rest[:8], rest[8:]
    (z1_ref, z2_ref, z3_ref, sums_ref), rest = rest[:4], rest[4:]
    z_reg, s_ref, t_ref, w_ref, o_ref, g1_ref, g2_ref = rest
    flags = position()
    z_reg[OWN : 2 * OWN, 8 * HALO_Z : 8 * (HALO_Z + OWN), :] = z1_own[...]
    for index, value in enumerate(received):
        passed = index >= 6
        part = (0, index - 6) if passed else PARTS[index]
        count = column_count(PARTS[index - 6] if passed else part, HALO_Z)
        place(z_reg, sparse(value[...])[:count], part, flags, HALO_Z, passed)

    def operand_1(x):
        split_store(load_columns(z_reg, x + 2, 1, 21), x, s_ref, t_ref)

    for x in range(21):
        operand_1(x)

    def keep(x):
        store_columns(z1_ref, x, load_columns(z_reg, x + 6, 5, 13))

    for x in range(13):
        keep(x)
    apply(matrix, s_ref, t_ref, young, w_ref, o_ref, 10, 5, 0)

    def image_2(x):
        image = collect(w_ref, o_ref, x + 2, 2, 17)
        inv = load_columns(dinv, x, 0, 17)
        image = SHIFTS[1] * jnp.where(inv > 0.0, image, 0.0)
        z2 = load_columns(z_reg, x + 4, 3, 17) - inv * image
        split_store(z2, x, s_ref, t_ref)

        if 2 <= x < 15:
            store_columns(z2_ref, x - 2, z2[2:15])

        if 4 <= x < 12:
            store_columns(g1_ref, x - 4, image[4:12])

    for x in range(17):
        image_2(x)
    apply(matrix, s_ref, t_ref, young, w_ref, o_ref, 8, 4, 1)

    def image_3(x):
        image = collect(w_ref, o_ref, x + 2, 2, 13)
        inv = load_columns(dinv, x + 2, 2, 13)
        image = SHIFTS[2] * jnp.where(inv > 0.0, image, 0.0)
        z3 = load_columns(z2_ref, x, 0, 13) - inv * image
        split_store(z3, x, s_ref, t_ref)
        store_columns(z3_ref, x, z3)

        if 2 <= x < 10:
            store_columns(g2_ref, x - 2, image[2:10])

    for x in range(13):
        image_3(x)
    apply(matrix, s_ref, t_ref, young, w_ref, o_ref, 5, 3, 2, last=(0, 1))
    sums = [jnp.zeros((8, 128), F32) for _ in dot_list()]

    def dots(x):
        inv = load_columns(dinv, x + 4, 4, 8)
        v0 = load_columns(v0_ref, x, 0, 8)
        last = SHIFTS[3] * jnp.where(inv > 0.0, collect(w_ref, o_ref, x + 2, 2, 8), 0.0)
        vectors = {
            "v": v0,
            "u": load_columns(u_ref, x + 2, 2, 8),
            "Au": jnp.where(inv > 0.0, load_columns(f_own, x, 0, 8), 0.0) - v0,
            ("z", 0): load_columns(z0_ref, x + 2, 2, 8),
            ("z", 1): load_columns(z1_own, x, 0, 8),
            ("z", 2): load_columns(z2_ref, x + 2, 2, 8),
            ("z", 3): load_columns(z3_ref, x + 2, 2, 8),
            ("g", 0): load_columns(g0_ref, x, 0, 8),
            ("g", 1): load_columns(g1_ref, x, 0, 8),
            ("g", 2): load_columns(g2_ref, x, 0, 8),
            ("g", 3): last,
        }
        for index, (one, other) in enumerate(dot_list()):
            first, second = vectors[one], vectors[other]
            sums[index] += jnp.sum(first * second, axis=0)

    for x in range(OWN):
        dots(x)
    shape = (48, 128)
    lines = [jnp.sum(value, axis=0, keepdims=True) for value in sums]
    lines = jnp.concatenate(lines + [jnp.zeros((shape[0] - len(lines), 128), F32)], axis=0)
    totals = jnp.sum(lines, axis=1, keepdims=True)
    line = jnp.sum(
        jnp.where(iota(shape, 0) == iota(shape, 1), jnp.broadcast_to(totals, shape), 0.0),
        axis=0,
        keepdims=True,
    )
    sums_ref[...] = jnp.broadcast_to(line, sums_ref.shape)


def dot_list():
    steps = range(SWEEPS)
    out = [("v", ("g", j)) for j in steps]
    out += [(("g", i), ("g", j)) for i in steps for j in steps if i <= j]
    out += [("u", "Au")] + [(("z", i), "Au") for i in steps] + [("u", ("g", j)) for j in steps]
    out += [(("z", i), ("g", j)) for i in steps for j in steps if i <= j]
    return out


def step_sizes(total):
    place_of = {pair: index for index, pair in enumerate(dot_list())}

    def dot(one, other):
        return total(place_of[one, other])

    def gram(i, j):
        return dot(("g", min(i, j)), ("g", max(i, j)))

    def work_of(i, j):
        if i <= j:
            return dot(("z", i), ("g", j))
        return dot(("z", j), ("g", i)) * (SHIFTS[j] / SHIFTS[i])

    taken = [jnp.zeros((1, 128), F32)] * SWEEPS
    coef = list(taken)
    for sweep in range(SWEEPS):
        known = range(sweep + 1)
        part = [(taken[i - 1] if i else 1.0) - taken[i] for i in known]
        image = [part[i] / SHIFTS[i] for i in known]
        top = sum(
            image[j] * (dot("v", ("g", j)) - sum(taken[i] * gram(i, j) for i in known)) for j in known
        )
        bottom = sum(image[j] * sum(image[i] * gram(i, j) for i in known) for j in known)
        omega = top / bottom
        for i in known:
            coef[i] = coef[i] + omega * part[i]
            taken[i] = taken[i] + omega * image[i]
    work = dot("u", "Au")
    for i in range(SWEEPS):
        work = work + coef[i] * dot(("z", i), "Au") + taken[i] * dot("u", ("g", i))
        work = work + coef[i] * sum(taken[j] * work_of(i, j) for j in range(SWEEPS))
    return coef, work


def last_kernel(matrix, sums, u_ref, z0_ref, z1_ref, z2_ref, z3_ref, factor, *rest):
    (out_u, out_f, out_c), (own, s_ref, t_ref, uf_ref, tf_ref, sens_ref) = rest[:3], rest[3:]
    flags = position()
    line = jnp.sum(sums[...], axis=0, keepdims=True)
    shape = (48, 128)
    spread = jnp.where(iota(shape, 0) == iota(shape, 1), jnp.broadcast_to(line, shape), 0.0)
    spread = jnp.broadcast_to(jnp.sum(spread, axis=1, keepdims=True), shape)
    coef, work = step_sizes(lambda index: spread[index : index + 1])
    out_c[...] = work

    def combine(x):
        value = load_columns(u_ref, x, 0, 13)
        for index, ref in enumerate((z0_ref, z1_ref, z2_ref, z3_ref)):
            value = value + coef[index] * load_columns(ref, x, 0, 13)
        store_columns(uf_ref, x, value)
        store_columns(tf_ref, x, split_store(value, x, s_ref, t_ref))
        if 2 <= x < 10:
            store_columns(own, x - 2, value[2:10])

    for x in range(13):
        combine(x)

    for i in range(6):
        for j in range(0, 6, 2):
            both = products(matrix[...], s_ref, t_ref, 2 * i, j)
            for e in range(2):
                k = j + e
                acc = jnp.zeros((8, 128), F32)
                for a in range(3):
                    left = uf_ref[2 * i + a, 16 * k : 16 * k + 24, :] * both[e][a][:24]
                    right = tf_ref[2 * i + a, 8 * k : 8 * k + 16, :] * both[e][a][24:]
                    acc = acc + left[:8] + left[8:16] + left[16:] + right[:8] + right[8:]
                sens_ref[i, k : k + 1, :] = jnp.sum(acc, axis=0, keepdims=True)
        sens_ref[i, 6:8, :] = jnp.zeros((2, 128), F32)
    edge = RADIUS - 1.0
    corner = RADIUS - math.sqrt(2.0)
    row = iota((8, 128), 0)
    lane = iota((8, 128), 1)
    sens = [sens_ref[x] * factor[x] for x in range(6)]
    low, high = flags[LOW_Y].astype(F32), flags[HIGH_Y].astype(F32)
    inside = jnp.where(row == 0, low, jnp.where(row < 5, 1.0, jnp.where(row == 5, high, 0.0)))
    inside_x = [flags[LOW_X].astype(F32)] + [1.0] * 4 + [flags[HIGH_X].astype(F32)]
    covered = [inside * value for value in inside_x]

    def along_y(v):
        return pltpu.roll(v, 1, 0) + pltpu.roll(v, 7, 0)

    def along_z(v):
        return jnp.where(lane > 0, pltpu.roll(v, 1, 1), 0.0) + jnp.where(lane < 127, pltpu.roll(v, 127, 1), 0.0)

    def gathered(layers, x):
        here, sides = layers[x], layers[x - 1] + layers[x + 1]
        ys = along_y(here)
        return (
            RADIUS * here
            + edge * (ys + along_z(here) + sides)
            + corner * (along_z(ys) + along_y(sides) + along_z(sides))
        )

    for x in range(ELEMS):
        out_f[x] = (gathered(sens, x + 1) / gathered(covered, x + 1))[1:5]
    merge = parity_matrix(True)
    for x in range(OWN):
        rows = [
            jnp.concatenate(
                [own[x, pl.ds(comp + 3 * parity, 8, stride=8), :] for parity in range(2)], axis=1
            )
            for comp in range(3)
        ]
        joined = exact_product(jnp.concatenate(rows, axis=0), merge)
        for comp in range(3):
            out_u[comp, x] = joined[8 * comp : 8 * comp + 8]


def partners(part, count_x, count_y):
    def other(i, k, count):
        if k is None:
            return i
        if k == 0:
            return i ^ 1
        return ((i + 1) ^ 1) - 1 if 0 < i < count - 1 else None

    out = []
    for x in range(count_x):
        for y in range(count_y):
            px, py = other(x, part[0], count_x), other(y, part[1], count_y)
            if px is None and py is None:
                px, py = count_x - 1 - x, y
            elif px is None:
                px, py = x, (y ^ 1 if part[1] is None else py)
            elif py is None:
                px, py = (x ^ 1 if part[0] is None else px), y
            out.append((x * count_y + y, px * count_y + py))
    return out


def shapes(*items):
    return [jax.ShapeDtypeStruct(item, F32) for item in items]


def call(kernel, out_shape, scratch, operands):
    spec = pl.BlockSpec(memory_space=pltpu.VMEM)
    return pl.pallas_call(
        kernel,
        out_shape=out_shape,
        in_specs=[spec] * len(operands),
        out_specs=[spec] * len(out_shape),
        scratch_shapes=scratch,
        compiler_params=pltpu.CompilerParams(vmem_limit_bytes=24 * 1024 * 1024),
    )(*operands)


def body(force, load_mask, support_mask, start_field, density, passive_mask):
    count_x, count_y = lax.axis_size("sx"), lax.axis_size("sy")
    devices = count_x * count_y
    stiff = element_matrix()
    matrix = jnp.asarray(operator_matrix(stiff))
    diag = jnp.asarray(diagonal_columns(stiff.astype(np.float32)))
    zero = F32(0.0)
    none = (0, 0, 0)
    small = ((0, OWN - ELEMS, 0), (0, OWN - ELEMS, 0), (0, 128, 0))
    fields = (
        lax.pad(start_field, zero, ((0, 7, 0), none, none, none))
        + lax.pad(force, zero, ((3, 4, 0), none, none, none))
        + lax.pad(density[None], zero, ((8, 1, 0), *small))
        + (
            lax.pad(load_mask[None], 0, ((6, 3, 0), none, none, none))
            + lax.pad(support_mask[None], 0, ((7, 2, 0), none, none, none))
            + lax.pad(passive_mask[None], 0, ((9, 0, 0), *small))
        ).astype(F32)
    )

    def send(value, part):
        return lax.ppermute(value, ("sx", "sy"), partners(part, count_x, count_y))

    def swap(values):
        first, second, *corners, x_side = [send(value, part) for part, value in zip(PARTS[:5], values)]
        x_side, mate = lax.optimization_barrier((x_side, values[5]))
        *corners, second = lax.optimization_barrier((*corners, second))
        passed = [send(value, MATE) for value in (mate, first, second)]
        return [first, second, *corners, x_side, *passed]

    def sizes(width):
        return [column_count(part, width) for part in PARTS]

    own = (OWN, OWN * 8, 128)
    middle = (13, 13 * 8, 128)
    first = call(
        prepare_kernel,
        [
            *shapes(own, own),
            *shapes(*((8 * (a + b), 128) for a, b in zip(sizes(HALO_U), sizes(HALO_F)))),
        ],
        [],
        [fields],
    )
    u_own, f_own = first[:2]
    second = call(
        first_kernel,
        shapes(
            middle,
            middle,
            (17, 17 * 8, 128),
            (10, 16, 128),
            (6, 8, 128),
            own,
            own,
            own,
            *(((a + 3) // 4 * 24, 128) for a in sizes(HALO_Z)),
        ),
        [
            pltpu.VMEM((24, 18 * 8, 128), F32),
            pltpu.VMEM((24, 14 * 8, 128), F32),
            pltpu.VMEM((17, 17 * 16, 128), BF16),
            pltpu.VMEM((17, 9 * 16, 128), BF16),
            pltpu.VMEM((17, 17 * 8, 128), F32),
            pltpu.VMEM((17, 9 * 8, 128), F32),
        ],
        [matrix, diag, u_own, f_own, *swap(first[2:])],
    )
    z0, u0, dinv, young, factor, w0, w1, z1 = second[:8]
    z1, z2, z3, sums = call(
        second_kernel,
        shapes(middle, middle, middle, (devices, 128)),
        [
            pltpu.VMEM((24, 22 * 8, 128), F32),
            pltpu.VMEM((21, 21 * 16, 128), BF16),
            pltpu.VMEM((21, 11 * 16, 128), BF16),
            pltpu.VMEM((21, 21 * 8, 128), F32),
            pltpu.VMEM((21, 11 * 8, 128), F32),
            pltpu.VMEM(own, F32),
            pltpu.VMEM(own, F32),
        ],
        [matrix, z1, dinv, young, w0, w1, z0, u0, f_own, *swap(second[8:])],
    )
    sums = lax.all_to_all(sums, ("sx", "sy"), 0, 0, tiled=True)
    displacement, filtered, compliance = call(
        last_kernel,
        shapes(start_field.shape, density.shape, (1, 128)),
        [
            pltpu.VMEM(own, F32),
            pltpu.VMEM((13, 13 * 16, 128), BF16),
            pltpu.VMEM((13, 7 * 16, 128), BF16),
            pltpu.VMEM(middle, F32),
            pltpu.VMEM((13, 7 * 8, 128), F32),
            pltpu.VMEM((6, 8, 128), F32),
        ],
        [matrix, sums, u0, z0, z1, z2, z3, factor],
    )
    return displacement, filtered, compliance[0, 0]


def solution(mesh):
    in_specs = (
        P(None, "sx", "sy", None),
        P("sx", "sy", None),
        P("sx", "sy", None),
        P(None, "sx", "sy", None),
        P("sx", "sy", None),
        P("sx", "sy", None),
    )
    out_specs = (P(None, "sx", "sy", None), P("sx", "sy", None), P())
    return jax.shard_map(body, mesh=mesh, in_specs=in_specs, out_specs=out_specs, check_vma=False)
```

```python
import functools
import math

import jax
import jax.numpy as jnp
import numpy as np
from jax import lax
from jax.experimental import pallas as pl
from jax.experimental.pallas import tpu as pltpu
from jax.sharding import PartitionSpec as P

SWEEPS = 4
EMIN = 0.001
RADIUS = 1.5

OWN = 8
ELEMS = OWN // 2
HALO_U = 5
HALO_F = 3
HALO_Z = 7
PARTS = [
    (None, 0),
    (None, 1),
    (1, 0),
    (1, 1),
    (1, None),
    (0, None),
]
MATE = (0, None)
UP_X, UP_Y, LOW_X, HIGH_X, LOW_Y, HIGH_Y = range(6)
SHIFTS = (0.59, 0.73, 0.645, 0.69)
F32 = jnp.float32
BF16 = jnp.bfloat16


def element_matrix():
    poisson = 0.3
    lame_first = poisson / ((1.0 + poisson) * (1.0 - 2.0 * poisson))
    shear = 1.0 / (2.0 * (1.0 + poisson))
    elastic = np.zeros((6, 6))
    elastic[:3, :3] = lame_first
    for entry in range(3):
        elastic[entry, entry] += 2.0 * shear
        elastic[entry + 3, entry + 3] = shear
    points = [-math.sqrt(0.6), 0.0, math.sqrt(0.6)]
    weights = [5.0 / 9.0, 8.0 / 9.0, 5.0 / 9.0]

    def values(point):
        return np.array(
            [point * (point - 1.0) / 2.0, 1.0 - point * point, point * (point + 1.0) / 2.0]
        )

    def slopes(point):
        return np.array([point - 0.5, -2.0 * point, point + 0.5])

    stiff = np.zeros((81, 81))
    for first in range(3):
        for second in range(3):
            for third in range(3):
                val_x, val_y, val_z = (
                    values(points[first]),
                    values(points[second]),
                    values(points[third]),
                )
                der_x, der_y, der_z = (
                    slopes(points[first]),
                    slopes(points[second]),
                    slopes(points[third]),
                )
                strain = np.zeros((6, 81))
                for node_a in range(3):
                    for node_b in range(3):
                        for node_c in range(3):
                            node = node_a * 9 + node_b * 3 + node_c
                            grad_x = 2.0 * der_x[node_a] * val_y[node_b] * val_z[node_c]
                            grad_y = 2.0 * val_x[node_a] * der_y[node_b] * val_z[node_c]
                            grad_z = 2.0 * val_x[node_a] * val_y[node_b] * der_z[node_c]
                            strain[0, node] = grad_x
                            strain[1, 27 + node] = grad_y
                            strain[2, 54 + node] = grad_z
                            strain[3, node] = grad_y
                            strain[3, 27 + node] = grad_x
                            strain[4, 27 + node] = grad_z
                            strain[4, 54 + node] = grad_y
                            strain[5, node] = grad_z
                            strain[5, 54 + node] = grad_x
                factor = weights[first] * weights[second] * weights[third] * 0.125
                stiff = stiff + factor * strain.T @ elastic @ strain
    return stiff


def balanced_parts(stiff):
    hi = stiff.astype(BF16).astype(np.float64)
    lo = (stiff - hi).astype(BF16).astype(np.float64)
    unit = 2.0 ** (np.floor(np.log2(np.maximum(np.abs(lo), 1e-30))) - 7)
    left = (hi + lo).reshape(81, 3, 27).sum(axis=2)
    moved = np.zeros((81, 81))
    for _ in range(6):
        for i in range(81):
            for j in range(i):
                first, second = left[i, j // 27], left[j, i // 27]
                step = np.clip(np.round(-(first + second) / 2 / unit[i, j]), -1 - moved[i, j], 1 - moved[i, j])
                if step and lo[i, j]:
                    moved[i, j] += step
                    left[i, j // 27] += step * unit[i, j]
                    left[j, i // 27] += step * unit[i, j]
    moved = moved + moved.T
    return hi.astype(np.float32), (lo + moved * unit).astype(np.float32)


def operator_matrix(stiff, size):
    hi, lo = balanced_parts(stiff)
    out = np.zeros((6 * size, 256), np.float32)

    def out_row(comp, a, b, c):
        first = 2 * size * a
        if c < 2:
            return first + b * 8 + c * 3 + comp
        if b == 2 and size == 32:
            return first + 6 + comp if comp < 2 else first + 27
        return first + 24 + (b // 2) * 8 + (b % 2) * 4 + comp

    def in_row(comp, a, b, c, low):
        if c < 2:
            return (a * 3 + b) * 16 + low * 8 + c * 3 + comp
        return 144 + (a * 2 + b // 2) * 16 + low * 8 + (b % 2) * 4 + comp

    index = [(p, a, b, c) for p in range(3) for a in range(3) for b in range(3) for c in range(3)]
    for i, first in enumerate(index):
        for j, second in enumerate(index):
            row = out_row(*first)
            out[row, in_row(*second, 0)] = hi[i, j]
            out[row, in_row(*second, 1)] = hi[i, j]
            out[row + size, in_row(*second, 0)] = lo[i, j]
            out[row + size, in_row(*second, 1)] = lo[i, j]
    return out.astype(BF16)


def diagonal_columns(stiff):
    out = np.zeros((4, 8, 128), np.float32)
    for pa in range(2):
        for pb in range(2):
            for c in range(2):
                for comp in range(3):
                    dof = comp * 27 + pa * 9 + pb * 3 + c
                    out[pa * 2 + pb, c * 3 + comp] = 1.0 / stiff[dof, dof]
    return out


def iota(shape, dim):
    return lax.broadcasted_iota(jnp.int32, shape, dim)


def parity_matrix(transposed):
    node = iota((256, 256), 1 if transposed else 0)
    place = iota((256, 256), 0 if transposed else 1)
    return (node == 2 * (place % 128) + place // 128).astype(F32).astype(BF16)


def exact_product(rows, matrix):
    first = rows.astype(BF16)
    left = rows - first.astype(F32)
    second = left.astype(BF16)
    third = (left - second.astype(F32)).astype(BF16)
    stacked = jnp.concatenate([first, second, third], axis=0)
    out = jnp.dot(stacked, matrix, preferred_element_type=F32)
    count = rows.shape[0]
    return out[:count] + out[count : 2 * count] + out[2 * count :]


def span(k, up, width):
    if k is None:
        return 0, OWN
    upward = up if k == 0 else 1 - up
    return upward * (OWN - width), width


def landing(k, up, width, margin):
    if k is None:
        return margin, OWN
    upward = up if k == 0 else 1 - up
    return upward * (OWN + margin) + (1 - upward) * (margin - width), width


def rows8(start):
    return pl.multiple_of(start * 8, 8) if not isinstance(start, int) else start * 8


def part_shape(part, width):
    return [OWN if k is None else width for k in part]


def take(ref, part, flags, width):
    sx, nx = span(part[0], flags[UP_X], width)
    sy, ny = span(part[1], flags[UP_Y], width)
    return ref[pl.ds(sx, nx), pl.ds(rows8(sy), ny * 8), :].reshape(nx * ny * 8, 128)


def place(ref, value, part, flags, width, passed=False):
    dx, nx = landing(part[0], flags[UP_X], OWN if passed else width, OWN)
    dy, ny = landing(part[1], flags[UP_Y], width, width)
    valid = present(part[0], flags, 0) * present(part[1], flags, 1)
    value = value * valid.astype(F32)
    ref[pl.ds(dx, nx), pl.ds(rows8(dy), ny * 8), :] = value.reshape(nx, ny * 8, 128)


def position():
    index = [lax.axis_index(axis) for axis in ("sx", "sy")]
    last = [lax.axis_size(axis) - 1 for axis in ("sx", "sy")]
    out = [1 - lax.rem(i, 2) for i in index]
    for i, end in zip(index, last):
        out += [jnp.minimum(i, 1), jnp.minimum(end - i, 1)]
    return out


def dense(cols):
    count = cols.shape[0] // 4
    c = cols.reshape(count, 4, 8, 128)
    row = iota((count, 8, 128), 1)
    tiles = [
        jnp.where(row < 6, c[:, 0], pltpu.roll(c[:, 1], 6, 1)),
        jnp.where(row < 4, pltpu.roll(c[:, 1], 6, 1), pltpu.roll(c[:, 2], 4, 1)),
        jnp.where(row < 2, pltpu.roll(c[:, 2], 4, 1), pltpu.roll(c[:, 3], 2, 1)),
    ]
    return jnp.stack(tiles, axis=1).reshape(count * 24, 128)


def sparse(rows):
    count = rows.shape[0] // 24
    t = rows.reshape(count, 3, 8, 128)
    row = iota((count, 8, 128), 1)
    cols = [
        t[:, 0],
        jnp.where(row < 2, pltpu.roll(t[:, 0], 2, 1), pltpu.roll(t[:, 1], 2, 1)),
        jnp.where(row < 4, pltpu.roll(t[:, 1], 4, 1), pltpu.roll(t[:, 2], 4, 1)),
        pltpu.roll(t[:, 2], 6, 1),
    ]
    return jnp.stack(cols, axis=1).reshape(count * 4, 8, 128)


def column_count(part, width):
    return math.prod(part_shape(part, width))


def present(k, flags, dim):
    if k is None:
        return 1
    up, low, high = flags[(UP_X, UP_Y)[dim]], flags[(LOW_X, LOW_Y)[dim]], flags[(HIGH_X, HIGH_Y)[dim]]
    upward = up if k == 0 else 1 - up
    return upward * high + (1 - upward) * low


def young_place(e):
    return e if e <= 2 else 7 if e == 3 else e + 4


def moduli_row(f_reg, e, f, row):
    start = 8 * (young_place(f) + HALO_F) + row
    return f_reg[young_place(e) + OWN, start : start + 1, :]


def parts_of(z):
    far = z * 65537.0
    hi = far - (far - z)
    return jnp.concatenate([hi, z - hi], axis=1).astype(BF16).reshape(z.shape[0] * 16, 128)


def split_store(z, x, s_ref, t_ref):
    count = z.shape[0]
    s_ref[x, : count * 16, :] = parts_of(z)
    if count % 2:
        z = jnp.concatenate([z, z[count - 1 :]], axis=0)
        count += 1
    z = z.reshape(count // 2, 2, 8, 128)
    nxt = jnp.where(iota((count // 2, 8, 128), 1) < 4, z[:, 0], pltpu.roll(z[:, 1], 4, 1))
    nxt = pltpu.roll(nxt.reshape(count * 4, 128), 127, 1)
    nxt = jnp.where(iota(nxt.shape, 1) < 127, nxt, 0.0).reshape(count // 2, 8, 128)
    t_ref[x, : count * 8, :] = parts_of(nxt)
    return nxt


def element_operand(s_ref, t_ref, x, y, pair):
    pieces = [s_ref[x + a, pl.ds(y * 16, 48), :] for a in range(3)]
    pieces += [t_ref[x + a, pl.ds(pair * 16, 32), :] for a in range(3)]
    pieces.append(jnp.zeros((16, 128), BF16))
    return jnp.concatenate(pieces, axis=0)


def products(matrix, s_ref, t_ref, x, j, size):
    operand = jnp.concatenate(
        [element_operand(s_ref, t_ref, x, 2 * e, e) for e in (j, j + 1)], axis=1
    )
    out = jnp.dot(matrix, operand, preferred_element_type=F32)
    layers = [out[r : r + size] + out[r + size : r + 2 * size] for r in range(0, matrix.shape[0], 2 * size)]
    return [[layer[:, :128] for layer in layers], [layer[:, 128:] for layer in layers]]


def apply(matrix_ref, s_ref, t_ref, young_ref, w_ref, o_ref, count_x, pairs_y, young_at, last=(0,)):
    for i in range(count_x):
        layers = (2,) if i == 0 else last if i == count_x - 1 else (0, 1, 2)
        matrix = matrix_ref[64 * layers[0] : 64 * (layers[-1] + 1), :]
        tails = [None] * 3
        for j in range(0, 2 * pairs_y, 2):
            both = products(matrix, s_ref, t_ref, 2 * i, j, 32)
            for e in range(2):
                k = j + e
                scale = young_ref[i + young_at, k + young_at : k + young_at + 1, :]
                for a, out in zip(layers, both[e]):
                    out = out * scale
                    x = 2 * i + a
                    nodes, over = out[:16], out[24:32]
                    if tails[a] is not None:
                        nodes = jnp.concatenate([nodes[:8] + tails[a], nodes[8:]], axis=0)
                    if a == 0:
                        nodes = nodes + w_ref[x, 16 * k : 16 * k + 16, :]
                        over = over + o_ref[x, 8 * k : 8 * k + 8, :]
                    w_ref[x, 16 * k : 16 * k + 16, :] = nodes
                    o_ref[x, 8 * k : 8 * k + 8, :] = over
                    tails[a] = out[16:24]
        k = 2 * pairs_y
        for a in layers:
            x = 2 * i + a
            nodes = tails[a]
            if a == 0:
                nodes = nodes + w_ref[x, 16 * k : 16 * k + 8, :]
            w_ref[x, 16 * k : 16 * k + 8, :] = nodes


def collect(w_ref, o_ref, x, low, count):
    half = (count + 1) // 2
    over = o_ref[x, 4 * low - 8 : 4 * low + 8 * half, :].reshape(half + 1, 8, 128)
    before = w_ref[x, 8 * low - 16 : 8 * low - 16 + 16 * half, :].reshape(half, 2, 8, 128)[:, 0]
    row = iota(before.shape, 1)
    third = jnp.where(row < 2, pltpu.roll(before, 2, 1), pltpu.roll(over[:-1], 7, 1))
    moved = jnp.where(row < 3, over[1:] + third, over[1:])
    moved = pltpu.roll(moved.reshape(half * 8, 128), 1, 1)
    moved = jnp.where(iota(moved.shape, 1) > 0, moved, 0.0).reshape(half, 8, 128)
    even = jnp.where(row < 3, moved, 0.0)
    odd = jnp.where(row < 3, pltpu.roll(moved, 4, 1), 0.0)
    both = jnp.stack([even, odd], axis=1).reshape(2 * half, 8, 128)[:count]
    return w_ref[x, 8 * low : 8 * (low + count), :].reshape(count, 8, 128) + both


def load_columns(ref, x, low, count):
    return ref[x, 8 * low : 8 * (low + count), :].reshape(count, 8, 128)


def store_columns(ref, x, value):
    ref[x, : 8 * value.shape[0], :] = value.reshape(8 * value.shape[0], 128)


def prepare_kernel(fields, u_ref, f_ref, *sends):
    flags = position()
    matrix = parity_matrix(False)
    solid = fields[9, :ELEMS, :ELEMS, :128] == 1.0
    rho = jnp.where(solid, 1.0, fields[8, :ELEMS, :ELEMS, :128])
    young = EMIN + (1.0 - EMIN) * (rho * rho * rho)
    factor = jnp.where(solid, 0.0, -3.0 * (1.0 - EMIN) * (rho * rho))
    for x in range(OWN):
        free = 1.0 - fields[7, x]
        loaded = free * fields[6, x]
        rows = [free * fields[c, x] for c in range(3)] + [loaded * fields[c, x] for c in range(3, 6)] + [free]
        split = exact_product(jnp.concatenate(rows, axis=0), matrix)
        for index in range(7):
            ref, row = ((u_ref, index), (f_ref, index - 3), (u_ref, 6))[index // 3]
            step = 1 if index == 6 else 3
            for parity in range(2):
                ref[x, pl.ds(row + parity * step, 8, stride=8), :] = split[
                    8 * index : 8 * index + 8, 128 * parity : 128 * parity + 128
                ]
        element = {0: 0, 1: 1, 2: 2, 5: 1, 6: 2, 7: 3}.get(x)
        for row, values in ((6, young), (7, factor)):
            if element is None:
                column = jnp.zeros((8, 128), F32)
            else:
                column = jnp.concatenate(
                    [values[element, :3], jnp.zeros((2, 128), F32), values[element, 1:]], axis=0
                )
            f_ref[x, pl.ds(row, 8, stride=8), :] = column
    for part, send in zip(PARTS, sends):
        first = take(u_ref, part, flags, HALO_U)
        send[: first.shape[0], :] = first
        send[first.shape[0] :, :] = take(f_ref, part, flags, HALO_F)


def first_kernel(matrix, diag, u_own, f_own, *rest):
    flags = position()
    received, rest = rest[:8], rest[8:]
    (z0_ref, u_ref, dinv, young, factor, v0_ref, g0_ref, z1_ref), rest = rest[:8], rest[8:]
    sends, (u_reg, f_reg, s_ref, t_ref, w_ref, o_ref) = rest[:6], rest[6:]
    u_reg[OWN : 2 * OWN, 8 * HALO_U : 8 * (HALO_U + OWN), :] = u_own[...]
    f_reg[OWN : 2 * OWN, 8 * HALO_F : 8 * (HALO_F + OWN), :] = f_own[...]
    for index, value in enumerate(received):
        passed = index >= 6
        part = (0, index - 6) if passed else PARTS[index]
        end = column_count(PARTS[index - 6] if passed else part, HALO_U) * 8
        place(u_reg, value[:end, :], part, flags, HALO_U, passed)
        place(f_reg, value[end:, :], part, flags, HALO_F, passed)
    zero = jnp.zeros((1, 128), F32)
    for e in range(-3, 7):
        rows = [moduli_row(f_reg, e, f, 6) for f in range(-3, 7)]
        young[e + 3] = jnp.concatenate(rows + [zero] * 6, axis=0)
    for e in range(-1, 5):
        rows = [moduli_row(f_reg, e, f, 7) for f in range(-1, 5)]
        factor[e + 1] = jnp.concatenate(rows + [zero] * 2, axis=0)

    def inverse(x):
        e = x // 2
        near = young[e] + young[e + 1] if x % 2 == 0 else young[e + 1]
        both = near + pltpu.roll(near, 1, 0)
        lines = {}
        for pb, total in ((0, both), (1, near)):
            before = jnp.where(iota(total.shape, 1) > 0, pltpu.roll(total, 1, 1), 0.0)
            for pc, value in ((0, total + before), (1, total)):
                lines[pb, pc] = jnp.where(value > 0.0, 1.0 / value, 0.0)
        row = iota((8, 128), 0)
        cols = []
        for y in range(17):
            pb, f = y % 2, y // 2 + 1
            even, odd = [
                lines[pb, pc][f : f + 1] * u_reg[x + 4, 8 * (y + 1) + 6 + pc : 8 * (y + 1) + 7 + pc, :]
                for pc in range(2)
            ]
            line = jnp.where(row < 3, jnp.broadcast_to(even, (8, 128)), jnp.broadcast_to(odd, (8, 128)))
            cols.append(line * diag[(x % 2) * 2 + pb])
        dinv[x] = jnp.concatenate(cols, axis=0)

    for x in range(17):
        inverse(x)

    def operand(x):
        split_store(load_columns(u_reg, x + 4, 1, 17), x, s_ref, t_ref)

    for x in range(17):
        operand(x)
    apply(matrix, s_ref, t_ref, young, w_ref, o_ref, 8, 4, 1)

    def residual(x):
        image = collect(w_ref, o_ref, x + 2, 2, 13)
        inv = load_columns(dinv, x + 2, 2, 13)
        res = load_columns(f_reg, x + 6, 1, 13) - image
        z0 = inv * res
        store_columns(z0_ref, x, z0)
        store_columns(u_ref, x, load_columns(u_reg, x + 6, 3, 13))

        if 2 <= x < 10:
            store_columns(v0_ref, x - 2, jnp.where(inv > 0.0, res, 0.0)[2:10])

    for x in range(13):
        residual(x)

    def operand_0(x):
        split_store(load_columns(z0_ref, x, 0, 13), x, s_ref, t_ref)

    for x in range(13):
        operand_0(x)
    apply(matrix, s_ref, t_ref, young, w_ref, o_ref, 5, 3, 2, last=(0, 1))

    def image_1(x):
        image = collect(w_ref, o_ref, x + 2, 2, 8)
        inv = load_columns(dinv, x + 4, 4, 8)
        image = SHIFTS[0] * jnp.where(inv > 0.0, image, 0.0)
        store_columns(g0_ref, x, image)
        store_columns(z1_ref, x, load_columns(z0_ref, x + 2, 2, 8) - inv * image)

    for x in range(OWN):
        image_1(x)
    for part, send in zip(PARTS, sends):
        cols = take(z1_ref, part, flags, HALO_Z)
        extra = send.shape[0] * 8 // 6 - cols.shape[0]
        if extra:
            cols = jnp.concatenate([cols, jnp.zeros((extra, 128), F32)], axis=0)
        send[...] = dense(cols.reshape(-1, 8, 128))


def second_kernel(matrix, z1_own, dinv, young, v0_ref, g0_ref, z0_ref, u_ref, f_own, *rest):
    received, rest = rest[:8], rest[8:]
    (z1_ref, z2_ref, z3_ref, sums_ref), rest = rest[:4], rest[4:]
    z_reg, s_ref, t_ref, w_ref, o_ref, g1_ref, g2_ref = rest
    flags = position()
    z_reg[OWN : 2 * OWN, 8 * HALO_Z : 8 * (HALO_Z + OWN), :] = z1_own[...]
    for index, value in enumerate(received):
        passed = index >= 6
        part = (0, index - 6) if passed else PARTS[index]
        count = column_count(PARTS[index - 6] if passed else part, HALO_Z)
        place(z_reg, sparse(value[...])[:count], part, flags, HALO_Z, passed)

    def operand_1(x):
        split_store(load_columns(z_reg, x + 2, 1, 21), x, s_ref, t_ref)

    for x in range(21):
        operand_1(x)

    def keep(x):
        store_columns(z1_ref, x, load_columns(z_reg, x + 6, 5, 13))

    for x in range(13):
        keep(x)
    apply(matrix, s_ref, t_ref, young, w_ref, o_ref, 10, 5, 0)

    def image_2(x):
        image = collect(w_ref, o_ref, x + 2, 2, 17)
        inv = load_columns(dinv, x, 0, 17)
        image = SHIFTS[1] * jnp.where(inv > 0.0, image, 0.0)
        z2 = load_columns(z_reg, x + 4, 3, 17) - inv * image
        split_store(z2, x, s_ref, t_ref)

        if 2 <= x < 15:
            store_columns(z2_ref, x - 2, z2[2:15])

        if 4 <= x < 12:
            store_columns(g1_ref, x - 4, image[4:12])

    for x in range(17):
        image_2(x)
    apply(matrix, s_ref, t_ref, young, w_ref, o_ref, 8, 4, 1)

    def image_3(x):
        image = collect(w_ref, o_ref, x + 2, 2, 13)
        inv = load_columns(dinv, x + 2, 2, 13)
        image = SHIFTS[2] * jnp.where(inv > 0.0, image, 0.0)
        z3 = load_columns(z2_ref, x, 0, 13) - inv * image
        split_store(z3, x, s_ref, t_ref)
        store_columns(z3_ref, x, z3)

        if 2 <= x < 10:
            store_columns(g2_ref, x - 2, image[2:10])

    for x in range(13):
        image_3(x)
    apply(matrix, s_ref, t_ref, young, w_ref, o_ref, 5, 3, 2, last=(0, 1))
    sums = [jnp.zeros((8, 128), F32) for _ in dot_list()]

    def dots(x):
        inv = load_columns(dinv, x + 4, 4, 8)
        v0 = load_columns(v0_ref, x, 0, 8)
        last = SHIFTS[3] * jnp.where(inv > 0.0, collect(w_ref, o_ref, x + 2, 2, 8), 0.0)
        vectors = {
            "v": v0,
            "u": load_columns(u_ref, x + 2, 2, 8),
            "Au": jnp.where(inv > 0.0, load_columns(f_own, x, 0, 8), 0.0) - v0,
            ("z", 0): load_columns(z0_ref, x + 2, 2, 8),
            ("z", 1): load_columns(z1_own, x, 0, 8),
            ("z", 2): load_columns(z2_ref, x + 2, 2, 8),
            ("z", 3): load_columns(z3_ref, x + 2, 2, 8),
            ("g", 0): load_columns(g0_ref, x, 0, 8),
            ("g", 1): load_columns(g1_ref, x, 0, 8),
            ("g", 2): load_columns(g2_ref, x, 0, 8),
            ("g", 3): last,
        }
        for index, (one, other) in enumerate(dot_list()):
            first, second = vectors[one], vectors[other]
            sums[index] += jnp.sum(first * second, axis=0)

    for x in range(OWN):
        dots(x)
    shape = (48, 128)
    lines = [jnp.sum(value, axis=0, keepdims=True) for value in sums]
    lines = jnp.concatenate(lines + [jnp.zeros((shape[0] - len(lines), 128), F32)], axis=0)
    totals = jnp.sum(lines, axis=1, keepdims=True)
    line = jnp.sum(
        jnp.where(iota(shape, 0) == iota(shape, 1), jnp.broadcast_to(totals, shape), 0.0),
        axis=0,
        keepdims=True,
    )
    sums_ref[...] = jnp.broadcast_to(line, sums_ref.shape)


def dot_list():
    steps = range(SWEEPS)
    out = [("v", ("g", j)) for j in steps]
    out += [(("g", i), ("g", j)) for i in steps for j in steps if i <= j]
    out += [("u", "Au")] + [(("z", i), "Au") for i in steps] + [("u", ("g", j)) for j in steps]
    out += [(("z", i), ("g", j)) for i in steps for j in steps if i <= j]
    return out


def step_sizes(total):
    place_of = {pair: index for index, pair in enumerate(dot_list())}

    def dot(one, other):
        return total(place_of[one, other])

    def gram(i, j):
        return dot(("g", min(i, j)), ("g", max(i, j)))

    def work_of(i, j):
        if i <= j:
            return dot(("z", i), ("g", j))
        return dot(("z", j), ("g", i)) * (SHIFTS[j] / SHIFTS[i])

    taken = [jnp.zeros((1, 128), F32)] * SWEEPS
    coef = list(taken)
    for sweep in range(SWEEPS):
        known = range(sweep + 1)
        part = [(taken[i - 1] if i else 1.0) - taken[i] for i in known]
        image = [part[i] / SHIFTS[i] for i in known]
        top = sum(
            image[j] * (dot("v", ("g", j)) - sum(taken[i] * gram(i, j) for i in known)) for j in known
        )
        bottom = sum(image[j] * sum(image[i] * gram(i, j) for i in known) for j in known)
        omega = top / bottom
        for i in known:
            coef[i] = coef[i] + omega * part[i]
            taken[i] = taken[i] + omega * image[i]
    work = dot("u", "Au")
    for i in range(SWEEPS):
        work = work + coef[i] * dot(("z", i), "Au") + taken[i] * dot("u", ("g", i))
        work = work + coef[i] * sum(taken[j] * work_of(i, j) for j in range(SWEEPS))
    return coef, work


def last_kernel(matrix, sums, u_ref, z0_ref, z1_ref, z2_ref, z3_ref, factor, *rest):
    (out_u, out_f, out_c), (own, s_ref, t_ref, uf_ref, tf_ref, sens_ref) = rest[:3], rest[3:]
    flags = position()
    line = jnp.sum(sums[...], axis=0, keepdims=True)
    shape = (48, 128)
    spread = jnp.where(iota(shape, 0) == iota(shape, 1), jnp.broadcast_to(line, shape), 0.0)
    spread = jnp.broadcast_to(jnp.sum(spread, axis=1, keepdims=True), shape)
    coef, work = step_sizes(lambda index: spread[index : index + 1])
    out_c[...] = work

    def combine(x):
        value = load_columns(u_ref, x, 0, 13)
        for index, ref in enumerate((z0_ref, z1_ref, z2_ref, z3_ref)):
            value = value + coef[index] * load_columns(ref, x, 0, 13)
        store_columns(uf_ref, x, value)
        store_columns(tf_ref, x, split_store(value, x, s_ref, t_ref))
        if 2 <= x < 10:
            store_columns(own, x - 2, value[2:10])

    for x in range(13):
        combine(x)

    for i in range(6):
        for j in range(0, 6, 2):
            both = products(matrix[...], s_ref, t_ref, 2 * i, j, 40)
            for e in range(2):
                k = j + e
                acc = jnp.zeros((8, 128), F32)
                for a in range(3):
                    left = uf_ref[2 * i + a, 16 * k : 16 * k + 24, :] * both[e][a][:24]
                    right = tf_ref[2 * i + a, 8 * k : 8 * k + 16, :] * both[e][a][24:]
                    acc = acc + left[:8] + left[8:16] + left[16:] + right[:8] + right[8:]
                sens_ref[i, k : k + 1, :] = jnp.sum(acc, axis=0, keepdims=True)
        sens_ref[i, 6:8, :] = jnp.zeros((2, 128), F32)
    edge = RADIUS - 1.0
    corner = RADIUS - math.sqrt(2.0)
    row = iota((8, 128), 0)
    lane = iota((8, 128), 1)
    sens = [sens_ref[x] * factor[x] for x in range(6)]
    low, high = flags[LOW_Y].astype(F32), flags[HIGH_Y].astype(F32)
    inside = jnp.where(row == 0, low, jnp.where(row < 5, 1.0, jnp.where(row == 5, high, 0.0)))
    inside_x = [flags[LOW_X].astype(F32)] + [1.0] * 4 + [flags[HIGH_X].astype(F32)]
    covered = [inside * value for value in inside_x]

    def along_y(v):
        return pltpu.roll(v, 1, 0) + pltpu.roll(v, 7, 0)

    def along_z(v):
        return jnp.where(lane > 0, pltpu.roll(v, 1, 1), 0.0) + jnp.where(lane < 127, pltpu.roll(v, 127, 1), 0.0)

    def gathered(layers, x):
        here, sides = layers[x], layers[x - 1] + layers[x + 1]
        ys = along_y(here)
        return (
            RADIUS * here
            + edge * (ys + along_z(here) + sides)
            + corner * (along_z(ys) + along_y(sides) + along_z(sides))
        )

    for x in range(ELEMS):
        out_f[x] = (gathered(sens, x + 1) / gathered(covered, x + 1))[1:5]
    merge = parity_matrix(True)
    for x in range(OWN):
        rows = [
            jnp.concatenate(
                [own[x, pl.ds(comp + 3 * parity, 8, stride=8), :] for parity in range(2)], axis=1
            )
            for comp in range(3)
        ]
        joined = exact_product(jnp.concatenate(rows, axis=0), merge)
        for comp in range(3):
            out_u[comp, x] = joined[8 * comp : 8 * comp + 8]


def partners(part, count_x, count_y):
    def other(i, k, count):
        if k is None:
            return i
        if k == 0:
            return i ^ 1
        return ((i + 1) ^ 1) - 1 if 0 < i < count - 1 else None

    out = []
    for x in range(count_x):
        for y in range(count_y):
            px, py = other(x, part[0], count_x), other(y, part[1], count_y)
            if px is None and py is None:
                px, py = count_x - 1 - x, y
            elif px is None:
                px, py = x, (y ^ 1 if part[1] is None else py)
            elif py is None:
                px, py = (x ^ 1 if part[0] is None else px), y
            out.append((x * count_y + y, px * count_y + py))
    return out


def shapes(*items):
    return [jax.ShapeDtypeStruct(item, F32) for item in items]


def call(kernel, out_shape, scratch, operands):
    spec = pl.BlockSpec(memory_space=pltpu.VMEM)
    return pl.pallas_call(
        kernel,
        out_shape=out_shape,
        in_specs=[spec] * len(operands),
        out_specs=[spec] * len(out_shape),
        scratch_shapes=scratch,
        compiler_params=pltpu.CompilerParams(vmem_limit_bytes=24 * 1024 * 1024),
    )(*operands)


def body(force, load_mask, support_mask, start_field, density, passive_mask):
    count_x, count_y = lax.axis_size("sx"), lax.axis_size("sy")
    devices = count_x * count_y
    stiff = element_matrix()
    matrix = jnp.asarray(operator_matrix(stiff, 32))
    wide = jnp.asarray(operator_matrix(stiff, 40))
    diag = jnp.asarray(diagonal_columns(stiff.astype(np.float32)))
    zero = F32(0.0)
    none = (0, 0, 0)
    small = ((0, OWN - ELEMS, 0), (0, OWN - ELEMS, 0), (0, 128, 0))
    fields = (
        lax.pad(start_field, zero, ((0, 7, 0), none, none, none))
        + lax.pad(force, zero, ((3, 4, 0), none, none, none))
        + lax.pad(density[None], zero, ((8, 1, 0), *small))
        + (
            lax.pad(load_mask[None], 0, ((6, 3, 0), none, none, none))
            + lax.pad(support_mask[None], 0, ((7, 2, 0), none, none, none))
            + lax.pad(passive_mask[None], 0, ((9, 0, 0), *small))
        ).astype(F32)
    )

    def send(value, part):
        return lax.ppermute(value, ("sx", "sy"), partners(part, count_x, count_y))

    def swap(values):
        first, second, *corners, x_side = [send(value, part) for part, value in zip(PARTS[:5], values)]
        x_side, mate = lax.optimization_barrier((x_side, values[5]))
        *corners, second = lax.optimization_barrier((*corners, second))
        passed = [send(value, MATE) for value in (mate, first, second)]
        return [first, second, *corners, x_side, *passed]

    def sizes(width):
        return [column_count(part, width) for part in PARTS]

    own = (OWN, OWN * 8, 128)
    middle = (13, 13 * 8, 128)
    first = call(
        prepare_kernel,
        [
            *shapes(own, own),
            *shapes(*((8 * (a + b), 128) for a, b in zip(sizes(HALO_U), sizes(HALO_F)))),
        ],
        [],
        [fields],
    )
    u_own, f_own = first[:2]
    second = call(
        first_kernel,
        shapes(
            middle,
            middle,
            (17, 17 * 8, 128),
            (10, 16, 128),
            (6, 8, 128),
            own,
            own,
            own,
            *(((a + 3) // 4 * 24, 128) for a in sizes(HALO_Z)),
        ),
        [
            pltpu.VMEM((24, 18 * 8, 128), F32),
            pltpu.VMEM((24, 14 * 8, 128), F32),
            pltpu.VMEM((17, 17 * 16, 128), BF16),
            pltpu.VMEM((17, 9 * 16, 128), BF16),
            pltpu.VMEM((17, 17 * 8, 128), F32),
            pltpu.VMEM((17, 9 * 8, 128), F32),
        ],
        [matrix, diag, u_own, f_own, *swap(first[2:])],
    )
    z0, u0, dinv, young, factor, w0, w1, z1 = second[:8]
    z1, z2, z3, sums = call(
        second_kernel,
        shapes(middle, middle, middle, (devices, 128)),
        [
            pltpu.VMEM((24, 22 * 8, 128), F32),
            pltpu.VMEM((21, 21 * 16, 128), BF16),
            pltpu.VMEM((21, 11 * 16, 128), BF16),
            pltpu.VMEM((21, 21 * 8, 128), F32),
            pltpu.VMEM((21, 11 * 8, 128), F32),
            pltpu.VMEM(own, F32),
            pltpu.VMEM(own, F32),
        ],
        [matrix, z1, dinv, young, w0, w1, z0, u0, f_own, *swap(second[8:])],
    )
    sums = lax.all_to_all(sums, ("sx", "sy"), 0, 0, tiled=True)
    displacement, filtered, compliance = call(
        last_kernel,
        shapes(start_field.shape, density.shape, (1, 128)),
        [
            pltpu.VMEM(own, F32),
            pltpu.VMEM((13, 13 * 16, 128), BF16),
            pltpu.VMEM((13, 7 * 16, 128), BF16),
            pltpu.VMEM(middle, F32),
            pltpu.VMEM((13, 7 * 8, 128), F32),
            pltpu.VMEM((6, 8, 128), F32),
        ],
        [wide, sums, u0, z0, z1, z2, z3, factor],
    )
    return displacement, filtered, compliance[0, 0]


def solution(mesh):
    in_specs = (
        P(None, "sx", "sy", None),
        P("sx", "sy", None),
        P("sx", "sy", None),
        P(None, "sx", "sy", None),
        P("sx", "sy", None),
        P("sx", "sy", None),
    )
    out_specs = (P(None, "sx", "sy", None), P("sx", "sy", None), P())
    return jax.shard_map(body, mesh=mesh, in_specs=in_specs, out_specs=out_specs, check_vma=False)
```
